32 devices in a mesh: row: 4 (over y, x), col: 8 (over z, core).
Axes of the slice: x: 2, y: 2, z: 4, core: 2. Of those that a mesh axis runs over, the one named last changes fastest.
Arguments:
- amplitudes: float32 [8, 8, 256, 256], P('row', 'col'), may hold values from -6 to 6
- coulomb: bfloat16 [8, 8, 256, 256], P('row'), may hold values from -6 to 6
- inner_list: int32 [8, 8, 8], P('row', 'col'), may hold values from 0 to 7, as said below
- inner_count: int32 [8, 8], P('row', 'col'), may hold values from 4 to 8
- reader_list: int32 [8, 8, 8], P('row'), may hold values from 0 to 7, as said below
- reader_count: int32 [8, 8], P('row'), may hold values from 4 to 8
- virtual_energy: float32 [256], replicated, may hold values from 0.5 to 2.5
- occupied_energy: float32 [8], replicated, may hold values from -1.5 to -0.3
Outputs:
- new_amplitudes: float32 [8, 8, 256, 256], P('row', 'col')
The draws below stay inside these ranges and needn't reach their ends.
Inputs may be any that keep to these rules, and one draw needn't show every extreme that they name: `inner_list`: for each pair block the 8 entries are distinct orbitals; only the first inner_count of them are used. `reader_list`: for each pair block the 8 entries are distinct orbitals; only the first reader_count of them are used.
All inputs are finite; a program needn't handle non-finite values.
Results may differ from the reference program's by a relative error of at most 0.0015.
Values may be sent and summed in bfloat16 or wider, within the bound.
No kernel may reach another device: no remote copies, remote signals or barrier semaphores. Data moves between devices by JAX's collectives and lax.ppermute only.
A program may use at most 64 MiB of HBM per device.

```python
import math
import jax
import jax.numpy as jnp
from jax import lax

V = 256
LMAX = 8
ITERS = 2
NO = 8


def distinct_lists(key):
    scores = jax.random.randint(key, (NO, NO, NO), 0, 2 ** 20) * NO + lax.broadcasted_iota(jnp.int32, (NO, NO, NO), 2)
    order = jnp.argsort(scores, axis=2)
    return order[:, :, :LMAX].astype(jnp.int32)


def listed_counts(key):
    counts = jax.random.randint(key, (NO, NO), LMAX // 2, LMAX + 1)
    return counts.at[0, 0].set(LMAX).astype(jnp.int32)


def draw_inner_list(key, part):
    return distinct_lists(jax.random.fold_in(key, 11))


def draw_inner_count(key, part):
    return listed_counts(jax.random.fold_in(key, 12))


def draw_reader_list(key, part):
    return distinct_lists(jax.random.fold_in(key, 13))


def draw_reader_count(key, part):
    return listed_counts(jax.random.fold_in(key, 14))


def shard_levels(stream_key, extent, split, smallest, largest):
    level = 1.0
    for axis_at, blocks in split:
        steps = jax.random.uniform(jax.random.fold_in(jax.random.fold_in(stream_key, 6), axis_at), (blocks,), jnp.float32, smallest / len(split), largest / len(split))
        level = level * jnp.repeat(jnp.exp(steps), extent[axis_at] // blocks).reshape((-1,) + (1,) * (len(extent) - 1 - axis_at))
    return level


def scatter_about(own_key, extent, scale, reach, cuts=(), kind=jnp.bfloat16):
    values = jax.random.normal(own_key, extent, jnp.float32) * scale
    if len(cuts) > 0:
        values = shard_levels(own_key, extent, cuts, -0.22, 0.18) * values
    return jnp.clip(values, min=-reach, max=reach).astype(kind)


def setup_inputs(seed: int = 0) -> dict:
    key_list = jax.random.split(jax.random.key(seed), 9)
    return {
        "amplitudes": scatter_about(key_list[0], (NO, NO, V, V), 1.0, 6.0, ((0, 4), (1, 8)), jnp.float32),
        "coulomb": scatter_about(key_list[1], (NO, NO, V, V), 1.0, 6.0, ((0, 4),)),
        "inner_list": draw_inner_list(jax.random.fold_in(key_list[8], 71), 0),
        "inner_count": draw_inner_count(jax.random.fold_in(key_list[8], 71), 0),
        "reader_list": draw_reader_list(jax.random.fold_in(key_list[8], 71), 0),
        "reader_count": draw_reader_count(jax.random.fold_in(key_list[8], 71), 0),
        "virtual_energy": jnp.clip(jnp.exp(jax.random.uniform(key_list[6], (V,), jnp.float32, math.log(0.5), math.log(2.5))), 0.5, 2.5),
        "occupied_energy": jnp.clip(jax.random.uniform(key_list[7], (NO,), jnp.float32, -1.5, -0.3), -1.5, -0.3),
    }


damping = 0.5
coupling = 0.03125


def reference(amplitudes, coulomb, inner_list, inner_count, reader_list, reader_count, virtual_energy, occupied_energy):
    slot_iota = jnp.arange(LMAX, dtype=jnp.int32)
    orbital_iota = jnp.arange(NO, dtype=jnp.int32)
    denominator = (virtual_energy[:, None] + virtual_energy[None, :])[None, None] - occupied_energy[:, None, None, None] - occupied_energy[None, :, None, None]
    amp_state = amplitudes
    for sweep_index in range(ITERS):
        amp_half = amp_state.astype(jnp.bfloat16)

        def coupled_row(orbital):
            listed = inner_list[orbital]
            weight = (slot_iota[None, :] < inner_count[orbital][:, None]).astype(jnp.float32)
            left_part = coulomb[orbital][listed].astype(jnp.float32)
            right_part = amp_half[listed, orbital_iota[:, None]].astype(jnp.float32)
            return jnp.einsum("jsab,jsbc,js->jac", left_part, right_part, weight)

        coupled = lax.map(coupled_row, orbital_iota).astype(jnp.bfloat16)

        def quad_row(orbital):
            listed = reader_list[orbital]
            weight = (slot_iota[None, :] < reader_count[orbital][:, None]).astype(jnp.float32)
            left_part = amp_half[orbital][listed].astype(jnp.float32)
            right_part = coupled[listed, orbital_iota[:, None]].astype(jnp.float32)
            return jnp.einsum("jsab,jsbc,js->jac", left_part, right_part, weight)

        quadratic = lax.map(quad_row, orbital_iota)
        mirror = jnp.transpose(coupled, (1, 0, 3, 2)).astype(jnp.float32)
        residual = coulomb.astype(jnp.float32) + coupling * (coupled.astype(jnp.float32) + mirror) + coupling * coupling * quadratic
        amp_state = damping * amp_state - residual / denominator
    return amp_state
```

```python
import functools

import jax
import jax.numpy as jnp
from jax import lax
from jax.experimental import pallas as pl
from jax.experimental.pallas import tpu as pltpu
from jax.sharding import PartitionSpec as P

ITERS = 2


damping = 0.5
coupling = 0.03125
ANY = pl.BlockSpec(memory_space=pl.ANY)
SMEM = pl.BlockSpec(memory_space=pltpu.SMEM)
VMEM = pl.BlockSpec(memory_space=pltpu.VMEM)
VMEM_BYTES = 32 * 1024 * 1024


def coupled_body(rows, meta, k_hbm, *refs):
    pieces = refs[:rows]
    out_ref, k_buf, a_buf, acc, k_sem, a_sem = refs[rows:]
    orb_rows = out_ref.shape[0]
    me = meta[2 * orb_rows, 0]
    k_copy = pltpu.make_async_copy(k_hbm, k_buf, k_sem)
    k_copy.start()
    copies = []
    for step in range(rows):
        start = (me ^ step) * orb_rows
        copy = pltpu.make_async_copy(pieces[step], a_buf.at[pl.ds(start, orb_rows)], a_sem.at[step])
        copy.start()
        copies.append(copy)
    acc[...] = jnp.zeros_like(acc)
    k_copy.wait()
    for step in range(rows):
        copies[step].wait()
        for t in range(orb_rows):
            orbital = (me ^ step) * orb_rows + t
            for i in range(orb_rows):

                @pl.when(meta[i, orbital] > 0)
                def _():
                    acc[i] += jnp.dot(k_buf[i, orbital], a_buf[orbital], preferred_element_type=jnp.float32)

    out_ref[...] = acc[...].astype(out_ref.dtype)


def coupled_blocks(rows, meta, coulomb, pieces):
    orb_rows, count, virt, _ = coulomb.shape
    return pl.pallas_call(
        functools.partial(coupled_body, rows),
        out_shape=jax.ShapeDtypeStruct((orb_rows, virt, virt), jnp.bfloat16),
        in_specs=[SMEM, ANY] + [ANY] * rows,
        out_specs=VMEM,
        scratch_shapes=[
            pltpu.VMEM((orb_rows, count, virt, virt), jnp.bfloat16),
            pltpu.VMEM((count, virt, virt), jnp.bfloat16),
            pltpu.VMEM((orb_rows, virt, virt), jnp.float32),
            pltpu.SemaphoreType.DMA,
            pltpu.SemaphoreType.DMA((rows,)),
        ],
        compiler_params=pltpu.CompilerParams(vmem_limit_bytes=VMEM_BYTES),
        cost_estimate=pl.CostEstimate(
            flops=2 * orb_rows * count * virt**3, bytes_accessed=2 * (orb_rows + 1) * count * virt**2, transcendentals=0
        ),
    )(meta, coulomb, *pieces)


def update_body(rows, halves, meta, *refs):
    c_pieces = refs[:rows]
    d_pieces = refs[rows : rows + 2 * halves]
    base_ref, state_ref, denom_ref = refs[rows + 2 * halves : rows + 2 * halves + 3]
    out_ref, half_ref, c_buf, d_buf, acc, c_sem, d_sem = refs[rows + 2 * halves + 3 :]
    orb_rows = out_ref.shape[0]
    me_row = meta[2 * orb_rows, 0]
    me_col = meta[2 * orb_rows, 1]
    copies = []
    for at in range(2 * halves):
        copy = pltpu.make_async_copy(d_pieces[at], d_buf.at[me_col ^ at], d_sem.at[at])
        copy.start()
        copies.append(copy)
    for step in range(rows):
        start = (me_row ^ step) * orb_rows
        copy = pltpu.make_async_copy(c_pieces[step], c_buf.at[pl.ds(start, orb_rows)], c_sem.at[step])
        copy.start()
        copies.append(copy)
    acc[...] = jnp.zeros_like(acc)
    for copy in copies:
        copy.wait()
    for orbital in range(c_buf.shape[0]):
        for i in range(orb_rows):

            @pl.when(meta[orb_rows + i, orbital] > 0)
            def _():
                acc[i] += jnp.dot(d_buf[orbital, i], c_buf[orbital], preferred_element_type=jnp.float32)

    residual = base_ref[...] + coupling * coupling * acc[...]
    state = damping * state_ref[...] - residual / denom_ref[...]
    out_ref[...] = state
    half_ref[...] = state.astype(half_ref.dtype)


def updated_state(rows, halves, meta, c_pieces, d_pieces, base, state, denominator):
    orb_rows, virt, _ = state.shape
    count = rows * orb_rows
    return pl.pallas_call(
        functools.partial(update_body, rows, halves),
        out_shape=(
            jax.ShapeDtypeStruct((orb_rows, virt, virt), jnp.float32),
            jax.ShapeDtypeStruct((orb_rows, virt, virt), jnp.bfloat16),
        ),
        in_specs=[SMEM] + [ANY] * (rows + 2 * halves) + [VMEM] * 3,
        out_specs=(VMEM, VMEM),
        scratch_shapes=[
            pltpu.VMEM((count, virt, virt), jnp.bfloat16),
            pltpu.VMEM((2 * halves, orb_rows, virt, virt), jnp.bfloat16),
            pltpu.VMEM((orb_rows, virt, virt), jnp.float32),
            pltpu.SemaphoreType.DMA((rows,)),
            pltpu.SemaphoreType.DMA((2 * halves,)),
        ],
        compiler_params=pltpu.CompilerParams(vmem_limit_bytes=VMEM_BYTES),
        cost_estimate=pl.CostEstimate(
            flops=2 * orb_rows * count * virt**3, bytes_accessed=2 * (orb_rows + 1) * count * virt**2, transcendentals=0
        ),
    )(meta, *c_pieces, *d_pieces, base, state, denominator)


def on_device(
    rows,
    cols,
    amplitudes,
    coulomb,
    inner_list,
    inner_count,
    reader_list,
    reader_count,
    virtual_energy,
    occupied_energy,
):
    orb_rows, orb_cols, virt, _ = amplitudes.shape
    count = coulomb.shape[1]
    slots = inner_list.shape[2]
    assert orb_cols == 1 and count == cols == rows * orb_rows and orb_rows == 2
    halves = cols // 2
    my_row = lax.axis_index("row")
    my_col = lax.axis_index("col")

    def from_row(x, step):
        return lax.ppermute(x, "row", [(r ^ step, r) for r in range(rows)])

    def from_col(x, at):
        return lax.ppermute(x, "col", [(c ^ at, c) for c in range(cols)])

    def mirrored(x, flip):
        pairs = []
        for r in range(rows):
            for c in range(cols):
                i = 2 * r + ((c % 2) ^ flip)
                pairs.append((r * cols + c, (c // 2) * cols + i))
        return lax.ppermute(x, ("row", "col"), pairs)

    state = amplitudes[:, 0]
    half = state.astype(jnp.bfloat16)

    slot_iota = jnp.arange(slots, dtype=jnp.int32)
    orbital_iota = jnp.arange(count, dtype=jnp.int32)

    def used(lists, counts):
        live = slot_iota[None] < counts[:, None]
        hit = (lists[:, :, None] == orbital_iota) & live[:, :, None]
        return jnp.any(hit, axis=1).astype(jnp.int32)

    inner_used = used(inner_list[:, 0], inner_count[:, 0])
    reader_used = used(
        lax.dynamic_index_in_dim(reader_list, my_col, 1, False), lax.dynamic_index_in_dim(reader_count, my_col, 1, False)
    )
    place = jnp.where(orbital_iota == 0, my_row, my_col).astype(jnp.int32)
    meta = jnp.concatenate([inner_used, reader_used, place[None]], axis=0)

    occ_rows = lax.dynamic_slice_in_dim(occupied_energy, my_row * orb_rows, orb_rows, 0)
    occ_col = lax.dynamic_slice_in_dim(occupied_energy, my_col, 1, 0)
    virt_pair = virtual_energy[:, None] + virtual_energy[None, :]
    denominator = virt_pair[None] - occ_rows[:, None, None] - occ_col[:, None, None]
    coulomb_own = lax.dynamic_index_in_dim(coulomb, my_col, 1, False).astype(jnp.float32)
    parity = my_col % 2

    for sweep_index in range(ITERS):
        a_pieces = [half] + [from_row(half, step) for step in range(1, rows)]
        d_own = [half] + [from_col(half, 2 * at) for at in range(1, halves)]
        d_pieces = []
        for piece in d_own:
            d_pieces += [piece, from_col(piece, 1)]
        coupled = coupled_blocks(rows, meta, coulomb, a_pieces)
        c_pieces = [coupled] + [from_row(coupled, step) for step in range(1, rows)]
        near = mirrored(lax.dynamic_index_in_dim(coupled, parity, 0, False), 0)
        far = mirrored(lax.dynamic_index_in_dim(coupled, 1 - parity, 0, False), 1)
        first = jnp.where(parity == 0, near, far)
        second = jnp.where(parity == 0, far, near)
        mirror = jnp.transpose(jnp.stack([first, second]), (0, 2, 1))
        base = coulomb_own + coupling * (coupled.astype(jnp.float32) + mirror.astype(jnp.float32))
        state, half = updated_state(rows, halves, meta, c_pieces, d_pieces, base, state, denominator)
    return state[:, None]


def solution(mesh):
    return jax.shard_map(
        functools.partial(on_device, mesh.shape["row"], mesh.shape["col"]),
        mesh=mesh,
        in_specs=(
            P("row", "col", None, None),
            P("row", None, None, None),
            P("row", "col", None),
            P("row", "col"),
            P("row", None, None),
            P("row", None),
            P(),
            P(),
        ),
        out_specs=P("row", "col", None, None),
        check_vma=False,
    )
```

```python
import functools

import jax
import jax.numpy as jnp
from jax import lax
from jax.experimental import pallas as pl
from jax.experimental.pallas import tpu as pltpu
from jax.sharding import PartitionSpec as P

ITERS = 2


damping = 0.5
coupling = 0.03125
ANY = pl.BlockSpec(memory_space=pl.ANY)
SMEM = pl.BlockSpec(memory_space=pltpu.SMEM)
VMEM = pl.BlockSpec(memory_space=pltpu.VMEM)
VMEM_BYTES = 32 * 1024 * 1024


def coupled_body(meta, k_ref, a_ref, out_ref, acc):
    orb_rows, count = k_ref.shape[:2]
    acc[...] = jnp.zeros_like(acc)
    for orbital in range(count):
        for i in range(orb_rows):

            @pl.when(meta[i, orbital] > 0)
            def _():
                acc[i] += jnp.dot(k_ref[i, orbital], a_ref[orbital], preferred_element_type=jnp.float32)

    out_ref[...] = acc[...].astype(out_ref.dtype)


def coupled_blocks(meta, coulomb, amp_column):
    orb_rows, count, virt, _ = coulomb.shape
    return pl.pallas_call(
        coupled_body,
        out_shape=jax.ShapeDtypeStruct((orb_rows, virt, virt), jnp.bfloat16),
        in_specs=[SMEM, VMEM, VMEM],
        out_specs=VMEM,
        scratch_shapes=[pltpu.VMEM((orb_rows, virt, virt), jnp.float32)],
        compiler_params=pltpu.CompilerParams(vmem_limit_bytes=VMEM_BYTES),
        cost_estimate=pl.CostEstimate(
            flops=2 * orb_rows * count * virt**3, bytes_accessed=2 * (orb_rows + 1) * count * virt**2, transcendentals=0
        ),
    )(meta, coulomb, amp_column)


def update_body(meta, c_ref, own_ref, other_ref, base_ref, state_ref, denom_ref, out_ref, half_ref, acc):
    halves, orb_rows = own_ref.shape[:2]
    parity = meta[2 * orb_rows, 0]
    acc[...] = jnp.zeros_like(acc)
    for ref, side in ((own_ref, parity), (other_ref, 1 - parity)):
        for at in range(halves):
            orbital = 2 * at + side
            for i in range(orb_rows):

                @pl.when(meta[orb_rows + i, orbital] > 0)
                def _():
                    acc[i] += jnp.dot(ref[at, i], c_ref[orbital], preferred_element_type=jnp.float32)

    residual = base_ref[...] + coupling * coupling * acc[...]
    state = damping * state_ref[...] - residual / denom_ref[...]
    out_ref[...] = state
    half_ref[...] = state.astype(half_ref.dtype)


def updated_state(meta, coupled_column, own_amps, other_amps, base, state, denominator):
    orb_rows, virt, _ = state.shape
    count = coupled_column.shape[0]
    return pl.pallas_call(
        update_body,
        out_shape=(
            jax.ShapeDtypeStruct((orb_rows, virt, virt), jnp.float32),
            jax.ShapeDtypeStruct((orb_rows, virt, virt), jnp.bfloat16),
        ),
        in_specs=[SMEM] + [VMEM] * 6,
        out_specs=(VMEM, VMEM),
        scratch_shapes=[pltpu.VMEM((orb_rows, virt, virt), jnp.float32)],
        compiler_params=pltpu.CompilerParams(vmem_limit_bytes=VMEM_BYTES),
        cost_estimate=pl.CostEstimate(
            flops=2 * orb_rows * count * virt**3, bytes_accessed=2 * (orb_rows + 1) * count * virt**2, transcendentals=0
        ),
    )(meta, coupled_column, own_amps, other_amps, base, state, denominator)


def on_device(
    rows,
    cols,
    amplitudes,
    coulomb,
    inner_list,
    inner_count,
    reader_list,
    reader_count,
    virtual_energy,
    occupied_energy,
):
    orb_rows, orb_cols, virt, _ = amplitudes.shape
    count = coulomb.shape[1]
    slots = inner_list.shape[2]
    assert orb_cols == 1 and count == cols == rows * orb_rows and orb_rows == 2
    halves = cols // 2
    my_row = lax.axis_index("row")
    my_col = lax.axis_index("col")

    groups = [[2 * at + side for at in range(halves)] for side in range(2)]

    def row_gathered(x):
        tiled = jnp.broadcast_to(x[None], (rows,) + x.shape)
        got = lax.all_to_all(tiled, "row", split_axis=0, concat_axis=0, tiled=True)
        return got.reshape((rows * x.shape[0],) + x.shape[1:])

    def column_gathered(x):
        tiled = jnp.broadcast_to(x[None], (halves,) + x.shape)
        return lax.all_to_all(tiled, "col", split_axis=0, concat_axis=0, axis_index_groups=groups, tiled=True)

    def swapped(x):
        return lax.ppermute(x, "col", [(c ^ 1, c) for c in range(cols)])

    def mirrored(x, flip):
        pairs = []
        for r in range(rows):
            for c in range(cols):
                i = 2 * r + ((c % 2) ^ flip)
                pairs.append((r * cols + c, (c // 2) * cols + i))
        return lax.ppermute(x, ("row", "col"), pairs)

    state = amplitudes[:, 0]
    half = state.astype(jnp.bfloat16)

    slot_iota = jnp.arange(slots, dtype=jnp.int32)
    orbital_iota = jnp.arange(count, dtype=jnp.int32)

    def used(lists, counts):
        live = slot_iota[None] < counts[:, None]
        hit = (lists[:, :, None] == orbital_iota) & live[:, :, None]
        return jnp.any(hit, axis=1).astype(jnp.int32)

    inner_used = used(inner_list[:, 0], inner_count[:, 0])
    reader_used = used(
        lax.dynamic_index_in_dim(reader_list, my_col, 1, False), lax.dynamic_index_in_dim(reader_count, my_col, 1, False)
    )
    parity = my_col % 2
    meta = jnp.concatenate([inner_used, reader_used, jnp.full((1, count), parity, jnp.int32)], axis=0)

    occ_rows = lax.dynamic_slice_in_dim(occupied_energy, my_row * orb_rows, orb_rows, 0)
    occ_col = lax.dynamic_slice_in_dim(occupied_energy, my_col, 1, 0)
    virt_pair = virtual_energy[:, None] + virtual_energy[None, :]
    denominator = virt_pair[None] - occ_rows[:, None, None] - occ_col[:, None, None]
    coulomb_own = lax.dynamic_index_in_dim(coulomb, my_col, 1, False).astype(jnp.float32)

    for sweep_index in range(ITERS):
        amp_column = row_gathered(half)
        own_amps = column_gathered(half)
        other_amps = swapped(own_amps)
        coupled = coupled_blocks(meta, coulomb, amp_column)
        coupled_column = row_gathered(coupled)
        near = mirrored(lax.dynamic_index_in_dim(coupled, parity, 0, False), 0)
        far = mirrored(lax.dynamic_index_in_dim(coupled, 1 - parity, 0, False), 1)
        first = jnp.where(parity == 0, near, far)
        second = jnp.where(parity == 0, far, near)
        mirror = jnp.transpose(jnp.stack([first, second]), (0, 2, 1))
        base = coulomb_own + coupling * (coupled.astype(jnp.float32) + mirror.astype(jnp.float32))
        state, half = updated_state(meta, coupled_column, own_amps, other_amps, base, state, denominator)
    return state[:, None]


def solution(mesh):
    return jax.shard_map(
        functools.partial(on_device, mesh.shape["row"], mesh.shape["col"]),
        mesh=mesh,
        in_specs=(
            P("row", "col", None, None),
            P("row", None, None, None),
            P("row", "col", None),
            P("row", "col"),
            P("row", None, None),
            P("row", None),
            P(),
            P(),
        ),
        out_specs=P("row", "col", None, None),
        check_vma=False,
    )
```

```python
import functools

import jax
import jax.numpy as jnp
from jax import lax
from jax.experimental import pallas as pl
from jax.experimental.pallas import tpu as pltpu
from jax.sharding import PartitionSpec as P

ITERS = 2


damping = 0.5
coupling = 0.03125
ANY = pl.BlockSpec(memory_space=pl.ANY)
SMEM = pl.BlockSpec(memory_space=pltpu.SMEM)
VMEM = pl.BlockSpec(memory_space=pltpu.VMEM)
VMEM_BYTES = 32 * 1024 * 1024


def call(body, out_shape, in_specs, flops, moved, *operands):
    single = isinstance(out_shape, jax.ShapeDtypeStruct)
    return pl.pallas_call(
        body,
        out_shape=out_shape,
        in_specs=in_specs,
        out_specs=VMEM if single else (VMEM,) * len(out_shape),
        compiler_params=pltpu.CompilerParams(vmem_limit_bytes=VMEM_BYTES),
        cost_estimate=pl.CostEstimate(flops=flops, bytes_accessed=moved, transcendentals=0),
    )(*operands)


def masked_coulomb_body(meta, k_ref, out_ref):
    orb_rows, _, virt, _ = k_ref.shape
    my_row = meta[2 * orb_rows, 0]
    for step in range(out_ref.shape[0]):
        for t in range(orb_rows):
            orbital = (my_row ^ step) * orb_rows + t
            for i in range(orb_rows):
                block = k_ref[i, orbital]
                keep = jnp.where(meta[i, orbital] > 0, block, jnp.zeros_like(block))
                out_ref[step, i * virt : (i + 1) * virt, t * virt : (t + 1) * virt] = keep


def masked_coulomb(rows, meta, coulomb):
    orb_rows, count, virt, _ = coulomb.shape
    shape = jax.ShapeDtypeStruct((rows, orb_rows * virt, orb_rows * virt), jnp.bfloat16)
    return call(masked_coulomb_body, shape, [SMEM, VMEM], 0, 4 * orb_rows * count * virt**2, meta, coulomb)


def coupled_body(rows, k_ref, *refs):
    out_ref = refs[rows]
    orb_rows, virt, _ = out_ref.shape
    total = None
    for step in range(rows):
        part = jnp.dot(
            k_ref[step], refs[step][...].reshape(orb_rows * virt, virt), preferred_element_type=jnp.float32
        )
        total = part if total is None else total + part
    out_ref[...] = total.astype(out_ref.dtype).reshape(out_ref.shape)


def coupled_blocks(rows, kept, pieces):
    orb_rows, virt, _ = pieces[0].shape
    count = rows * orb_rows
    shape = jax.ShapeDtypeStruct((orb_rows, virt, virt), jnp.bfloat16)
    body = functools.partial(coupled_body, rows)
    flops, moved = 2 * orb_rows * count * virt**3, 2 * (orb_rows + 1) * count * virt**2
    return call(body, shape, [VMEM] * (1 + rows), flops, moved, kept, *pieces)


def collected_body(places, meta, crossed_ref, *refs):
    out_ref = refs[len(places)]
    orb_rows = crossed_ref.shape[0]
    halves = (out_ref.shape[0] - 1) // orb_rows
    my_col = meta[2 * orb_rows, 1]
    at = my_col // 2
    for ref, hops in zip(refs, places):
        for hop in hops:
            spot = at + hop

            @pl.when(jnp.logical_and(spot >= 0, spot < halves))
            def _():
                out_ref[pl.ds(spot * orb_rows, orb_rows)] = ref[...]

    out_ref[orb_rows * halves] = crossed_ref[1 - my_col % 2]


def collected(meta, halves, crossed, pieces, places):
    orb_rows, virt, _ = crossed.shape
    shape = jax.ShapeDtypeStruct((orb_rows * halves + 1, virt, virt), jnp.bfloat16)
    body = functools.partial(collected_body, places)
    moved = 4 * (orb_rows * halves + 1) * virt**2
    return call(body, shape, [SMEM] + [VMEM] * (1 + len(pieces)), 0, moved, meta, crossed, *pieces)


def tied_body(*refs):
    pass


def tied(x, *others):
    return pl.pallas_call(
        tied_body,
        out_shape=jax.ShapeDtypeStruct(x.shape, x.dtype),
        in_specs=[ANY] * (1 + len(others)),
        out_specs=ANY,
        input_output_aliases={0: 0},
    )(x, *others)


def quadratic_part(rows, meta, side, left_ref, c_refs):
    orb_rows = c_refs[0].shape[0]
    my_row = meta[2 * orb_rows, 0]
    total = None
    for step in range(rows):
        at = my_row ^ step
        blocks = []
        for i in range(orb_rows):
            block = left_ref[at * orb_rows + i]
            blocks.append(jnp.where(meta[orb_rows + i, 2 * at + side] > 0, block, jnp.zeros_like(block)))
        part = jnp.dot(jnp.concatenate(blocks, axis=0), c_refs[step][side], preferred_element_type=jnp.float32)
        total = part if total is None else total + part
    return total.reshape(orb_rows, -1, total.shape[1])


def turned(block):
    return jnp.transpose(block.astype(jnp.float32), (1, 0))


def first_body(rows, meta, left_ref, *refs):
    c_refs = refs[:rows]
    crossed_ref, state_ref, coulomb_ref, inverse_ref, out_ref = refs[rows:]
    orb_rows = out_ref.shape[0]
    side = meta[2 * orb_rows, 1] % 2
    quadratic = quadratic_part(rows, meta, side, left_ref, c_refs)
    linear = coulomb_ref[...].astype(jnp.float32) + coupling * c_refs[0][...].astype(jnp.float32)
    residual = linear + coupling * coupling * quadratic
    out_ref[...] = damping * state_ref[...] - residual * inverse_ref[...]
    out_ref[side] -= coupling * turned(crossed_ref[side]) * inverse_ref[side]


def second_body(rows, meta, left_ref, *refs):
    c_refs = refs[:rows]
    part_ref, inverse_ref, out_ref, half_ref = refs[rows:]
    orb_rows = out_ref.shape[0]
    side = 1 - meta[2 * orb_rows, 1] % 2
    quadratic = quadratic_part(rows, meta, side, left_ref, c_refs)
    out_ref[...] = part_ref[...] - coupling * coupling * quadratic * inverse_ref[...]
    out_ref[side] -= coupling * turned(left_ref[left_ref.shape[0] - 1]) * inverse_ref[side]
    half_ref[...] = out_ref[...].astype(half_ref.dtype)


def updated_state(rows, meta, own, swapped, c_pieces, crossed, state, coulomb_own, inverse):
    orb_rows, virt, _ = state.shape
    count = rows * orb_rows
    whole = jax.ShapeDtypeStruct((orb_rows, virt, virt), jnp.float32)
    half = jax.ShapeDtypeStruct((orb_rows, virt, virt), jnp.bfloat16)
    flops, moved = orb_rows * count * virt**3, 2 * (orb_rows + 1) * count * virt**2
    part = call(
        functools.partial(first_body, rows), whole, [SMEM] + [VMEM] * (rows + 5), flops, moved,
        meta, own, *c_pieces, crossed, state, coulomb_own, inverse,
    )
    return call(
        functools.partial(second_body, rows), (whole, half), [SMEM] + [VMEM] * (rows + 3), flops, moved,
        meta, swapped, *c_pieces, part, inverse,
    )


def on_device(
    rows,
    cols,
    amplitudes,
    coulomb,
    inner_list,
    inner_count,
    reader_list,
    reader_count,
    virtual_energy,
    occupied_energy,
):
    orb_rows, orb_cols, virt, _ = amplitudes.shape
    count = coulomb.shape[1]
    slots = inner_list.shape[2]
    assert orb_cols == 1 and count == cols == rows * orb_rows and orb_rows == 2
    halves = cols // 2
    my_row = lax.axis_index("row")
    my_col = lax.axis_index("col")

    def from_row(x, step):
        return lax.ppermute(x, "row", [(r ^ step, r) for r in range(rows)])

    def along(x, hops):
        return lax.ppermute(
            x, "col", [(2 * at + k, 2 * (at + hop) + k) for at, hop in hops for k in range(2)]
        )

    def relayed(x):
        pieces, places = [x], [(0,)]
        up = down = x
        for stage in range(1, halves):
            ups = [(at, 1) for at in range(stage - 1, halves - 1)]
            downs = [(at, -1) for at in range(1, halves - stage + 1)]
            if stage - 1 > halves - stage:
                up = down = along(jnp.where(my_col // 2 >= stage - 1, up, down), ups + downs)
                pieces.append(up)
                places.append((-stage, stage))
            else:
                up, down = along(up, ups), along(down, downs)
                pieces += [up, down]
                places += [(-stage,), (stage,)]
        return pieces, tuple(places)

    def across(x):
        pairs = [(r * cols + c, (c // 2) * cols + 2 * r + c % 2) for r in range(rows) for c in range(cols)]
        return lax.ppermute(x, ("row", "col"), pairs)

    state = amplitudes[:, 0]
    half = state.astype(jnp.bfloat16)

    slot_iota = jnp.arange(slots, dtype=jnp.int32)
    orbital_iota = jnp.arange(count, dtype=jnp.int32)

    def used(lists, counts):
        live = slot_iota[None] < counts[:, None]
        hit = (lists[:, :, None] == orbital_iota) & live[:, :, None]
        return jnp.any(hit, axis=1).astype(jnp.int32)

    inner_used = used(inner_list[:, 0], inner_count[:, 0])
    reader_used = used(
        lax.dynamic_index_in_dim(reader_list, my_col, 1, False), lax.dynamic_index_in_dim(reader_count, my_col, 1, False)
    )
    place = jnp.where(orbital_iota == 0, my_row, my_col).astype(jnp.int32)
    meta = jnp.concatenate([inner_used, reader_used, place[None]], axis=0)

    occ_rows = lax.dynamic_slice_in_dim(occupied_energy, my_row * orb_rows, orb_rows, 0)
    occ_col = lax.dynamic_slice_in_dim(occupied_energy, my_col, 1, 0)
    virt_pair = virtual_energy[:, None] + virtual_energy[None, :]
    inverse = 1.0 / (virt_pair[None] - occ_rows[:, None, None] - occ_col[:, None, None])
    coulomb_own = lax.dynamic_index_in_dim(coulomb, my_col, 1, False)
    kept = masked_coulomb(rows, meta, coulomb)

    for sweep_index in range(ITERS):
        a_pieces = [half] + [from_row(half, step) for step in range(1, rows)]
        column, places = relayed(half)
        coupled = coupled_blocks(rows, kept, a_pieces)
        c_pieces = [coupled] + [from_row(coupled, step) for step in range(1, rows)]
        crossed = across(coupled)
        own = collected(meta, halves, crossed, column, places)
        own = tied(own, *c_pieces)
        swapped = lax.ppermute(own, "col", [(c ^ 1, c) for c in range(cols)])
        state, half = updated_state(rows, meta, own, swapped, c_pieces, crossed, state, coulomb_own, inverse)
    return state[:, None]


def solution(mesh):
    return jax.shard_map(
        functools.partial(on_device, mesh.shape["row"], mesh.shape["col"]),
        mesh=mesh,
        in_specs=(
            P("row", "col", None, None),
            P("row", None, None, None),
            P("row", "col", None),
            P("row", "col"),
            P("row", None, None),
            P("row", None),
            P(),
            P(),
        ),
        out_specs=P("row", "col", None, None),
        check_vma=False,
    )
```

```python
import functools

import jax
import jax.numpy as jnp
from jax import lax
from jax.experimental import pallas as pl
from jax.experimental.pallas import tpu as pltpu
from jax.sharding import PartitionSpec as P

ITERS = 2


damping = 0.5
coupling = 0.03125
ANY = pl.BlockSpec(memory_space=pl.ANY)
SMEM = pl.BlockSpec(memory_space=pltpu.SMEM)
VMEM = pl.BlockSpec(memory_space=pltpu.VMEM)
VMEM_BYTES = 32 * 1024 * 1024


def call(body, out_shape, in_specs, flops, moved, *operands):
    single = isinstance(out_shape, jax.ShapeDtypeStruct)
    return pl.pallas_call(
        body,
        out_shape=out_shape,
        in_specs=in_specs,
        out_specs=VMEM if single else (VMEM,) * len(out_shape),
        compiler_params=pltpu.CompilerParams(vmem_limit_bytes=VMEM_BYTES),
        cost_estimate=pl.CostEstimate(flops=flops, bytes_accessed=moved, transcendentals=0),
    )(*operands)


def prologue_body(meta, occupied, k_ref, virt_row, virt_col, kept_ref, own_ref, inverse_ref):
    orb_rows, _, virt, _ = k_ref.shape
    my_row = meta[2 * orb_rows, 0]
    my_col = meta[2 * orb_rows, 1]
    for step in range(kept_ref.shape[0]):
        for t in range(orb_rows):
            orbital = (my_row ^ step) * orb_rows + t
            for i in range(orb_rows):
                block = k_ref[i, orbital]
                keep = jnp.where(meta[i, orbital] > 0, block, jnp.zeros_like(block))
                kept_ref[step, i * virt : (i + 1) * virt, t * virt : (t + 1) * virt] = keep
    virt_pair = virt_col[...] + virt_row[...]
    for i in range(orb_rows):
        own_ref[i] = k_ref[i, my_col]
        inverse_ref[i] = 1.0 / (virt_pair - occupied[0, my_row * orb_rows + i] - occupied[0, my_col])


def prologue(rows, meta, coulomb, virtual_energy, occupied_energy):
    orb_rows, count, virt, _ = coulomb.shape
    shape = (
        jax.ShapeDtypeStruct((rows, orb_rows * virt, orb_rows * virt), jnp.bfloat16),
        jax.ShapeDtypeStruct((orb_rows, virt, virt), jnp.bfloat16),
        jax.ShapeDtypeStruct((orb_rows, virt, virt), jnp.float32),
    )
    return call(
        prologue_body, shape, [SMEM, SMEM, VMEM, VMEM, VMEM], 0, 4 * orb_rows * count * virt**2,
        meta, occupied_energy[None], coulomb, virtual_energy[None], virtual_energy[:, None],
    )


def coupled_body(rows, k_ref, *refs):
    out_ref = refs[rows]
    orb_rows, virt, _ = out_ref.shape
    total = None
    for step in range(rows):
        part = jnp.dot(
            k_ref[step], refs[step][...].reshape(orb_rows * virt, virt), preferred_element_type=jnp.float32
        )
        total = part if total is None else total + part
    out_ref[...] = total.astype(out_ref.dtype).reshape(out_ref.shape)


def coupled_blocks(rows, kept, pieces):
    orb_rows, virt, _ = pieces[0].shape
    count = rows * orb_rows
    shape = jax.ShapeDtypeStruct((orb_rows, virt, virt), jnp.bfloat16)
    body = functools.partial(coupled_body, rows)
    flops, moved = 2 * orb_rows * count * virt**3, 2 * (orb_rows + 1) * count * virt**2
    return call(body, shape, [VMEM] * (1 + rows), flops, moved, kept, *pieces)


def placed(meta, ref, hops, out_ref):
    orb_rows = ref.shape[0]
    halves = out_ref.shape[0] // orb_rows
    for hop in hops:
        spot = meta[2 * orb_rows, 1] // 2 + hop

        @pl.when(jnp.logical_and(spot >= 0, spot < halves))
        def _():
            out_ref[pl.ds(spot * orb_rows, orb_rows)] = ref[...]


def early_body(places, meta, *refs):
    out_ref = refs[len(places)]
    for ref, hops in zip(refs, places):
        placed(meta, ref, hops, out_ref)


def early_column(meta, halves, pieces, places):
    orb_rows, virt, _ = pieces[0].shape
    shape = jax.ShapeDtypeStruct((orb_rows * halves + 1, virt, virt), jnp.bfloat16)
    body = functools.partial(early_body, places)
    moved = 4 * (orb_rows * halves + 1) * virt**2
    return call(body, shape, [SMEM] + [VMEM] * len(pieces), 0, moved, meta, *pieces)


def whole_body(hops, meta, early_ref, crossed_ref, last_ref, part_ref, out_ref):
    orb_rows = crossed_ref.shape[0]
    placed(meta, last_ref, hops, out_ref)
    out_ref[out_ref.shape[0] - 1] = crossed_ref[1 - meta[2 * orb_rows, 1] % 2]


def whole_column(meta, early, crossed, last, hops, part):
    return pl.pallas_call(
        functools.partial(whole_body, hops),
        out_shape=jax.ShapeDtypeStruct(early.shape, early.dtype),
        in_specs=[SMEM] + [VMEM] * 4,
        out_specs=VMEM,
        input_output_aliases={1: 0},
        compiler_params=pltpu.CompilerParams(vmem_limit_bytes=VMEM_BYTES),
    )(meta, early, crossed, last, part)


def quadratic_part(rows, meta, side, left_ref, c_refs, kept):
    orb_rows = c_refs[0].shape[0]
    my_row = meta[2 * orb_rows, 0]
    total = None
    for step in range(rows):
        at = my_row ^ step
        blocks = []
        for i in range(orb_rows):
            block = left_ref[at * orb_rows + i]
            use = jnp.logical_and(meta[orb_rows + i, 2 * at + side] > 0, kept(at))
            blocks.append(jnp.where(use, block, jnp.zeros_like(block)))
        part = jnp.dot(jnp.concatenate(blocks, axis=0), c_refs[step][side], preferred_element_type=jnp.float32)
        total = part if total is None else total + part
    return total


def is_late(meta, hops, orb_rows):
    my_place = meta[2 * orb_rows, 1] // 2

    def test(at):
        late = at == my_place + hops[0]
        for hop in hops[1:]:
            late = jnp.logical_or(late, at == my_place + hop)
        return late

    return test


def turned(block):
    return jnp.transpose(block.astype(jnp.float32), (1, 0))


def first_body(rows, hops, meta, early_ref, *refs):
    c_refs = refs[:rows]
    state_ref, coulomb_ref, inverse_ref, out_ref = refs[rows:]
    orb_rows = out_ref.shape[0]
    side = meta[2 * orb_rows, 1] % 2
    late = is_late(meta, hops, orb_rows)
    quadratic = quadratic_part(rows, meta, side, early_ref, c_refs, lambda at: jnp.logical_not(late(at)))
    linear = coulomb_ref[...].astype(jnp.float32) + coupling * c_refs[0][...].astype(jnp.float32)
    residual = linear + coupling * coupling * quadratic.reshape(out_ref.shape)
    out_ref[...] = damping * state_ref[...] - residual * inverse_ref[...]


def second_body(rows, hops, meta, own_ref, swapped_ref, *refs):
    c_refs = refs[:rows]
    crossed_ref, part_ref, inverse_ref, out_ref, half_ref = refs[rows:]
    orb_rows = out_ref.shape[0]
    side = meta[2 * orb_rows, 1] % 2
    late = is_late(meta, hops, orb_rows)
    quadratic = quadratic_part(rows, meta, side, own_ref, c_refs, late)
    quadratic += quadratic_part(rows, meta, 1 - side, swapped_ref, c_refs, lambda at: True)
    out_ref[...] = part_ref[...] - coupling * coupling * quadratic.reshape(out_ref.shape) * inverse_ref[...]
    out_ref[side] -= coupling * turned(crossed_ref[side]) * inverse_ref[side]
    out_ref[1 - side] -= coupling * turned(swapped_ref[swapped_ref.shape[0] - 1]) * inverse_ref[1 - side]
    half_ref[...] = out_ref[...].astype(half_ref.dtype)


def first_update(rows, hops, meta, early, c_pieces, state, coulomb_own, inverse):
    orb_rows, virt, _ = state.shape
    shape = jax.ShapeDtypeStruct((orb_rows, virt, virt), jnp.float32)
    flops, moved = orb_rows**2 * rows * virt**3, 2 * (orb_rows + 1) * orb_rows * rows * virt**2
    return call(
        functools.partial(first_body, rows, hops), shape, [SMEM] + [VMEM] * (rows + 4), flops, moved,
        meta, early, *c_pieces, state, coulomb_own, inverse,
    )


def second_update(rows, hops, meta, own, swapped, c_pieces, crossed, part, inverse):
    orb_rows, virt, _ = part.shape
    shape = (
        jax.ShapeDtypeStruct((orb_rows, virt, virt), jnp.float32),
        jax.ShapeDtypeStruct((orb_rows, virt, virt), jnp.bfloat16),
    )
    flops, moved = orb_rows**2 * rows * virt**3, 2 * (orb_rows + 1) * orb_rows * rows * virt**2
    return call(
        functools.partial(second_body, rows, hops), shape, [SMEM] + [VMEM] * (rows + 5), flops, moved,
        meta, own, swapped, *c_pieces, crossed, part, inverse,
    )


def on_device(
    rows,
    cols,
    amplitudes,
    coulomb,
    inner_list,
    inner_count,
    reader_list,
    reader_count,
    virtual_energy,
    occupied_energy,
):
    orb_rows, orb_cols, virt, _ = amplitudes.shape
    count = coulomb.shape[1]
    slots = inner_list.shape[2]
    assert orb_cols == 1 and count == cols == rows * orb_rows and orb_rows == 2
    halves = cols // 2
    my_row = lax.axis_index("row")
    my_col = lax.axis_index("col")

    def from_row(x, step):
        return lax.ppermute(x, "row", [(r ^ step, r) for r in range(rows)])

    def along(x, hops):
        return lax.ppermute(
            x, "col", [(2 * at + k, 2 * (at + hop) + k) for at, hop in hops for k in range(2)]
        )

    def relayed(x):
        pieces, places = [x], [(0,)]
        up = down = x
        for stage in range(1, halves):
            ups = [(at, 1) for at in range(stage - 1, halves - 1)]
            downs = [(at, -1) for at in range(1, halves - stage + 1)]
            if stage - 1 > halves - stage:
                up = down = along(jnp.where(my_col // 2 >= stage - 1, up, down), ups + downs)
                pieces.append(up)
                places.append((-stage, stage))
            else:
                up, down = along(up, ups), along(down, downs)
                pieces += [up, down]
                places += [(-stage,), (stage,)]
        return pieces, tuple(places)

    def across(x):
        pairs = [(r * cols + c, (c // 2) * cols + 2 * r + c % 2) for r in range(rows) for c in range(cols)]
        return lax.ppermute(x, ("row", "col"), pairs)

    state = amplitudes[:, 0]
    half = state.astype(jnp.bfloat16)

    slot_iota = jnp.arange(slots, dtype=jnp.int32)
    orbital_iota = jnp.arange(count, dtype=jnp.int32)

    def used(lists, counts):
        live = slot_iota[None] < counts[:, None]
        hit = (lists[:, :, None] == orbital_iota) & live[:, :, None]
        return jnp.any(hit, axis=1).astype(jnp.int32)

    inner_used = used(inner_list[:, 0], inner_count[:, 0])
    reader_used = used(
        lax.dynamic_index_in_dim(reader_list, my_col, 1, False), lax.dynamic_index_in_dim(reader_count, my_col, 1, False)
    )
    place = jnp.where(orbital_iota == 0, my_row, my_col).astype(jnp.int32)
    meta = jnp.concatenate([inner_used, reader_used, place[None]], axis=0)

    kept, coulomb_own, inverse = prologue(rows, meta, coulomb, virtual_energy, occupied_energy)

    for sweep_index in range(ITERS):
        a_pieces = [half] + [from_row(half, step) for step in range(1, rows)]
        column, places = relayed(half)
        coupled = coupled_blocks(rows, kept, a_pieces)
        c_pieces = [coupled] + [from_row(coupled, step) for step in range(1, rows)]
        crossed = across(coupled)
        early = early_column(meta, halves, column[:-1], places[:-1])
        part = first_update(rows, places[-1], meta, early, c_pieces, state, coulomb_own, inverse)
        own = whole_column(meta, early, crossed, column[-1], places[-1], part)
        swapped = lax.ppermute(own, "col", [(c ^ 1, c) for c in range(cols)])
        state, half = second_update(rows, places[-1], meta, own, swapped, c_pieces, crossed, part, inverse)
    return state[:, None]


def solution(mesh):
    return jax.shard_map(
        functools.partial(on_device, mesh.shape["row"], mesh.shape["col"]),
        mesh=mesh,
        in_specs=(
            P("row", "col", None, None),
            P("row", None, None, None),
            P("row", "col", None),
            P("row", "col"),
            P("row", None, None),
            P("row", None),
            P(),
            P(),
        ),
        out_specs=P("row", "col", None, None),
        check_vma=False,
    )
```

```python
import functools

import jax
import jax.numpy as jnp
from jax import lax
from jax.experimental import pallas as pl
from jax.experimental.pallas import tpu as pltpu
from jax.sharding import PartitionSpec as P

ITERS = 2


damping = 0.5
coupling = 0.03125
ANY = pl.BlockSpec(memory_space=pl.ANY)
SMEM = pl.BlockSpec(memory_space=pltpu.SMEM)
VMEM = pl.BlockSpec(memory_space=pltpu.VMEM)
VMEM_BYTES = 32 * 1024 * 1024


def call(body, out_shape, in_specs, flops, moved, *operands):
    single = isinstance(out_shape, jax.ShapeDtypeStruct)
    return pl.pallas_call(
        body,
        out_shape=out_shape,
        in_specs=in_specs,
        out_specs=VMEM if single else (VMEM,) * len(out_shape),
        compiler_params=pltpu.CompilerParams(vmem_limit_bytes=VMEM_BYTES),
        cost_estimate=pl.CostEstimate(flops=flops, bytes_accessed=moved, transcendentals=0),
    )(*operands)


def prologue_body(meta, occupied, k_ref, virt_row, virt_col, kept_ref, own_ref, inverse_ref):
    orb_rows, _, virt, _ = k_ref.shape
    my_row = meta[2 * orb_rows, 0]
    my_col = meta[2 * orb_rows, 1]
    for step in range(kept_ref.shape[0]):
        for t in range(orb_rows):
            orbital = (my_row ^ step) * orb_rows + t
            for i in range(orb_rows):
                block = k_ref[i, orbital]
                keep = jnp.where(meta[i, orbital] > 0, block, jnp.zeros_like(block))
                kept_ref[step, i * virt : (i + 1) * virt, t * virt : (t + 1) * virt] = keep
    virt_pair = virt_col[...] + virt_row[...]
    for i in range(orb_rows):
        own_ref[i] = k_ref[i, my_col]
        inverse_ref[i] = 1.0 / (virt_pair - occupied[0, my_row * orb_rows + i] - occupied[0, my_col])


def prologue(rows, meta, coulomb, virtual_energy, occupied_energy):
    orb_rows, count, virt, _ = coulomb.shape
    shape = (
        jax.ShapeDtypeStruct((rows, orb_rows * virt, orb_rows * virt), jnp.bfloat16),
        jax.ShapeDtypeStruct((orb_rows, virt, virt), jnp.bfloat16),
        jax.ShapeDtypeStruct((orb_rows, virt, virt), jnp.float32),
    )
    return call(
        prologue_body, shape, [SMEM, SMEM, VMEM, VMEM, VMEM], 0, 4 * orb_rows * count * virt**2,
        meta, occupied_energy[None], coulomb, virtual_energy[None], virtual_energy[:, None],
    )


def piece_blocks(refs, rows):
    found, refs, size = [], list(refs), refs[0].shape[0]
    for step in range(rows):
        blocks = []
        while len(blocks) < size:
            ref = refs.pop(0)
            blocks += [(ref, at) for at in range(ref.shape[0])]
        found.append(blocks)
    return found


def coupled_body(rows, k_ref, *refs):
    out_ref = refs[-1]
    orb_rows, virt, _ = out_ref.shape
    blocks = piece_blocks(refs[:-1], rows)
    total = None
    for step in range(rows):
        for t in range(orb_rows):
            ref, at = blocks[step][t]
            left = k_ref[step, :, t * virt : (t + 1) * virt]
            part = jnp.dot(left, ref[at], preferred_element_type=jnp.float32)
            total = part if total is None else total + part
    out_ref[...] = total.astype(out_ref.dtype).reshape(out_ref.shape)


def coupled_blocks(rows, kept, pieces):
    orb_rows, virt, _ = pieces[0].shape
    count = rows * orb_rows
    shape = jax.ShapeDtypeStruct((orb_rows, virt, virt), jnp.bfloat16)
    body = functools.partial(coupled_body, rows)
    flops, moved = 2 * orb_rows * count * virt**3, 2 * (orb_rows + 1) * count * virt**2
    return call(body, shape, [VMEM] * (1 + len(pieces)), flops, moved, kept, *pieces)


def placed(meta, ref, hops, out_ref):
    orb_rows = ref.shape[0]
    halves = out_ref.shape[0] // orb_rows
    for hop in hops:
        spot = meta[2 * orb_rows, 1] // 2 + hop

        @pl.when(jnp.logical_and(spot >= 0, spot < halves))
        def _():
            out_ref[pl.ds(spot * orb_rows, orb_rows)] = ref[...]


def column_body(places, meta, crossing_ref, *refs):
    out_ref, same_ref, other_ref = refs[-3:]
    side = meta[2 * crossing_ref.shape[0], 1] % 2
    for ref, hops in zip(refs, places):
        placed(meta, ref, hops, out_ref)
    same_ref[...] = crossing_ref[side]
    other_ref[...] = crossing_ref[1 - side]


def whole_column(meta, halves, pieces, places, crossing, others):
    orb_rows, virt, _ = pieces[0].shape
    block = jax.ShapeDtypeStruct((virt, virt), jnp.bfloat16)
    shape = (jax.ShapeDtypeStruct((orb_rows * halves, virt, virt), jnp.bfloat16), block, block)
    operands = [crossing, *pieces, *others]
    moved = 4 * orb_rows * (halves + 1) * virt**2
    body = functools.partial(column_body, places)
    return call(body, shape, [SMEM] + [VMEM] * len(operands), 0, moved, meta, *operands)


def masked_pair(meta, orbital, blocks):
    orb_rows = len(blocks)
    kept = [jnp.where(meta[orb_rows + i, orbital] > 0, block, jnp.zeros_like(block)) for i, block in enumerate(blocks)]
    return jnp.concatenate(kept, axis=0)


def turned(block):
    return jnp.transpose(block.astype(jnp.float32), (1, 0))


def first_body(rows, meta, own_ref, other_ref, *refs):
    state_ref, coulomb_ref, inverse_ref, out_ref = refs[-4:]
    orb_rows = out_ref.shape[0]
    blocks = piece_blocks(refs[:-4], rows)
    my_row, side = meta[2 * orb_rows, 0], meta[2 * orb_rows, 1] % 2
    total = None
    for step in range(rows):
        at = my_row ^ step
        for t in range(orb_rows):
            left = [
                jnp.where(side == t, own_ref[at * orb_rows + i], other_ref[at * orb_rows + i]) for i in range(orb_rows)
            ]
            ref, place = blocks[step][t]
            left = masked_pair(meta, at * orb_rows + t, left)
            part = jnp.dot(left, ref[place], preferred_element_type=jnp.float32)
            total = part if total is None else total + part
    linear = coulomb_ref[...].astype(jnp.float32) + coupling * refs[0][...].astype(jnp.float32)
    residual = linear + coupling * coupling * total.reshape(out_ref.shape)
    out_ref[...] = damping * state_ref[...] - residual * inverse_ref[...]


def second_body(meta, same_ref, other_ref, part_ref, inverse_ref, out_ref, half_ref):
    side = meta[2 * out_ref.shape[0], 1] % 2
    for ref, at in ((same_ref, side), (other_ref, 1 - side)):
        state = part_ref[at] - coupling * turned(ref[...]) * inverse_ref[at]
        out_ref[at] = state
        half_ref[at] = state.astype(half_ref.dtype)


def first_update(rows, meta, own, other, c_pieces, state, coulomb_own, inverse):
    orb_rows, virt, _ = state.shape
    shape = jax.ShapeDtypeStruct(state.shape, jnp.float32)
    flops, moved = 2 * orb_rows**2 * rows * virt**3, 4 * (orb_rows + 1) * orb_rows * rows * virt**2
    return call(
        functools.partial(first_body, rows), shape, [SMEM] + [VMEM] * (len(c_pieces) + 5), flops, moved,
        meta, own, other, *c_pieces, state, coulomb_own, inverse,
    )


def second_update(meta, same, other, part, inverse):
    shape = (jax.ShapeDtypeStruct(part.shape, jnp.float32), jax.ShapeDtypeStruct(part.shape, jnp.bfloat16))
    return call(second_body, shape, [SMEM] + [VMEM] * 4, 0, 16 * part.size, meta, same, other, part, inverse)


def on_device(
    rows,
    cols,
    amplitudes,
    coulomb,
    inner_list,
    inner_count,
    reader_list,
    reader_count,
    virtual_energy,
    occupied_energy,
):
    orb_rows, orb_cols, virt, _ = amplitudes.shape
    count = coulomb.shape[1]
    slots = inner_list.shape[2]
    assert orb_cols == 1 and count == cols == rows * orb_rows and orb_rows == 2
    halves = cols // 2
    my_row = lax.axis_index("row")
    my_col = lax.axis_index("col")

    def from_row(x, step):
        return lax.ppermute(x, "row", [(r ^ step, r) for r in range(rows)])

    def row_gathered(x, halved):
        near = from_row(x, 1)
        pieces = [x, near]
        for step in range(2, rows, 2):
            piece = from_row(x, step)
            if halved:
                pieces += [piece, from_row(piece[0:1], 1), from_row(near[1:2], step)]
            else:
                pieces += [piece, from_row(near, step)]
        return pieces

    def swapped(x):
        return lax.ppermute(x, "col", [(c ^ 1, c) for c in range(cols)])

    def along(x, hops):
        return lax.ppermute(
            x, "col", [(2 * at + k, 2 * (at + hop) + k) for at, hop in hops for k in range(2)]
        )

    def relayed(x):
        pieces, places = [x], [(0,)]
        up = down = x
        for stage in range(1, halves):
            ups = [(at, 1) for at in range(stage - 1, halves - 1)]
            downs = [(at, -1) for at in range(1, halves - stage + 1)]
            if stage - 1 > halves - stage:
                up = down = along(jnp.where(my_col // 2 >= stage - 1, up, down), ups + downs)
                pieces.append(up)
                places.append((-stage, stage))
            else:
                up, down = along(up, ups), along(down, downs)
                pieces += [up, down]
                places += [(-stage,), (stage,)]
        return pieces, tuple(places)

    def crossing(x, place, flip=0):
        pairs = []
        for r in range(rows):
            for c in range(cols):
                to_r, to_z = place(r, c // 2)
                pairs.append((r * cols + c, to_r * cols + 2 * to_z + (c % 2 ^ flip)))
        return lax.ppermute(x, ("row", "col"), pairs)

    def high_parts(r, z):
        return z - z % 2 + r % 2, r - r % 2 + z % 2

    def last_bits(r, z):
        return r - r % 2 + z % 2, z - z % 2 + r % 2

    state = amplitudes[:, 0]
    half = state.astype(jnp.bfloat16)

    slot_iota = jnp.arange(slots, dtype=jnp.int32)
    orbital_iota = jnp.arange(count, dtype=jnp.int32)

    def used(lists, counts):
        live = slot_iota[None] < counts[:, None]
        hit = (lists[:, :, None] == orbital_iota) & live[:, :, None]
        return jnp.any(hit, axis=1).astype(jnp.int32)

    inner_used = used(inner_list[:, 0], inner_count[:, 0])
    reader_used = used(
        lax.dynamic_index_in_dim(reader_list, my_col, 1, False), lax.dynamic_index_in_dim(reader_count, my_col, 1, False)
    )
    place = jnp.where(orbital_iota == 0, my_row, my_col).astype(jnp.int32)
    meta = jnp.concatenate([inner_used, reader_used, place[None]], axis=0)

    kept, coulomb_own, inverse = prologue(rows, meta, coulomb, virtual_energy, occupied_energy)

    for sweep_index in range(ITERS):
        a_pieces = row_gathered(half, True)
        column, places = relayed(half)
        coupled = coupled_blocks(rows, kept, a_pieces)
        c_pieces = row_gathered(coupled, False)
        half_way = crossing(coupled, high_parts)
        own, same, other = whole_column(meta, halves, column, places, half_way, c_pieces[1:3])
        same, other = crossing(same, last_bits), crossing(other, last_bits, 1)
        part = first_update(rows, meta, own, swapped(own), c_pieces, state, coulomb_own, inverse)
        state, half = second_update(meta, same, other, part, inverse)
    return state[:, None]


def solution(mesh):
    return jax.shard_map(
        functools.partial(on_device, mesh.shape["row"], mesh.shape["col"]),
        mesh=mesh,
        in_specs=(
            P("row", "col", None, None),
            P("row", None, None, None),
            P("row", "col", None),
            P("row", "col"),
            P("row", None, None),
            P("row", None),
            P(),
            P(),
        ),
        out_specs=P("row", "col", None, None),
        check_vma=False,
    )
```

```python
import functools

import jax
import jax.numpy as jnp
from jax import lax
from jax.experimental import pallas as pl
from jax.experimental.pallas import tpu as pltpu
from jax.sharding import PartitionSpec as P

ITERS = 2


damping = 0.5
coupling = 0.03125
ANY = pl.BlockSpec(memory_space=pl.ANY)
SMEM = pl.BlockSpec(memory_space=pltpu.SMEM)
VMEM = pl.BlockSpec(memory_space=pltpu.VMEM)
VMEM_BYTES = 32 * 1024 * 1024


def call(body, out_shape, in_specs, flops, moved, *operands):
    single = isinstance(out_shape, jax.ShapeDtypeStruct)
    return pl.pallas_call(
        body,
        out_shape=out_shape,
        in_specs=in_specs,
        out_specs=VMEM if single else (VMEM,) * len(out_shape),
        compiler_params=pltpu.CompilerParams(vmem_limit_bytes=VMEM_BYTES),
        cost_estimate=pl.CostEstimate(flops=flops, bytes_accessed=moved, transcendentals=0),
    )(*operands)


def prologue_body(meta, occupied, k_ref, virt_row, virt_col, kept_ref, own_ref, inverse_ref):
    orb_rows, _, virt, _ = k_ref.shape
    my_row = meta[2 * orb_rows, 0]
    my_col = meta[2 * orb_rows, 1]
    for step in range(kept_ref.shape[0]):
        for t in range(orb_rows):
            orbital = (my_row ^ step) * orb_rows + t
            for i in range(orb_rows):
                block = k_ref[i, orbital]
                keep = jnp.where(meta[i, orbital] > 0, block, jnp.zeros_like(block))
                kept_ref[step, i * virt : (i + 1) * virt, t * virt : (t + 1) * virt] = keep
    virt_pair = virt_col[...] + virt_row[...]
    for i in range(orb_rows):
        own_ref[i] = k_ref[i, my_col]
        inverse_ref[i] = 1.0 / (virt_pair - occupied[0, my_row * orb_rows + i] - occupied[0, my_col])


def prologue(rows, meta, coulomb, virtual_energy, occupied_energy):
    orb_rows, count, virt, _ = coulomb.shape
    shape = (
        jax.ShapeDtypeStruct((rows, orb_rows * virt, orb_rows * virt), jnp.bfloat16),
        jax.ShapeDtypeStruct((orb_rows, virt, virt), jnp.bfloat16),
        jax.ShapeDtypeStruct((orb_rows, virt, virt), jnp.float32),
    )
    return call(
        prologue_body, shape, [SMEM, SMEM, VMEM, VMEM, VMEM], 0, 4 * orb_rows * count * virt**2,
        meta, occupied_energy[None], coulomb, virtual_energy[None], virtual_energy[:, None],
    )


def piece_blocks(refs, rows):
    found, refs, size = [], list(refs), refs[0].shape[0]
    for step in range(rows):
        blocks = []
        while len(blocks) < size:
            ref = refs.pop(0)
            blocks += [(ref, at) for at in range(ref.shape[0])]
        found.append(blocks)
    return found


def coupled_body(rows, k_ref, *refs):
    out_ref = refs[-1]
    orb_rows, virt, _ = out_ref.shape
    blocks = piece_blocks(refs[:-1], rows)
    total = None
    for step in range(rows):
        for t in range(orb_rows):
            ref, at = blocks[step][t]
            left = k_ref[step, :, t * virt : (t + 1) * virt]
            part = jnp.dot(left, ref[at], preferred_element_type=jnp.float32)
            total = part if total is None else total + part
    out_ref[...] = total.astype(out_ref.dtype).reshape(out_ref.shape)


def coupled_blocks(rows, kept, pieces):
    orb_rows, virt, _ = pieces[0].shape
    count = rows * orb_rows
    shape = jax.ShapeDtypeStruct((orb_rows, virt, virt), jnp.bfloat16)
    body = functools.partial(coupled_body, rows)
    flops, moved = 2 * orb_rows * count * virt**3, 2 * (orb_rows + 1) * count * virt**2
    return call(body, shape, [VMEM] * (1 + len(pieces)), flops, moved, kept, *pieces)


def parted_body(meta, crossing_ref, *refs):
    same_ref, other_ref = refs[-2:]
    side = meta[2 * crossing_ref.shape[0], 1] % 2
    same_ref[...] = crossing_ref[side]
    other_ref[...] = crossing_ref[1 - side]


def parted(meta, crossing, others):
    block = jax.ShapeDtypeStruct(crossing.shape[1:], crossing.dtype)
    in_specs = [SMEM] + [VMEM] * (1 + len(others))
    return call(parted_body, (block, block), in_specs, 0, 4 * crossing.size, meta, crossing, *others)


def tied_body(*refs):
    pass


def tied(x, *others):
    return pl.pallas_call(
        tied_body,
        out_shape=jax.ShapeDtypeStruct(x.shape, x.dtype),
        in_specs=[VMEM] * (1 + len(others)),
        out_specs=VMEM,
        input_output_aliases={0: 0},
        compiler_params=pltpu.CompilerParams(vmem_limit_bytes=VMEM_BYTES),
    )(x, *others)


def masked_pair(meta, orbital, blocks):
    orb_rows = len(blocks)
    kept = [jnp.where(meta[orb_rows + i, orbital] > 0, block, jnp.zeros_like(block)) for i, block in enumerate(blocks)]
    return jnp.concatenate(kept, axis=0)


def turned(block):
    return jnp.transpose(block.astype(jnp.float32), (1, 0))


def first_body(rows, meta, own_ref, other_ref, *refs):
    state_ref, coulomb_ref, inverse_ref, out_ref = refs[-4:]
    orb_rows = out_ref.shape[0]
    blocks = piece_blocks(refs[:-4], rows)
    my_row, side = meta[2 * orb_rows, 0], meta[2 * orb_rows, 1] % 2
    total = None
    for step in range(rows):
        at = my_row ^ step
        for t in range(orb_rows):
            left = [
                jnp.where(side == t, own_ref[at * orb_rows + i], other_ref[at * orb_rows + i]) for i in range(orb_rows)
            ]
            ref, place = blocks[step][t]
            left = masked_pair(meta, at * orb_rows + t, left)
            part = jnp.dot(left, ref[place], preferred_element_type=jnp.float32)
            total = part if total is None else total + part
    linear = coulomb_ref[...].astype(jnp.float32) + coupling * refs[0][...].astype(jnp.float32)
    residual = linear + coupling * coupling * total.reshape(out_ref.shape)
    out_ref[...] = damping * state_ref[...] - residual * inverse_ref[...]


def second_body(meta, same_ref, other_ref, part_ref, inverse_ref, out_ref, half_ref):
    side = meta[2 * out_ref.shape[0], 1] % 2
    for ref, at in ((same_ref, side), (other_ref, 1 - side)):
        state = part_ref[at] - coupling * turned(ref[...]) * inverse_ref[at]
        out_ref[at] = state
        half_ref[at] = state.astype(half_ref.dtype)


def first_update(rows, meta, own, other, c_pieces, state, coulomb_own, inverse):
    orb_rows, virt, _ = state.shape
    shape = jax.ShapeDtypeStruct(state.shape, jnp.float32)
    flops, moved = 2 * orb_rows**2 * rows * virt**3, 4 * (orb_rows + 1) * orb_rows * rows * virt**2
    return call(
        functools.partial(first_body, rows), shape, [SMEM] + [VMEM] * (len(c_pieces) + 5), flops, moved,
        meta, own, other, *c_pieces, state, coulomb_own, inverse,
    )


def second_update(meta, same, other, part, inverse):
    shape = (jax.ShapeDtypeStruct(part.shape, jnp.float32), jax.ShapeDtypeStruct(part.shape, jnp.bfloat16))
    return call(second_body, shape, [SMEM] + [VMEM] * 4, 0, 16 * part.size, meta, same, other, part, inverse)


def on_device(
    rows,
    cols,
    amplitudes,
    coulomb,
    inner_list,
    inner_count,
    reader_list,
    reader_count,
    virtual_energy,
    occupied_energy,
):
    orb_rows, orb_cols, virt, _ = amplitudes.shape
    count = coulomb.shape[1]
    slots = inner_list.shape[2]
    assert orb_cols == 1 and count == cols == rows * orb_rows and orb_rows == 2
    halves = cols // 2
    my_row = lax.axis_index("row")
    my_col = lax.axis_index("col")

    def from_row(x, step):
        return lax.ppermute(x, "row", [(r ^ step, r) for r in range(rows)])

    def row_gathered(x, halved):
        near = from_row(x, 1)
        pieces = [x, near]
        for step in range(2, rows, 2):
            piece = from_row(x, step)
            if halved:
                pieces += [piece, from_row(piece[0:1], 1), from_row(near[1:2], step)]
            else:
                pieces += [piece, from_row(near, step)]
        return pieces

    def swapped(x):
        return lax.ppermute(x, "col", [(c ^ 1, c) for c in range(cols)])

    one_core = [[2 * at + side for at in range(halves)] for side in range(2)]

    def crossing(x, place, flip=0):
        pairs = []
        for r in range(rows):
            for c in range(cols):
                to_r, to_z = place(r, c // 2)
                pairs.append((r * cols + c, to_r * cols + 2 * to_z + (c % 2 ^ flip)))
        return lax.ppermute(x, ("row", "col"), pairs)

    def high_parts(r, z):
        return z - z % 2 + r % 2, r - r % 2 + z % 2

    def last_bits(r, z):
        return r - r % 2 + z % 2, z - z % 2 + r % 2

    state = amplitudes[:, 0]
    half = state.astype(jnp.bfloat16)

    slot_iota = jnp.arange(slots, dtype=jnp.int32)
    orbital_iota = jnp.arange(count, dtype=jnp.int32)

    def used(lists, counts):
        live = slot_iota[None] < counts[:, None]
        hit = (lists[:, :, None] == orbital_iota) & live[:, :, None]
        return jnp.any(hit, axis=1).astype(jnp.int32)

    inner_used = used(inner_list[:, 0], inner_count[:, 0])
    reader_used = used(
        lax.dynamic_index_in_dim(reader_list, my_col, 1, False), lax.dynamic_index_in_dim(reader_count, my_col, 1, False)
    )
    place = jnp.where(orbital_iota == 0, my_row, my_col).astype(jnp.int32)
    meta = jnp.concatenate([inner_used, reader_used, place[None]], axis=0)

    kept, coulomb_own, inverse = prologue(rows, meta, coulomb, virtual_energy, occupied_energy)

    for sweep_index in range(ITERS):
        a_pieces = row_gathered(half, True)
        own = lax.all_gather(half, "col", axis=0, tiled=True, axis_index_groups=one_core)
        coupled = coupled_blocks(rows, kept, a_pieces)
        c_pieces = row_gathered(coupled, False)
        half_way = crossing(coupled, high_parts)
        same, other = parted(meta, half_way, c_pieces[1:3])
        own = tied(own, same)
        same, other = crossing(same, last_bits), crossing(other, last_bits, 1)
        part = first_update(rows, meta, own, swapped(own), c_pieces, state, coulomb_own, inverse)
        state, half = second_update(meta, same, other, part, inverse)
    return state[:, None]


def solution(mesh):
    return jax.shard_map(
        functools.partial(on_device, mesh.shape["row"], mesh.shape["col"]),
        mesh=mesh,
        in_specs=(
            P("row", "col", None, None),
            P("row", None, None, None),
            P("row", "col", None),
            P("row", "col"),
            P("row", None, None),
            P("row", None),
            P(),
            P(),
        ),
        out_specs=P("row", "col", None, None),
        check_vma=False,
    )
```

```python
import functools

import jax
import jax.numpy as jnp
from jax import lax
from jax.experimental import pallas as pl
from jax.experimental.pallas import tpu as pltpu
from jax.sharding import PartitionSpec as P

ITERS = 2


damping = 0.5
coupling = 0.03125
ANY = pl.BlockSpec(memory_space=pl.ANY)
SMEM = pl.BlockSpec(memory_space=pltpu.SMEM)
VMEM = pl.BlockSpec(memory_space=pltpu.VMEM)
VMEM_BYTES = 32 * 1024 * 1024


def call(body, out_shape, in_specs, flops, moved, *operands):
    single = isinstance(out_shape, jax.ShapeDtypeStruct)
    return pl.pallas_call(
        body,
        out_shape=out_shape,
        in_specs=in_specs,
        out_specs=VMEM if single else (VMEM,) * len(out_shape),
        compiler_params=pltpu.CompilerParams(vmem_limit_bytes=VMEM_BYTES),
        cost_estimate=pl.CostEstimate(flops=flops, bytes_accessed=moved, transcendentals=0),
    )(*operands)


def prologue_body(meta, occupied, k_ref, virt_row, virt_col, kept_ref, own_ref, inverse_ref):
    orb_rows, _, virt, _ = k_ref.shape
    my_row = meta[2 * orb_rows, 0]
    my_col = meta[2 * orb_rows, 1]
    for step in range(kept_ref.shape[0]):
        for t in range(orb_rows):
            orbital = (my_row ^ step) * orb_rows + t
            for i in range(orb_rows):
                block = k_ref[i, orbital]
                keep = jnp.where(meta[i, orbital] > 0, block, jnp.zeros_like(block))
                kept_ref[step, i * virt : (i + 1) * virt, t * virt : (t + 1) * virt] = keep
    virt_pair = virt_col[...] + virt_row[...]
    for i in range(orb_rows):
        own_ref[i] = k_ref[i, my_col]
        inverse_ref[i] = 1.0 / (virt_pair - occupied[0, my_row * orb_rows + i] - occupied[0, my_col])


def prologue(rows, meta, coulomb, virtual_energy, occupied_energy):
    orb_rows, count, virt, _ = coulomb.shape
    shape = (
        jax.ShapeDtypeStruct((rows, orb_rows * virt, orb_rows * virt), jnp.bfloat16),
        jax.ShapeDtypeStruct((orb_rows, virt, virt), jnp.bfloat16),
        jax.ShapeDtypeStruct((orb_rows, virt, virt), jnp.float32),
    )
    return call(
        prologue_body, shape, [SMEM, SMEM, VMEM, VMEM, VMEM], 0, 4 * orb_rows * count * virt**2,
        meta, occupied_energy[None], coulomb, virtual_energy[None], virtual_energy[:, None],
    )


def piece_blocks(refs, rows):
    found, refs, size = [], list(refs), refs[0].shape[0]
    for step in range(rows):
        blocks = []
        while len(blocks) < size:
            ref = refs.pop(0)
            blocks += [(ref, at) for at in range(ref.shape[0])]
        found.append(blocks)
    return found


def coupled_body(rows, k_ref, *refs):
    out_ref = refs[-1]
    orb_rows, virt, _ = out_ref.shape
    blocks = piece_blocks(refs[:-1], rows)
    total = None
    for step in range(rows):
        for t in range(orb_rows):
            ref, at = blocks[step][t]
            left = k_ref[step, :, t * virt : (t + 1) * virt]
            part = jnp.dot(left, ref[at], preferred_element_type=jnp.float32)
            total = part if total is None else total + part
    out_ref[...] = total.astype(out_ref.dtype).reshape(out_ref.shape)


def coupled_blocks(rows, kept, pieces):
    orb_rows, virt, _ = pieces[0].shape
    count = rows * orb_rows
    shape = jax.ShapeDtypeStruct((orb_rows, virt, virt), jnp.bfloat16)
    body = functools.partial(coupled_body, rows)
    flops, moved = 2 * orb_rows * count * virt**3, 2 * (orb_rows + 1) * count * virt**2
    return call(body, shape, [VMEM] * (1 + len(pieces)), flops, moved, kept, *pieces)


def column_body(meta, crossing_ref, *refs):
    out_ref, same_ref, other_ref = refs[-3:]
    orb_rows = crossing_ref.shape[0]
    my_col = meta[2 * orb_rows, 1]
    for step in range(out_ref.shape[0] // orb_rows):
        out_ref[pl.ds((my_col // 2 ^ step) * orb_rows, orb_rows)] = refs[step][...]
    same_ref[...] = crossing_ref[my_col % 2]
    other_ref[...] = crossing_ref[1 - my_col % 2]


def whole_column(meta, pieces, crossing, others):
    orb_rows, virt, _ = crossing.shape
    block = jax.ShapeDtypeStruct((virt, virt), jnp.bfloat16)
    shape = (jax.ShapeDtypeStruct((orb_rows * len(pieces), virt, virt), jnp.bfloat16), block, block)
    operands = [crossing, *pieces, *others]
    moved = 4 * orb_rows * (len(pieces) + 1) * virt**2
    return call(column_body, shape, [SMEM] + [VMEM] * len(operands), 0, moved, meta, *operands)


def masked_pair(meta, orbital, blocks):
    orb_rows = len(blocks)
    kept = [jnp.where(meta[orb_rows + i, orbital] > 0, block, jnp.zeros_like(block)) for i, block in enumerate(blocks)]
    return jnp.concatenate(kept, axis=0)


def turned(block):
    return jnp.transpose(block.astype(jnp.float32), (1, 0))


def first_body(rows, meta, own_ref, other_ref, *refs):
    state_ref, coulomb_ref, inverse_ref, out_ref = refs[-4:]
    orb_rows = out_ref.shape[0]
    blocks = piece_blocks(refs[:-4], rows)
    my_row, side = meta[2 * orb_rows, 0], meta[2 * orb_rows, 1] % 2
    total = None
    for step in range(rows):
        at = my_row ^ step
        for t in range(orb_rows):
            left = [
                jnp.where(side == t, own_ref[at * orb_rows + i], other_ref[at * orb_rows + i]) for i in range(orb_rows)
            ]
            ref, place = blocks[step][t]
            left = masked_pair(meta, at * orb_rows + t, left)
            part = jnp.dot(left, ref[place], preferred_element_type=jnp.float32)
            total = part if total is None else total + part
    linear = coulomb_ref[...].astype(jnp.float32) + coupling * refs[0][...].astype(jnp.float32)
    residual = linear + coupling * coupling * total.reshape(out_ref.shape)
    out_ref[...] = damping * state_ref[...] - residual * inverse_ref[...]


def second_body(meta, same_ref, other_ref, part_ref, inverse_ref, out_ref, half_ref):
    side = meta[2 * out_ref.shape[0], 1] % 2
    for ref, at in ((same_ref, side), (other_ref, 1 - side)):
        state = part_ref[at] - coupling * turned(ref[...]) * inverse_ref[at]
        out_ref[at] = state
        half_ref[at] = state.astype(half_ref.dtype)


def first_update(rows, meta, own, other, c_pieces, state, coulomb_own, inverse):
    orb_rows, virt, _ = state.shape
    shape = jax.ShapeDtypeStruct(state.shape, jnp.float32)
    flops, moved = 2 * orb_rows**2 * rows * virt**3, 4 * (orb_rows + 1) * orb_rows * rows * virt**2
    return call(
        functools.partial(first_body, rows), shape, [SMEM] + [VMEM] * (len(c_pieces) + 5), flops, moved,
        meta, own, other, *c_pieces, state, coulomb_own, inverse,
    )


def second_update(meta, same, other, part, inverse):
    shape = (jax.ShapeDtypeStruct(part.shape, jnp.float32), jax.ShapeDtypeStruct(part.shape, jnp.bfloat16))
    return call(second_body, shape, [SMEM] + [VMEM] * 4, 0, 16 * part.size, meta, same, other, part, inverse)


def on_device(
    rows,
    cols,
    amplitudes,
    coulomb,
    inner_list,
    inner_count,
    reader_list,
    reader_count,
    virtual_energy,
    occupied_energy,
):
    orb_rows, orb_cols, virt, _ = amplitudes.shape
    count = coulomb.shape[1]
    slots = inner_list.shape[2]
    assert orb_cols == 1 and count == cols == rows * orb_rows and orb_rows == 2
    halves = cols // 2
    my_row = lax.axis_index("row")
    my_col = lax.axis_index("col")

    def from_row(x, step):
        return lax.ppermute(x, "row", [(r ^ step, r) for r in range(rows)])

    def row_gathered(x, halved):
        near = from_row(x, 1)
        pieces = [x, near]
        for step in range(2, rows, 2):
            piece = from_row(x, step)
            if halved:
                pieces += [piece, from_row(piece[0:1], 1), from_row(near[1:2], step)]
            else:
                pieces += [piece, from_row(near, step)]
        return pieces

    def swapped(x):
        return lax.ppermute(x, "col", [(c ^ 1, c) for c in range(cols)])

    def column_gathered(x):
        def from_chip(x, step):
            return lax.ppermute(x, "col", [(c ^ 2 * step, c) for c in range(cols)])

        pieces = [x, from_chip(x, 1)]
        for step in range(2, halves, 2):
            piece = from_chip(x, step)
            pieces += [piece, from_chip(piece, 1)]
        return pieces

    def crossing(x, place, flip=0):
        pairs = []
        for r in range(rows):
            for c in range(cols):
                to_r, to_z = place(r, c // 2)
                pairs.append((r * cols + c, to_r * cols + 2 * to_z + (c % 2 ^ flip)))
        return lax.ppermute(x, ("row", "col"), pairs)

    def high_parts(r, z):
        return z - z % 2 + r % 2, r - r % 2 + z % 2

    def last_bits(r, z):
        return r - r % 2 + z % 2, z - z % 2 + r % 2

    state = amplitudes[:, 0]
    half = state.astype(jnp.bfloat16)

    slot_iota = jnp.arange(slots, dtype=jnp.int32)
    orbital_iota = jnp.arange(count, dtype=jnp.int32)

    def used(lists, counts):
        live = slot_iota[None] < counts[:, None]
        hit = (lists[:, :, None] == orbital_iota) & live[:, :, None]
        return jnp.any(hit, axis=1).astype(jnp.int32)

    inner_used = used(inner_list[:, 0], inner_count[:, 0])
    reader_used = used(
        lax.dynamic_index_in_dim(reader_list, my_col, 1, False), lax.dynamic_index_in_dim(reader_count, my_col, 1, False)
    )
    place = jnp.where(orbital_iota == 0, my_row, my_col).astype(jnp.int32)
    meta = jnp.concatenate([inner_used, reader_used, place[None]], axis=0)

    kept, coulomb_own, inverse = prologue(rows, meta, coulomb, virtual_energy, occupied_energy)

    for sweep_index in range(ITERS):
        a_pieces = row_gathered(half, True)
        column = column_gathered(half)
        coupled = coupled_blocks(rows, kept, a_pieces)
        c_pieces = row_gathered(coupled, False)
        half_way = crossing(coupled, high_parts)
        own, same, other = whole_column(meta, column, half_way, c_pieces[1:3])
        same, other = crossing(same, last_bits), crossing(other, last_bits, 1)
        part = first_update(rows, meta, own, swapped(own), c_pieces, state, coulomb_own, inverse)
        state, half = second_update(meta, same, other, part, inverse)
    return state[:, None]


def solution(mesh):
    return jax.shard_map(
        functools.partial(on_device, mesh.shape["row"], mesh.shape["col"]),
        mesh=mesh,
        in_specs=(
            P("row", "col", None, None),
            P("row", None, None, None),
            P("row", "col", None),
            P("row", "col"),
            P("row", None, None),
            P("row", None),
            P(),
            P(),
        ),
        out_specs=P("row", "col", None, None),
        check_vma=False,
    )
```

```python
import functools

import jax
import jax.numpy as jnp
from jax import lax
from jax.experimental import pallas as pl
from jax.experimental.pallas import tpu as pltpu
from jax.sharding import PartitionSpec as P

ITERS = 2


damping = 0.5
coupling = 0.03125
ANY = pl.BlockSpec(memory_space=pl.ANY)
SMEM = pl.BlockSpec(memory_space=pltpu.SMEM)
VMEM = pl.BlockSpec(memory_space=pltpu.VMEM)
VMEM_BYTES = 32 * 1024 * 1024


def call(body, out_shape, in_specs, flops, moved, *operands):
    single = isinstance(out_shape, jax.ShapeDtypeStruct)
    return pl.pallas_call(
        body,
        out_shape=out_shape,
        in_specs=in_specs,
        out_specs=VMEM if single else (VMEM,) * len(out_shape),
        compiler_params=pltpu.CompilerParams(vmem_limit_bytes=VMEM_BYTES),
        cost_estimate=pl.CostEstimate(flops=flops, bytes_accessed=moved, transcendentals=0),
    )(*operands)


def prologue_body(meta, occupied, k_ref, virt_row, virt_col, kept_ref, own_ref, inverse_ref):
    orb_rows, _, virt, _ = k_ref.shape
    my_row = meta[2 * orb_rows, 0]
    my_col = meta[2 * orb_rows, 1]
    for step in range(kept_ref.shape[0]):
        for t in range(orb_rows):
            orbital = (my_row ^ step) * orb_rows + t
            for i in range(orb_rows):
                block = k_ref[i, orbital]
                keep = jnp.where(meta[i, orbital] > 0, block, jnp.zeros_like(block))
                kept_ref[step, i * virt : (i + 1) * virt, t * virt : (t + 1) * virt] = keep
    virt_pair = virt_col[...] + virt_row[...]
    for i in range(orb_rows):
        own_ref[i] = k_ref[i, my_col]
        inverse_ref[i] = 1.0 / (virt_pair - occupied[0, my_row * orb_rows + i] - occupied[0, my_col])


def prologue(rows, meta, coulomb, virtual_energy, occupied_energy):
    orb_rows, count, virt, _ = coulomb.shape
    shape = (
        jax.ShapeDtypeStruct((rows, orb_rows * virt, orb_rows * virt), jnp.bfloat16),
        jax.ShapeDtypeStruct((orb_rows, virt, virt), jnp.bfloat16),
        jax.ShapeDtypeStruct((orb_rows, virt, virt), jnp.float32),
    )
    return call(
        prologue_body, shape, [SMEM, SMEM, VMEM, VMEM, VMEM], 0, 4 * orb_rows * count * virt**2,
        meta, occupied_energy[None], coulomb, virtual_energy[None], virtual_energy[:, None],
    )


def piece_blocks(refs, rows):
    found, refs, size = [], list(refs), refs[0].shape[0]
    for step in range(rows):
        blocks = []
        while len(blocks) < size:
            ref = refs.pop(0)
            blocks += [(ref, at) for at in range(ref.shape[0])]
        found.append(blocks)
    return found


def coupled_body(rows, k_ref, *refs):
    out_ref = refs[-1]
    orb_rows, virt, _ = out_ref.shape
    blocks = piece_blocks(refs[:-1], rows)
    total = None
    for step in range(rows):
        for t in range(orb_rows):
            ref, at = blocks[step][t]
            left = k_ref[step, :, t * virt : (t + 1) * virt]
            part = jnp.dot(left, ref[at], preferred_element_type=jnp.float32)
            total = part if total is None else total + part
    out_ref[...] = total.astype(out_ref.dtype).reshape(out_ref.shape)


def coupled_blocks(rows, kept, pieces):
    orb_rows, virt, _ = pieces[0].shape
    count = rows * orb_rows
    shape = jax.ShapeDtypeStruct((orb_rows, virt, virt), jnp.bfloat16)
    body = functools.partial(coupled_body, rows)
    flops, moved = 2 * orb_rows * count * virt**3, 2 * (orb_rows + 1) * count * virt**2
    return call(body, shape, [VMEM] * (1 + len(pieces)), flops, moved, kept, *pieces)


def column_body(meta, crossing_ref, *refs):
    out_ref, same_ref, other_ref = refs[-3:]
    orb_rows = crossing_ref.shape[0]
    my_col = meta[2 * orb_rows, 1]
    for step in range(out_ref.shape[0] // orb_rows):
        out_ref[pl.ds((my_col // 2 ^ step) * orb_rows, orb_rows)] = refs[step][...]
    same_ref[...] = crossing_ref[my_col % 2]
    other_ref[...] = crossing_ref[1 - my_col % 2]


def whole_column(meta, pieces, crossing, others):
    orb_rows, virt, _ = crossing.shape
    block = jax.ShapeDtypeStruct((virt, virt), jnp.bfloat16)
    shape = (jax.ShapeDtypeStruct((orb_rows * len(pieces), virt, virt), jnp.bfloat16), block, block)
    operands = [crossing, *pieces, *others]
    moved = 4 * orb_rows * (len(pieces) + 1) * virt**2
    return call(column_body, shape, [SMEM] + [VMEM] * len(operands), 0, moved, meta, *operands)


def tied_body(*refs):
    pass


def tied(x, *others):
    return pl.pallas_call(
        tied_body,
        out_shape=jax.ShapeDtypeStruct(x.shape, x.dtype),
        in_specs=[VMEM] * (1 + len(others)),
        out_specs=VMEM,
        input_output_aliases={0: 0},
        compiler_params=pltpu.CompilerParams(vmem_limit_bytes=VMEM_BYTES),
    )(x, *others)


def masked_pair(meta, orbital, blocks):
    orb_rows = len(blocks)
    kept = [jnp.where(meta[orb_rows + i, orbital] > 0, block, jnp.zeros_like(block)) for i, block in enumerate(blocks)]
    return jnp.concatenate(kept, axis=0)


def turned(block):
    return jnp.transpose(block.astype(jnp.float32), (1, 0))


def first_body(rows, meta, own_ref, other_ref, *refs):
    state_ref, coulomb_ref, inverse_ref, out_ref = refs[-4:]
    orb_rows = out_ref.shape[0]
    blocks = piece_blocks(refs[:-4], rows)
    my_row, side = meta[2 * orb_rows, 0], meta[2 * orb_rows, 1] % 2
    total = None
    for step in range(rows):
        at = my_row ^ step
        for t in range(orb_rows):
            left = [
                jnp.where(side == t, own_ref[at * orb_rows + i], other_ref[at * orb_rows + i]) for i in range(orb_rows)
            ]
            ref, place = blocks[step][t]
            left = masked_pair(meta, at * orb_rows + t, left)
            part = jnp.dot(left, ref[place], preferred_element_type=jnp.float32)
            total = part if total is None else total + part
    linear = coulomb_ref[...].astype(jnp.float32) + coupling * refs[0][...].astype(jnp.float32)
    residual = linear + coupling * coupling * total.reshape(out_ref.shape)
    out_ref[...] = damping * state_ref[...] - residual * inverse_ref[...]


def second_body(meta, same_ref, other_ref, part_ref, inverse_ref, out_ref, half_ref):
    side = meta[2 * out_ref.shape[0], 1] % 2
    for ref, at in ((same_ref, side), (other_ref, 1 - side)):
        state = part_ref[at] - coupling * turned(ref[...]) * inverse_ref[at]
        out_ref[at] = state
        half_ref[at] = state.astype(half_ref.dtype)


def first_update(rows, meta, own, other, c_pieces, state, coulomb_own, inverse):
    orb_rows, virt, _ = state.shape
    shape = jax.ShapeDtypeStruct(state.shape, jnp.float32)
    flops, moved = 2 * orb_rows**2 * rows * virt**3, 4 * (orb_rows + 1) * orb_rows * rows * virt**2
    return call(
        functools.partial(first_body, rows), shape, [SMEM] + [VMEM] * (len(c_pieces) + 5), flops, moved,
        meta, own, other, *c_pieces, state, coulomb_own, inverse,
    )


def second_update(meta, same, other, part, inverse):
    shape = (jax.ShapeDtypeStruct(part.shape, jnp.float32), jax.ShapeDtypeStruct(part.shape, jnp.bfloat16))
    return call(second_body, shape, [SMEM] + [VMEM] * 4, 0, 16 * part.size, meta, same, other, part, inverse)


def on_device(
    rows,
    cols,
    amplitudes,
    coulomb,
    inner_list,
    inner_count,
    reader_list,
    reader_count,
    virtual_energy,
    occupied_energy,
):
    orb_rows, orb_cols, virt, _ = amplitudes.shape
    count = coulomb.shape[1]
    slots = inner_list.shape[2]
    assert orb_cols == 1 and count == cols == rows * orb_rows and orb_rows == 2
    halves = cols // 2
    my_row = lax.axis_index("row")
    my_col = lax.axis_index("col")

    def from_row(x, step):
        return lax.ppermute(x, "row", [(r ^ step, r) for r in range(rows)])

    def row_gathered(x):
        return [x] + [from_row(x, step) for step in range(1, rows)]

    def swapped(x):
        return lax.ppermute(x, "col", [(c ^ 1, c) for c in range(cols)])

    def from_chip(x, step):
        return lax.ppermute(x, "col", [(c ^ 2 * step, c) for c in range(cols)])

    def crossing(x, place, flip=0):
        pairs = []
        for r in range(rows):
            for c in range(cols):
                to_r, to_z = place(r, c // 2)
                pairs.append((r * cols + c, to_r * cols + 2 * to_z + (c % 2 ^ flip)))
        return lax.ppermute(x, ("row", "col"), pairs)

    def high_parts(r, z):
        return z - z % 2 + r % 2, r - r % 2 + z % 2

    def last_bits(r, z):
        return r - r % 2 + z % 2, z - z % 2 + r % 2

    state = amplitudes[:, 0]
    half = state.astype(jnp.bfloat16)

    slot_iota = jnp.arange(slots, dtype=jnp.int32)
    orbital_iota = jnp.arange(count, dtype=jnp.int32)

    def used(lists, counts):
        live = slot_iota[None] < counts[:, None]
        hit = (lists[:, :, None] == orbital_iota) & live[:, :, None]
        return jnp.any(hit, axis=1).astype(jnp.int32)

    inner_used = used(inner_list[:, 0], inner_count[:, 0])
    reader_used = used(
        lax.dynamic_index_in_dim(reader_list, my_col, 1, False), lax.dynamic_index_in_dim(reader_count, my_col, 1, False)
    )
    place = jnp.where(orbital_iota == 0, my_row, my_col).astype(jnp.int32)
    meta = jnp.concatenate([inner_used, reader_used, place[None]], axis=0)

    kept, coulomb_own, inverse = prologue(rows, meta, coulomb, virtual_energy, occupied_energy)

    for sweep_index in range(ITERS):
        a_pieces = row_gathered(half)
        column = {0: half, 1: from_chip(half, 1)}
        for step in range(2, halves, 2):
            column[step] = from_chip(half, step)
        coupled = coupled_blocks(rows, kept, a_pieces)
        c_pieces = row_gathered(coupled)
        half_way = crossing(coupled, high_parts)
        for step in range(2, halves, 2):
            column[step] = tied(column[step], coupled)
            column[step + 1] = from_chip(column[step], 1)
        column = [column[step] for step in range(halves)]
        own, same, other = whole_column(meta, column, half_way, c_pieces[1:])
        same, other = crossing(same, last_bits), crossing(other, last_bits, 1)
        part = first_update(rows, meta, own, swapped(own), c_pieces, state, coulomb_own, inverse)
        state, half = second_update(meta, same, other, part, inverse)
    return state[:, None]


def solution(mesh):
    return jax.shard_map(
        functools.partial(on_device, mesh.shape["row"], mesh.shape["col"]),
        mesh=mesh,
        in_specs=(
            P("row", "col", None, None),
            P("row", None, None, None),
            P("row", "col", None),
            P("row", "col"),
            P("row", None, None),
            P("row", None),
            P(),
            P(),
        ),
        out_specs=P("row", "col", None, None),
        check_vma=False,
    )
```

```python
import functools

import jax
import jax.numpy as jnp
from jax import lax
from jax.experimental import pallas as pl
from jax.experimental.pallas import tpu as pltpu
from jax.sharding import PartitionSpec as P

ITERS = 2


damping = 0.5
coupling = 0.03125
ANY = pl.BlockSpec(memory_space=pl.ANY)
SMEM = pl.BlockSpec(memory_space=pltpu.SMEM)
VMEM = pl.BlockSpec(memory_space=pltpu.VMEM)
VMEM_BYTES = 32 * 1024 * 1024


def call(body, out_shape, in_specs, flops, moved, *operands):
    single = isinstance(out_shape, jax.ShapeDtypeStruct)
    return pl.pallas_call(
        body,
        out_shape=out_shape,
        in_specs=in_specs,
        out_specs=VMEM if single else (VMEM,) * len(out_shape),
        compiler_params=pltpu.CompilerParams(vmem_limit_bytes=VMEM_BYTES),
        cost_estimate=pl.CostEstimate(flops=flops, bytes_accessed=moved, transcendentals=0),
    )(*operands)


def prologue_body(meta, occupied, k_ref, virt_row, virt_col, kept_ref, own_ref, inverse_ref):
    orb_rows, _, virt, _ = k_ref.shape
    my_row = meta[2 * orb_rows, 0]
    my_col = meta[2 * orb_rows, 1]
    for step in range(kept_ref.shape[0]):
        for t in range(orb_rows):
            orbital = (my_row ^ step) * orb_rows + t
            for i in range(orb_rows):
                block = k_ref[i, orbital]
                keep = jnp.where(meta[i, orbital] > 0, block, jnp.zeros_like(block))
                kept_ref[step, i * virt : (i + 1) * virt, t * virt : (t + 1) * virt] = keep
    virt_pair = virt_col[...] + virt_row[...]
    for i in range(orb_rows):
        own_ref[i] = k_ref[i, my_col]
        inverse_ref[i] = 1.0 / (virt_pair - occupied[0, my_row * orb_rows + i] - occupied[0, my_col])


def prologue(rows, meta, coulomb, virtual_energy, occupied_energy):
    orb_rows, count, virt, _ = coulomb.shape
    shape = (
        jax.ShapeDtypeStruct((rows, orb_rows * virt, orb_rows * virt), jnp.bfloat16),
        jax.ShapeDtypeStruct((orb_rows, virt, virt), jnp.bfloat16),
        jax.ShapeDtypeStruct((orb_rows, virt, virt), jnp.float32),
    )
    return call(
        prologue_body, shape, [SMEM, SMEM, VMEM, VMEM, VMEM], 0, 4 * orb_rows * count * virt**2,
        meta, occupied_energy[None], coulomb, virtual_energy[None], virtual_energy[:, None],
    )


def coupled_body(rows, meta, k_ref, *refs):
    out_ref, same_ref, other_ref = refs[-3:]
    orb_rows, virt, _ = out_ref.shape
    side = meta[2 * orb_rows, 1] % 2
    total = None
    for step in range(rows):
        for t in range(orb_rows):
            left = k_ref[step, :, t * virt : (t + 1) * virt]
            part = jnp.dot(left, refs[step][t], preferred_element_type=jnp.float32)
            total = part if total is None else total + part
    out_ref[...] = total.astype(out_ref.dtype).reshape(out_ref.shape)
    same_ref[...] = out_ref[side]
    other_ref[...] = out_ref[1 - side]


def coupled_blocks(rows, meta, kept, pieces):
    orb_rows, virt, _ = pieces[0].shape
    count = rows * orb_rows
    block = jax.ShapeDtypeStruct((virt, virt), jnp.bfloat16)
    shape = (jax.ShapeDtypeStruct((orb_rows, virt, virt), jnp.bfloat16), block, block)
    body = functools.partial(coupled_body, rows)
    flops, moved = 2 * orb_rows * count * virt**3, 2 * (orb_rows + 1) * count * virt**2
    return call(body, shape, [SMEM] + [VMEM] * (1 + len(pieces)), flops, moved, meta, kept, *pieces)


def column_body(meta, *refs):
    out_ref = refs[-1]
    orb_rows = refs[0].shape[0]
    my_place = meta[2 * orb_rows, 1] // 2
    for step in range(out_ref.shape[0] // orb_rows):
        out_ref[pl.ds((my_place ^ step) * orb_rows, orb_rows)] = refs[step][...]


def whole_column(meta, pieces, others):
    orb_rows, virt, _ = pieces[0].shape
    shape = jax.ShapeDtypeStruct((orb_rows * len(pieces), virt, virt), jnp.bfloat16)
    operands = [*pieces, *others]
    moved = 4 * orb_rows * len(pieces) * virt**2
    return call(column_body, shape, [SMEM] + [VMEM] * len(operands), 0, moved, meta, *operands)


def tied_body(*refs):
    pass


def tied(x, *others):
    return pl.pallas_call(
        tied_body,
        out_shape=jax.ShapeDtypeStruct(x.shape, x.dtype),
        in_specs=[VMEM] * (1 + len(others)),
        out_specs=VMEM,
        input_output_aliases={0: 0},
        compiler_params=pltpu.CompilerParams(vmem_limit_bytes=VMEM_BYTES),
    )(x, *others)


def masked_pair(meta, orbital, blocks):
    orb_rows = len(blocks)
    kept = [jnp.where(meta[orb_rows + i, orbital] > 0, block, jnp.zeros_like(block)) for i, block in enumerate(blocks)]
    return jnp.concatenate(kept, axis=0)


def turned(block):
    return jnp.transpose(block.astype(jnp.float32), (1, 0))


def first_body(rows, meta, own_ref, other_ref, *refs):
    state_ref, coulomb_ref, inverse_ref, out_ref = refs[-4:]
    orb_rows = out_ref.shape[0]
    my_row, side = meta[2 * orb_rows, 0], meta[2 * orb_rows, 1] % 2
    total = None
    for step in range(rows):
        at = my_row ^ step
        for t in range(orb_rows):
            left = [
                jnp.where(side == t, own_ref[at * orb_rows + i], other_ref[at * orb_rows + i]) for i in range(orb_rows)
            ]
            left = masked_pair(meta, at * orb_rows + t, left)
            part = jnp.dot(left, refs[step][t], preferred_element_type=jnp.float32)
            total = part if total is None else total + part
    linear = coulomb_ref[...].astype(jnp.float32) + coupling * refs[0][...].astype(jnp.float32)
    residual = linear + coupling * coupling * total.reshape(out_ref.shape)
    out_ref[...] = damping * state_ref[...] - residual * inverse_ref[...]


def second_body(meta, same_ref, other_ref, part_ref, inverse_ref, out_ref, half_ref):
    side = meta[2 * out_ref.shape[0], 1] % 2
    for ref, at in ((same_ref, side), (other_ref, 1 - side)):
        state = part_ref[at] - coupling * turned(ref[...]) * inverse_ref[at]
        out_ref[at] = state
        half_ref[at] = state.astype(half_ref.dtype)


def first_update(rows, meta, own, other, c_pieces, state, coulomb_own, inverse):
    orb_rows, virt, _ = state.shape
    shape = jax.ShapeDtypeStruct(state.shape, jnp.float32)
    flops, moved = 2 * orb_rows**2 * rows * virt**3, 4 * (orb_rows + 1) * orb_rows * rows * virt**2
    return call(
        functools.partial(first_body, rows), shape, [SMEM] + [VMEM] * (len(c_pieces) + 5), flops, moved,
        meta, own, other, *c_pieces, state, coulomb_own, inverse,
    )


def second_update(meta, same, other, part, inverse):
    shape = (jax.ShapeDtypeStruct(part.shape, jnp.float32), jax.ShapeDtypeStruct(part.shape, jnp.bfloat16))
    return call(second_body, shape, [SMEM] + [VMEM] * 4, 0, 16 * part.size, meta, same, other, part, inverse)


def on_device(
    rows,
    cols,
    amplitudes,
    coulomb,
    inner_list,
    inner_count,
    reader_list,
    reader_count,
    virtual_energy,
    occupied_energy,
):
    orb_rows, orb_cols, virt, _ = amplitudes.shape
    count = coulomb.shape[1]
    slots = inner_list.shape[2]
    assert orb_cols == 1 and count == cols == rows * orb_rows and orb_rows == 2
    halves = cols // 2
    my_row = lax.axis_index("row")
    my_col = lax.axis_index("col")

    def from_row(x, step):
        return lax.ppermute(x, "row", [(r ^ step, r) for r in range(rows)])

    def row_gathered(x):
        return [x] + [from_row(x, step) for step in range(1, rows)]

    def swapped(x):
        return lax.ppermute(x, "col", [(c ^ 1, c) for c in range(cols)])

    def from_chip(x, step):
        return lax.ppermute(x, "col", [(c ^ 2 * step, c) for c in range(cols)])

    def crossing(x, place, flip=0):
        pairs = []
        for r in range(rows):
            for c in range(cols):
                to_r, to_z = place(r, c // 2)
                pairs.append((r * cols + c, to_r * cols + 2 * to_z + (c % 2 ^ flip)))
        return lax.ppermute(x, ("row", "col"), pairs)

    def high_parts(r, z):
        return z - z % 2 + r % 2, r - r % 2 + z % 2

    def last_bits(r, z):
        return r - r % 2 + z % 2, z - z % 2 + r % 2

    state = amplitudes[:, 0]
    half = state.astype(jnp.bfloat16)

    slot_iota = jnp.arange(slots, dtype=jnp.int32)
    orbital_iota = jnp.arange(count, dtype=jnp.int32)

    def used(lists, counts):
        live = slot_iota[None] < counts[:, None]
        hit = (lists[:, :, None] == orbital_iota) & live[:, :, None]
        return jnp.any(hit, axis=1).astype(jnp.int32)

    inner_used = used(inner_list[:, 0], inner_count[:, 0])
    reader_used = used(
        lax.dynamic_index_in_dim(reader_list, my_col, 1, False), lax.dynamic_index_in_dim(reader_count, my_col, 1, False)
    )
    place = jnp.where(orbital_iota == 0, my_row, my_col).astype(jnp.int32)
    meta = jnp.concatenate([inner_used, reader_used, place[None]], axis=0)

    kept, coulomb_own, inverse = prologue(rows, meta, coulomb, virtual_energy, occupied_energy)

    for sweep_index in range(ITERS):
        a_pieces = row_gathered(half)
        column = {0: half, 1: from_chip(half, 1)}
        for step in range(2, halves, 2):
            column[step] = from_chip(half, step)
        coupled, same, other = coupled_blocks(rows, meta, kept, a_pieces)
        c_pieces = {0: coupled, 1: from_row(coupled, 1)}
        for step in range(2, rows, 2):
            c_pieces[step] = from_row(coupled, step)
            c_pieces[step + 1] = from_row(c_pieces[step], 1)
        c_pieces = [c_pieces[step] for step in range(rows)]
        same, other = crossing(same, high_parts), crossing(other, last_bits)
        for step in range(2, halves, 2):
            column[step] = tied(column[step], coupled)
            column[step + 1] = from_chip(column[step], 1)
        column = [column[step] for step in range(halves)]
        own = whole_column(meta, column, [c_pieces[1], c_pieces[2], same, other])
        same, other = crossing(same, last_bits), crossing(other, high_parts, 1)
        part = first_update(rows, meta, own, swapped(own), c_pieces, state, coulomb_own, inverse)
        state, half = second_update(meta, same, other, part, inverse)
    return state[:, None]


def solution(mesh):
    return jax.shard_map(
        functools.partial(on_device, mesh.shape["row"], mesh.shape["col"]),
        mesh=mesh,
        in_specs=(
            P("row", "col", None, None),
            P("row", None, None, None),
            P("row", "col", None),
            P("row", "col"),
            P("row", None, None),
            P("row", None),
            P(),
            P(),
        ),
        out_specs=P("row", "col", None, None),
        check_vma=False,
    )
```

```python
import functools

import jax
import jax.numpy as jnp
from jax import lax
from jax.experimental import pallas as pl
from jax.experimental.pallas import tpu as pltpu
from jax.sharding import PartitionSpec as P

ITERS = 2


damping = 0.5
coupling = 0.03125
ANY = pl.BlockSpec(memory_space=pl.ANY)
SMEM = pl.BlockSpec(memory_space=pltpu.SMEM)
VMEM = pl.BlockSpec(memory_space=pltpu.VMEM)
VMEM_BYTES = 32 * 1024 * 1024


def call(body, out_shape, in_specs, flops, moved, *operands):
    single = isinstance(out_shape, jax.ShapeDtypeStruct)
    return pl.pallas_call(
        body,
        out_shape=out_shape,
        in_specs=in_specs,
        out_specs=VMEM if single else (VMEM,) * len(out_shape),
        compiler_params=pltpu.CompilerParams(vmem_limit_bytes=VMEM_BYTES),
        cost_estimate=pl.CostEstimate(flops=flops, bytes_accessed=moved, transcendentals=0),
    )(*operands)


def prologue_body(meta, occupied, k_ref, virt_row, virt_col, kept_ref, own_ref, inverse_ref):
    orb_rows, _, virt, _ = k_ref.shape
    my_row = meta[2 * orb_rows, 0]
    my_col = meta[2 * orb_rows, 1]
    for step in range(kept_ref.shape[0]):
        for t in range(orb_rows):
            orbital = (my_row ^ step) * orb_rows + t
            for i in range(orb_rows):
                block = k_ref[i, orbital]
                keep = jnp.where(meta[i, orbital] > 0, block, jnp.zeros_like(block))
                kept_ref[step, i * virt : (i + 1) * virt, t * virt : (t + 1) * virt] = keep
    virt_pair = virt_col[...] + virt_row[...]
    for i in range(orb_rows):
        own_ref[i] = k_ref[i, my_col]
        inverse_ref[i] = 1.0 / (virt_pair - occupied[0, my_row * orb_rows + i] - occupied[0, my_col])


def prologue(rows, meta, coulomb, virtual_energy, occupied_energy):
    orb_rows, count, virt, _ = coulomb.shape
    shape = (
        jax.ShapeDtypeStruct((rows, orb_rows * virt, orb_rows * virt), jnp.bfloat16),
        jax.ShapeDtypeStruct((orb_rows, virt, virt), jnp.bfloat16),
        jax.ShapeDtypeStruct((orb_rows, virt, virt), jnp.float32),
    )
    return call(
        prologue_body, shape, [SMEM, SMEM, VMEM, VMEM, VMEM], 0, 4 * orb_rows * count * virt**2,
        meta, occupied_energy[None], coulomb, virtual_energy[None], virtual_energy[:, None],
    )


def piece_blocks(refs, rows):
    found, refs, size = [], list(refs), refs[0].shape[0]
    for step in range(rows):
        blocks = []
        while len(blocks) < size:
            ref = refs.pop(0)
            blocks += [(ref, at) for at in range(ref.shape[0])]
        found.append(blocks)
    return found


def coupled_body(rows, meta, k_ref, *refs):
    out_ref, same_ref, other_ref = refs[-3:]
    orb_rows, virt, _ = out_ref.shape
    side = meta[2 * orb_rows, 1] % 2
    total = None
    for step in range(rows):
        for t in range(orb_rows):
            left = k_ref[step, :, t * virt : (t + 1) * virt]
            part = jnp.dot(left, refs[step][t], preferred_element_type=jnp.float32)
            total = part if total is None else total + part
    first, second = total[:virt].astype(out_ref.dtype), total[virt:].astype(out_ref.dtype)
    out_ref[0], out_ref[1] = first, second
    same_ref[...] = jnp.where(side == 0, first, second)
    other_ref[...] = jnp.where(side == 0, second, first)


def coupled_blocks(rows, meta, kept, pieces, other):
    orb_rows, virt, _ = pieces[0].shape
    count = rows * orb_rows
    block = jax.ShapeDtypeStruct((virt, virt), jnp.bfloat16)
    shape = (jax.ShapeDtypeStruct((orb_rows, virt, virt), jnp.bfloat16), block, block)
    body = functools.partial(coupled_body, rows)
    flops, moved = 2 * orb_rows * count * virt**3, 2 * (orb_rows + 1) * count * virt**2
    return call(body, shape, [SMEM] + [VMEM] * (2 + len(pieces)), flops, moved, meta, kept, *pieces, other)


def column_body(meta, *refs):
    out_ref = refs[-1]
    orb_rows = refs[0].shape[0]
    my_place = meta[2 * orb_rows, 1] // 2
    for step in range(out_ref.shape[0] // orb_rows):
        out_ref[pl.ds((my_place ^ step) * orb_rows, orb_rows)] = refs[step][...]


def whole_column(meta, pieces, others):
    orb_rows, virt, _ = pieces[0].shape
    shape = jax.ShapeDtypeStruct((orb_rows * len(pieces), virt, virt), jnp.bfloat16)
    operands = [*pieces, *others]
    moved = 4 * orb_rows * len(pieces) * virt**2
    return call(column_body, shape, [SMEM] + [VMEM] * len(operands), 0, moved, meta, *operands)


def tied_body(*refs):
    pass


def tied(x, *others):
    return pl.pallas_call(
        tied_body,
        out_shape=jax.ShapeDtypeStruct(x.shape, x.dtype),
        in_specs=[VMEM] * (1 + len(others)),
        out_specs=VMEM,
        input_output_aliases={0: 0},
        compiler_params=pltpu.CompilerParams(vmem_limit_bytes=VMEM_BYTES),
    )(x, *others)


def masked_pair(meta, orbital, blocks):
    orb_rows = len(blocks)
    kept = [jnp.where(meta[orb_rows + i, orbital] > 0, block, jnp.zeros_like(block)) for i, block in enumerate(blocks)]
    return jnp.concatenate(kept, axis=0)


def turned(block):
    return jnp.transpose(block.astype(jnp.float32), (1, 0))


def first_body(rows, meta, own_ref, other_ref, *refs):
    state_ref, coulomb_ref, inverse_ref, out_ref = refs[-4:]
    orb_rows = out_ref.shape[0]
    blocks = piece_blocks(refs[:-4], rows)
    my_row, side = meta[2 * orb_rows, 0], meta[2 * orb_rows, 1] % 2
    total = None
    for step in range(rows):
        at = my_row ^ step
        for t in range(orb_rows):
            left = [
                jnp.where(side == t, own_ref[at * orb_rows + i], other_ref[at * orb_rows + i]) for i in range(orb_rows)
            ]
            left = masked_pair(meta, at * orb_rows + t, left)
            ref, place = blocks[step][t]
            part = jnp.dot(left, ref[place], preferred_element_type=jnp.float32)
            total = part if total is None else total + part
    linear = coulomb_ref[...].astype(jnp.float32) + coupling * refs[0][...].astype(jnp.float32)
    residual = linear + coupling * coupling * total.reshape(out_ref.shape)
    out_ref[...] = damping * state_ref[...] - residual * inverse_ref[...]


def second_body(meta, same_ref, other_ref, part_ref, inverse_ref, out_ref, *half_refs):
    side = meta[2 * out_ref.shape[0], 1] % 2
    for ref, at in ((same_ref, side), (other_ref, 1 - side)):
        state = part_ref[at] - coupling * turned(ref[...]) * inverse_ref[at]
        out_ref[at] = state
        for half_ref in half_refs:
            half_ref[at] = state.astype(half_ref.dtype)


def first_update(rows, meta, own, other, c_pieces, state, coulomb_own, inverse):
    orb_rows, virt, _ = state.shape
    shape = jax.ShapeDtypeStruct(state.shape, jnp.float32)
    flops, moved = 2 * orb_rows**2 * rows * virt**3, 4 * (orb_rows + 1) * orb_rows * rows * virt**2
    return call(
        functools.partial(first_body, rows), shape, [SMEM] + [VMEM] * (len(c_pieces) + 5), flops, moved,
        meta, own, other, *c_pieces, state, coulomb_own, inverse,
    )


def second_update(meta, same, other, part, inverse, with_half):
    shape = (jax.ShapeDtypeStruct(part.shape, jnp.float32), jax.ShapeDtypeStruct(part.shape, jnp.bfloat16))
    shape = shape if with_half else shape[:1]
    return call(second_body, shape, [SMEM] + [VMEM] * 4, 0, 16 * part.size, meta, same, other, part, inverse)


def on_device(
    rows,
    cols,
    amplitudes,
    coulomb,
    inner_list,
    inner_count,
    reader_list,
    reader_count,
    virtual_energy,
    occupied_energy,
):
    orb_rows, orb_cols, virt, _ = amplitudes.shape
    count = coulomb.shape[1]
    slots = inner_list.shape[2]
    assert orb_cols == 1 and count == cols == rows * orb_rows and orb_rows == 2
    halves = cols // 2
    my_row = lax.axis_index("row")
    my_col = lax.axis_index("col")

    def from_row(x, step):
        return lax.ppermute(x, "row", [(r ^ step, r) for r in range(rows)])

    def row_gathered(x):
        return [x] + [from_row(x, step) for step in range(1, rows)]

    def swapped(x):
        return lax.ppermute(x, "col", [(c ^ 1, c) for c in range(cols)])

    def from_chip(x, step):
        return lax.ppermute(x, "col", [(c ^ 2 * step, c) for c in range(cols)])

    def crossing(x, place, flip=0):
        pairs = []
        for r in range(rows):
            for c in range(cols):
                to_r, to_z = place(r, c // 2)
                pairs.append((r * cols + c, to_r * cols + 2 * to_z + (c % 2 ^ flip)))
        return lax.ppermute(x, ("row", "col"), pairs)

    def high_parts(r, z):
        return z - z % 2 + r % 2, r - r % 2 + z % 2

    def last_bits(r, z):
        return r - r % 2 + z % 2, z - z % 2 + r % 2

    state = amplitudes[:, 0]
    half = state.astype(jnp.bfloat16)

    slot_iota = jnp.arange(slots, dtype=jnp.int32)
    orbital_iota = jnp.arange(count, dtype=jnp.int32)

    def used(lists, counts):
        live = slot_iota[None] < counts[:, None]
        hit = (lists[:, :, None] == orbital_iota) & live[:, :, None]
        return jnp.any(hit, axis=1).astype(jnp.int32)

    inner_used = used(inner_list[:, 0], inner_count[:, 0])
    reader_used = used(
        lax.dynamic_index_in_dim(reader_list, my_col, 1, False), lax.dynamic_index_in_dim(reader_count, my_col, 1, False)
    )
    place = jnp.where(orbital_iota == 0, my_row, my_col).astype(jnp.int32)
    meta = jnp.concatenate([inner_used, reader_used, place[None]], axis=0)

    kept, coulomb_own, inverse = prologue(rows, meta, coulomb, virtual_energy, occupied_energy)

    for sweep_index in range(ITERS):
        a_pieces = row_gathered(half)
        column = {0: half, 1: from_chip(half, 1)}
        for step in range(2, halves, 2):
            column[step] = from_chip(half, step)
        coupled, same, other = coupled_blocks(rows, meta, kept, a_pieces, column[1])
        near = from_row(coupled, 1)
        c_pieces, far = [coupled, near], []
        for step in range(2, rows, 2):
            piece = from_row(coupled, step)
            far += [from_row(piece[0:1], 1), from_row(near[1:2], step)]
            c_pieces += [piece, *far[-2:]]
        same, other = crossing(same, high_parts), crossing(other, last_bits)
        for step in range(2, halves, 2):
            column[step] = tied(column[step], coupled)
            column[step + 1] = from_chip(column[step], 1)
        column = [column[step] for step in range(halves)]
        own = whole_column(meta, column, [*far, same, other])
        same, other = crossing(same, last_bits), crossing(other, high_parts, 1)
        part = first_update(rows, meta, own, swapped(own), c_pieces, state, coulomb_own, inverse)
        state, *halves_out = second_update(meta, same, other, part, inverse, sweep_index < ITERS - 1)
        half = halves_out[0] if halves_out else None
    return state[:, None]


def solution(mesh):
    return jax.shard_map(
        functools.partial(on_device, mesh.shape["row"], mesh.shape["col"]),
        mesh=mesh,
        in_specs=(
            P("row", "col", None, None),
            P("row", None, None, None),
            P("row", "col", None),
            P("row", "col"),
            P("row", None, None),
            P("row", None),
            P(),
            P(),
        ),
        out_specs=P("row", "col", None, None),
        check_vma=False,
    )
```

```python
import functools

import jax
import jax.numpy as jnp
from jax import lax
from jax.experimental import pallas as pl
from jax.experimental.pallas import tpu as pltpu
from jax.sharding import PartitionSpec as P

ITERS = 2


damping = 0.5
coupling = 0.03125
ANY = pl.BlockSpec(memory_space=pl.ANY)
SMEM = pl.BlockSpec(memory_space=pltpu.SMEM)
VMEM = pl.BlockSpec(memory_space=pltpu.VMEM)
VMEM_BYTES = 32 * 1024 * 1024


def call(body, out_shape, in_specs, flops, moved, *operands):
    single = isinstance(out_shape, jax.ShapeDtypeStruct)
    return pl.pallas_call(
        body,
        out_shape=out_shape,
        in_specs=in_specs,
        out_specs=VMEM if single else (VMEM,) * len(out_shape),
        compiler_params=pltpu.CompilerParams(vmem_limit_bytes=VMEM_BYTES),
        cost_estimate=pl.CostEstimate(flops=flops, bytes_accessed=moved, transcendentals=0),
    )(*operands)


def prologue_body(meta, occupied, k_ref, virt_row, virt_col, kept_ref, own_ref, inverse_ref):
    orb_rows, _, virt, _ = k_ref.shape
    my_row = meta[2 * orb_rows, 0]
    my_col = meta[2 * orb_rows, 1]
    for step in range(kept_ref.shape[0]):
        for t in range(orb_rows):
            orbital = (my_row ^ step) * orb_rows + t
            for i in range(orb_rows):
                block = k_ref[i, orbital]
                keep = jnp.where(meta[i, orbital] > 0, block, jnp.zeros_like(block))
                kept_ref[step, i * virt : (i + 1) * virt, t * virt : (t + 1) * virt] = keep
    virt_pair = virt_col[...] + virt_row[...]
    for i in range(orb_rows):
        own_ref[i] = k_ref[i, my_col]
        inverse_ref[i] = 1.0 / (virt_pair - occupied[0, my_row * orb_rows + i] - occupied[0, my_col])


def prologue(rows, meta, coulomb, virtual_energy, occupied_energy):
    orb_rows, count, virt, _ = coulomb.shape
    shape = (
        jax.ShapeDtypeStruct((rows, orb_rows * virt, orb_rows * virt), jnp.bfloat16),
        jax.ShapeDtypeStruct((orb_rows, virt, virt), jnp.bfloat16),
        jax.ShapeDtypeStruct((orb_rows, virt, virt), jnp.float32),
    )
    return call(
        prologue_body, shape, [SMEM, SMEM, VMEM, VMEM, VMEM], 0, 4 * orb_rows * count * virt**2,
        meta, occupied_energy[None], coulomb, virtual_energy[None], virtual_energy[:, None],
    )


def piece_blocks(refs, rows):
    found, refs, size = [], list(refs), refs[0].shape[0]
    for step in range(rows):
        blocks = []
        while len(blocks) < size:
            ref = refs.pop(0)
            blocks += [(ref, at) for at in range(ref.shape[0])]
        found.append(blocks)
    return found


def coupled_body(rows, meta, k_ref, *refs):
    out_ref, same_ref, other_ref = refs[-3:]
    orb_rows, virt, _ = out_ref.shape
    side = meta[2 * orb_rows, 1] % 2
    total = None
    for step in range(rows):
        for t in range(orb_rows):
            left = k_ref[step, :, t * virt : (t + 1) * virt]
            part = jnp.dot(left, refs[step][t], preferred_element_type=jnp.float32)
            total = part if total is None else total + part
    first, second = total[:virt].astype(out_ref.dtype), total[virt:].astype(out_ref.dtype)
    out_ref[0], out_ref[1] = first, second
    same_ref[...] = jnp.where(side == 0, first, second)
    other_ref[...] = jnp.where(side == 0, second, first)


def coupled_blocks(rows, meta, kept, pieces):
    orb_rows, virt, _ = pieces[0].shape
    count = rows * orb_rows
    block = jax.ShapeDtypeStruct((virt, virt), jnp.bfloat16)
    shape = (jax.ShapeDtypeStruct((orb_rows, virt, virt), jnp.bfloat16), block, block)
    body = functools.partial(coupled_body, rows)
    flops, moved = 2 * orb_rows * count * virt**3, 2 * (orb_rows + 1) * count * virt**2
    return call(body, shape, [SMEM] + [VMEM] * (1 + len(pieces)), flops, moved, meta, kept, *pieces)


def column_body(meta, *refs):
    out_ref = refs[-1]
    orb_rows = refs[0].shape[0]
    my_place = meta[2 * orb_rows, 1] // 2
    for step in range(out_ref.shape[0] // orb_rows):
        out_ref[pl.ds((my_place ^ step) * orb_rows, orb_rows)] = refs[step][...]


def whole_column(meta, pieces, others):
    orb_rows, virt, _ = pieces[0].shape
    shape = jax.ShapeDtypeStruct((orb_rows * len(pieces), virt, virt), jnp.bfloat16)
    operands = [*pieces, *others]
    moved = 4 * orb_rows * len(pieces) * virt**2
    return call(column_body, shape, [SMEM] + [VMEM] * len(operands), 0, moved, meta, *operands)


def tied_body(*refs):
    pass


def tied(x, *others):
    return pl.pallas_call(
        tied_body,
        out_shape=jax.ShapeDtypeStruct(x.shape, x.dtype),
        in_specs=[VMEM] * (1 + len(others)),
        out_specs=VMEM,
        input_output_aliases={0: 0},
        compiler_params=pltpu.CompilerParams(vmem_limit_bytes=VMEM_BYTES),
    )(x, *others)


def masked_pair(meta, orbital, blocks):
    orb_rows = len(blocks)
    kept = [jnp.where(meta[orb_rows + i, orbital] > 0, block, jnp.zeros_like(block)) for i, block in enumerate(blocks)]
    return jnp.concatenate(kept, axis=0)


def turned(block):
    return jnp.transpose(block.astype(jnp.float32), (1, 0))


def first_body(rows, meta, own_ref, other_ref, *refs):
    state_ref, coulomb_ref, inverse_ref, out_ref = refs[-4:]
    orb_rows = out_ref.shape[0]
    blocks = piece_blocks(refs[:-4], rows)
    my_row, side = meta[2 * orb_rows, 0], meta[2 * orb_rows, 1] % 2
    total = None
    for step in range(rows):
        at = my_row ^ step
        for t in range(orb_rows):
            left = [
                jnp.where(side == t, own_ref[at * orb_rows + i], other_ref[at * orb_rows + i]) for i in range(orb_rows)
            ]
            left = masked_pair(meta, at * orb_rows + t, left)
            ref, place = blocks[step][t]
            part = jnp.dot(left, ref[place], preferred_element_type=jnp.float32)
            total = part if total is None else total + part
    linear = coulomb_ref[...].astype(jnp.float32) + coupling * refs[0][...].astype(jnp.float32)
    residual = linear + coupling * coupling * total.reshape(out_ref.shape)
    out_ref[...] = damping * state_ref[...] - residual * inverse_ref[...]


def second_body(meta, same_ref, other_ref, part_ref, inverse_ref, out_ref, *half_refs):
    side = meta[2 * out_ref.shape[0], 1] % 2
    for ref, at in ((same_ref, side), (other_ref, 1 - side)):
        state = part_ref[at] - coupling * turned(ref[...]) * inverse_ref[at]
        out_ref[at] = state
        for half_ref in half_refs:
            half_ref[at] = state.astype(half_ref.dtype)


def first_update(rows, meta, own, other, c_pieces, state, coulomb_own, inverse):
    orb_rows, virt, _ = state.shape
    shape = jax.ShapeDtypeStruct(state.shape, jnp.float32)
    flops, moved = 2 * orb_rows**2 * rows * virt**3, 4 * (orb_rows + 1) * orb_rows * rows * virt**2
    return call(
        functools.partial(first_body, rows), shape, [SMEM] + [VMEM] * (len(c_pieces) + 5), flops, moved,
        meta, own, other, *c_pieces, state, coulomb_own, inverse,
    )


def second_update(meta, same, other, part, inverse, with_half):
    shape = (jax.ShapeDtypeStruct(part.shape, jnp.float32), jax.ShapeDtypeStruct(part.shape, jnp.bfloat16))
    shape = shape if with_half else shape[:1]
    return call(second_body, shape, [SMEM] + [VMEM] * 4, 0, 16 * part.size, meta, same, other, part, inverse)


def on_device(
    rows,
    cols,
    amplitudes,
    coulomb,
    inner_list,
    inner_count,
    reader_list,
    reader_count,
    virtual_energy,
    occupied_energy,
):
    orb_rows, orb_cols, virt, _ = amplitudes.shape
    count = coulomb.shape[1]
    slots = inner_list.shape[2]
    assert orb_cols == 1 and count == cols == rows * orb_rows and orb_rows == 2
    halves = cols // 2
    my_row = lax.axis_index("row")
    my_col = lax.axis_index("col")

    def from_row(x, step):
        return lax.ppermute(x, "row", [(r ^ step, r) for r in range(rows)])

    def row_gathered(x):
        return [x] + [from_row(x, step) for step in range(1, rows)]

    def swapped(x):
        return lax.ppermute(x, "col", [(c ^ 1, c) for c in range(cols)])

    def from_chip(x, step):
        return lax.ppermute(x, "col", [(c ^ 2 * step, c) for c in range(cols)])

    def crossing(x, place, flip=0):
        pairs = []
        for r in range(rows):
            for c in range(cols):
                to_r, to_z = place(r, c // 2)
                pairs.append((r * cols + c, to_r * cols + 2 * to_z + (c % 2 ^ flip)))
        return lax.ppermute(x, ("row", "col"), pairs)

    def high_parts(r, z):
        return z - z % 2 + r % 2, r - r % 2 + z % 2

    def last_bits(r, z):
        return r - r % 2 + z % 2, z - z % 2 + r % 2

    state = amplitudes[:, 0]
    half = state.astype(jnp.bfloat16)

    slot_iota = jnp.arange(slots, dtype=jnp.int32)
    orbital_iota = jnp.arange(count, dtype=jnp.int32)

    def used(lists, counts):
        live = slot_iota[None] < counts[:, None]
        hit = (lists[:, :, None] == orbital_iota) & live[:, :, None]
        return jnp.any(hit, axis=1).astype(jnp.int32)

    inner_used = used(inner_list[:, 0], inner_count[:, 0])
    reader_used = used(
        lax.dynamic_index_in_dim(reader_list, my_col, 1, False), lax.dynamic_index_in_dim(reader_count, my_col, 1, False)
    )
    place = jnp.where(orbital_iota == 0, my_row, my_col).astype(jnp.int32)
    meta = jnp.concatenate([inner_used, reader_used, place[None]], axis=0)

    kept, coulomb_own, inverse = prologue(rows, meta, coulomb, virtual_energy, occupied_energy)

    for sweep_index in range(ITERS):
        a_pieces = row_gathered(half)
        column = {0: half, 1: from_chip(half, 1)}
        for step in range(2, halves, 2):
            column[step] = from_chip(half, step)
        coupled, same, other = coupled_blocks(rows, meta, kept, a_pieces)
        near = from_row(coupled, 1)
        c_pieces, far = [coupled, near], []
        for step in range(2, rows, 2):
            piece = from_row(coupled, step)
            far += [from_row(piece[0:1], 1), from_row(near[1:2], step)]
            c_pieces += [piece, *far[-2:]]
        same, other = crossing(same, high_parts), crossing(other, last_bits)
        for step in range(2, halves, 2):
            column[step] = tied(column[step], column[1], coupled)
            column[step + 1] = from_chip(column[step], 1)
        column = [column[step] for step in range(halves)]
        own = whole_column(meta, column, [*far, same, other])
        same, other = crossing(same, last_bits), crossing(other, high_parts, 1)
        part = first_update(rows, meta, own, swapped(own), c_pieces, state, coulomb_own, inverse)
        state, *halves_out = second_update(meta, same, other, part, inverse, sweep_index < ITERS - 1)
        half = halves_out[0] if halves_out else None
    return state[:, None]


def solution(mesh):
    return jax.shard_map(
        functools.partial(on_device, mesh.shape["row"], mesh.shape["col"]),
        mesh=mesh,
        in_specs=(
            P("row", "col", None, None),
            P("row", None, None, None),
            P("row", "col", None),
            P("row", "col"),
            P("row", None, None),
            P("row", None),
            P(),
            P(),
        ),
        out_specs=P("row", "col", None, None),
        check_vma=False,
    )
```

```python
import functools

import jax
import jax.numpy as jnp
from jax import lax
from jax.experimental import pallas as pl
from jax.experimental.pallas import tpu as pltpu
from jax.sharding import PartitionSpec as P

ITERS = 2


damping = 0.5
coupling = 0.03125
ANY = pl.BlockSpec(memory_space=pl.ANY)
SMEM = pl.BlockSpec(memory_space=pltpu.SMEM)
VMEM = pl.BlockSpec(memory_space=pltpu.VMEM)
VMEM_BYTES = 32 * 1024 * 1024


def call(body, out_shape, in_specs, flops, moved, *operands):
    single = isinstance(out_shape, jax.ShapeDtypeStruct)
    return pl.pallas_call(
        body,
        out_shape=out_shape,
        in_specs=in_specs,
        out_specs=VMEM if single else (VMEM,) * len(out_shape),
        compiler_params=pltpu.CompilerParams(vmem_limit_bytes=VMEM_BYTES),
        cost_estimate=pl.CostEstimate(flops=flops, bytes_accessed=moved, transcendentals=0),
    )(*operands)


def prologue_body(meta, occupied, k_ref, virt_row, virt_col, kept_ref, own_ref, inverse_ref):
    orb_rows, _, virt, _ = k_ref.shape
    my_row = meta[2 * orb_rows, 0]
    my_col = meta[2 * orb_rows, 1]
    for step in range(kept_ref.shape[0]):
        for t in range(orb_rows):
            orbital = (my_row ^ step) * orb_rows + t
            for i in range(orb_rows):
                block = k_ref[i, orbital]
                keep = jnp.where(meta[i, orbital] > 0, block, jnp.zeros_like(block))
                kept_ref[step, i * virt : (i + 1) * virt, t * virt : (t + 1) * virt] = keep
    virt_pair = virt_col[...] + virt_row[...]
    for i in range(orb_rows):
        own_ref[i] = k_ref[i, my_col]
        inverse_ref[i] = 1.0 / (virt_pair - occupied[0, my_row * orb_rows + i] - occupied[0, my_col])


def prologue(rows, meta, coulomb, virtual_energy, occupied_energy):
    orb_rows, count, virt, _ = coulomb.shape
    shape = (
        jax.ShapeDtypeStruct((rows, orb_rows * virt, orb_rows * virt), jnp.bfloat16),
        jax.ShapeDtypeStruct((orb_rows, virt, virt), jnp.bfloat16),
        jax.ShapeDtypeStruct((orb_rows, virt, virt), jnp.float32),
    )
    return call(
        prologue_body, shape, [SMEM, SMEM, VMEM, VMEM, VMEM], 0, 4 * orb_rows * count * virt**2,
        meta, occupied_energy[None], coulomb, virtual_energy[None], virtual_energy[:, None],
    )


def piece_blocks(refs, rows):
    found, refs, size = [], list(refs), refs[0].shape[0]
    for step in range(rows):
        blocks = []
        while len(blocks) < size:
            ref = refs.pop(0)
            blocks += [(ref, at) for at in range(ref.shape[0])]
        found.append(blocks)
    return found


def coupled_body(rows, k_ref, *refs):
    out_ref, same_ref, other_ref = refs[-3:]
    orb_rows, virt, _ = out_ref.shape
    side = lax.rem(lax.axis_index("col"), 2)
    total = None
    for step in range(rows):
        for t in range(orb_rows):
            left = k_ref[step, :, t * virt : (t + 1) * virt]
            part = jnp.dot(left, refs[step][t], preferred_element_type=jnp.float32)
            total = part if total is None else total + part
    first, second = total[:virt].astype(out_ref.dtype), total[virt:].astype(out_ref.dtype)
    out_ref[0], out_ref[1] = first, second

    @pl.when(side == 0)
    def _():
        same_ref[...], other_ref[...] = first, second

    @pl.when(side == 1)
    def _():
        same_ref[...], other_ref[...] = second, first


def coupled_blocks(rows, kept, pieces):
    orb_rows, virt, _ = pieces[0].shape
    count = rows * orb_rows
    block = jax.ShapeDtypeStruct((virt, virt), jnp.bfloat16)
    shape = (jax.ShapeDtypeStruct((orb_rows, virt, virt), jnp.bfloat16), block, block)
    body = functools.partial(coupled_body, rows)
    flops, moved = 2 * orb_rows * count * virt**3, 2 * (orb_rows + 1) * count * virt**2
    return call(body, shape, [VMEM] * (1 + len(pieces)), flops, moved, kept, *pieces)


def column_body(*refs):
    out_ref = refs[-1]
    orb_rows = refs[0].shape[0]
    my_place = lax.div(lax.axis_index("col"), 2)
    for step in range(out_ref.shape[0] // orb_rows):
        out_ref[pl.ds((my_place ^ step) * orb_rows, orb_rows)] = refs[step][...]


def whole_column(pieces, others):
    orb_rows, virt, _ = pieces[0].shape
    shape = jax.ShapeDtypeStruct((orb_rows * len(pieces), virt, virt), jnp.bfloat16)
    operands = [*pieces, *others]
    moved = 4 * orb_rows * len(pieces) * virt**2
    return call(column_body, shape, [VMEM] * len(operands), 0, moved, *operands)


def tied_body(*refs):
    pass


def tied(x, *others):
    return pl.pallas_call(
        tied_body,
        out_shape=jax.ShapeDtypeStruct(x.shape, x.dtype),
        in_specs=[VMEM] * (1 + len(others)),
        out_specs=VMEM,
        input_output_aliases={0: 0},
        compiler_params=pltpu.CompilerParams(vmem_limit_bytes=VMEM_BYTES),
    )(x, *others)


def masked_pair(meta, orbital, blocks):
    orb_rows = len(blocks)
    kept = [jnp.where(meta[orb_rows + i, orbital] > 0, block, jnp.zeros_like(block)) for i, block in enumerate(blocks)]
    return jnp.concatenate(kept, axis=0)


def turned(block):
    return jnp.transpose(block.astype(jnp.float32), (1, 0))


def first_body(rows, meta, own_ref, other_ref, *refs):
    state_ref, coulomb_ref, inverse_ref, out_ref = refs[-4:]
    orb_rows = out_ref.shape[0]
    blocks = piece_blocks(refs[:-4], rows)
    my_row, side = meta[2 * orb_rows, 0], meta[2 * orb_rows, 1] % 2
    total = None
    for step in range(rows):
        at = my_row ^ step
        for t in range(orb_rows):
            left = [
                jnp.where(side == t, own_ref[at * orb_rows + i], other_ref[at * orb_rows + i]) for i in range(orb_rows)
            ]
            left = masked_pair(meta, at * orb_rows + t, left)
            ref, place = blocks[step][t]
            part = jnp.dot(left, ref[place], preferred_element_type=jnp.float32)
            total = part if total is None else total + part
    linear = coulomb_ref[...].astype(jnp.float32) + coupling * refs[0][...].astype(jnp.float32)
    residual = linear + coupling * coupling * total.reshape(out_ref.shape)
    out_ref[...] = damping * state_ref[...] - residual * inverse_ref[...]


def second_body(same_ref, other_ref, part_ref, inverse_ref, out_ref, *half_refs):
    side = lax.rem(lax.axis_index("col"), 2)
    for ref, at in ((same_ref, side), (other_ref, 1 - side)):
        state = part_ref[at] - coupling * turned(ref[...]) * inverse_ref[at]
        out_ref[at] = state
        for half_ref in half_refs:
            half_ref[at] = state.astype(half_ref.dtype)


def first_update(rows, meta, own, other, c_pieces, state, coulomb_own, inverse):
    orb_rows, virt, _ = state.shape
    shape = jax.ShapeDtypeStruct(state.shape, jnp.float32)
    flops, moved = 2 * orb_rows**2 * rows * virt**3, 4 * (orb_rows + 1) * orb_rows * rows * virt**2
    return call(
        functools.partial(first_body, rows), shape, [SMEM] + [VMEM] * (len(c_pieces) + 5), flops, moved,
        meta, own, other, *c_pieces, state, coulomb_own, inverse,
    )


def second_update(same, other, part, inverse, with_half):
    shape = (jax.ShapeDtypeStruct(part.shape, jnp.float32), jax.ShapeDtypeStruct(part.shape, jnp.bfloat16))
    shape = shape if with_half else shape[:1]
    return call(second_body, shape, [VMEM] * 4, 0, 16 * part.size, same, other, part, inverse)


def on_device(
    rows,
    cols,
    amplitudes,
    coulomb,
    inner_list,
    inner_count,
    reader_list,
    reader_count,
    virtual_energy,
    occupied_energy,
):
    orb_rows, orb_cols, virt, _ = amplitudes.shape
    count = coulomb.shape[1]
    slots = inner_list.shape[2]
    assert orb_cols == 1 and count == cols == rows * orb_rows and orb_rows == 2
    halves = cols // 2
    my_row = lax.axis_index("row")
    my_col = lax.axis_index("col")

    def from_row(x, step):
        return lax.ppermute(x, "row", [(r ^ step, r) for r in range(rows)])

    def row_gathered(x):
        return [x] + [from_row(x, step) for step in range(1, rows)]

    def swapped(x):
        return lax.ppermute(x, "col", [(c ^ 1, c) for c in range(cols)])

    def from_chip(x, step):
        return lax.ppermute(x, "col", [(c ^ 2 * step, c) for c in range(cols)])

    def crossing(x, place, flip=0):
        pairs = []
        for r in range(rows):
            for c in range(cols):
                to_r, to_z = place(r, c // 2)
                pairs.append((r * cols + c, to_r * cols + 2 * to_z + (c % 2 ^ flip)))
        return lax.ppermute(x, ("row", "col"), pairs)

    def high_parts(r, z):
        return z - z % 2 + r % 2, r - r % 2 + z % 2

    def last_bits(r, z):
        return r - r % 2 + z % 2, z - z % 2 + r % 2

    state = amplitudes[:, 0]
    half = state.astype(jnp.bfloat16)

    slot_iota = jnp.arange(slots, dtype=jnp.int32)
    orbital_iota = jnp.arange(count, dtype=jnp.int32)

    def used(lists, counts):
        live = slot_iota[None] < counts[:, None]
        hit = (lists[:, :, None] == orbital_iota) & live[:, :, None]
        return jnp.any(hit, axis=1).astype(jnp.int32)

    inner_used = used(inner_list[:, 0], inner_count[:, 0])
    reader_used = used(
        lax.dynamic_index_in_dim(reader_list, my_col, 1, False), lax.dynamic_index_in_dim(reader_count, my_col, 1, False)
    )
    place = jnp.where(orbital_iota == 0, my_row, my_col).astype(jnp.int32)
    meta = jnp.concatenate([inner_used, reader_used, place[None]], axis=0)

    kept, coulomb_own, inverse = prologue(rows, meta, coulomb, virtual_energy, occupied_energy)

    for sweep_index in range(ITERS):
        a_pieces = row_gathered(half)
        column = {0: half, 1: from_chip(half, 1)}
        for step in range(2, halves, 2):
            column[step] = from_chip(half, step)
        coupled, same, other = coupled_blocks(rows, kept, a_pieces)
        near = from_row(coupled, 1)
        c_pieces, far = [coupled, near], []
        for step in range(2, rows, 2):
            piece = from_row(coupled, step)
            far += [from_row(piece[0:1], 1), from_row(near[1:2], step)]
            c_pieces += [piece, *far[-2:]]
        same, other = crossing(same, high_parts), crossing(other, last_bits)
        for step in range(2, halves, 2):
            column[step] = tied(column[step], column[1], coupled)
            column[step + 1] = from_chip(column[step], 1)
        column = [column[step] for step in range(halves)]
        own = whole_column(column, [*far, same, other])
        same, other = crossing(same, last_bits), crossing(other, high_parts, 1)
        part = first_update(rows, meta, own, swapped(own), c_pieces, state, coulomb_own, inverse)
        state, *halves_out = second_update(same, other, part, inverse, sweep_index < ITERS - 1)
        half = halves_out[0] if halves_out else None
    return state[:, None]


def solution(mesh):
    return jax.shard_map(
        functools.partial(on_device, mesh.shape["row"], mesh.shape["col"]),
        mesh=mesh,
        in_specs=(
            P("row", "col", None, None),
            P("row", None, None, None),
            P("row", "col", None),
            P("row", "col"),
            P("row", None, None),
            P("row", None),
            P(),
            P(),
        ),
        out_specs=P("row", "col", None, None),
        check_vma=False,
    )
```

```python
import functools

import jax
import jax.numpy as jnp
from jax import lax
from jax.experimental import pallas as pl
from jax.experimental.pallas import tpu as pltpu
from jax.sharding import PartitionSpec as P

ITERS = 2


damping = 0.5
coupling = 0.03125
ANY = pl.BlockSpec(memory_space=pl.ANY)
SMEM = pl.BlockSpec(memory_space=pltpu.SMEM)
VMEM = pl.BlockSpec(memory_space=pltpu.VMEM)
VMEM_BYTES = 32 * 1024 * 1024


def call(body, out_shape, in_specs, flops, moved, *operands):
    single = isinstance(out_shape, jax.ShapeDtypeStruct)
    return pl.pallas_call(
        body,
        out_shape=out_shape,
        in_specs=in_specs,
        out_specs=VMEM if single else (VMEM,) * len(out_shape),
        compiler_params=pltpu.CompilerParams(vmem_limit_bytes=VMEM_BYTES),
        cost_estimate=pl.CostEstimate(flops=flops, bytes_accessed=moved, transcendentals=0),
    )(*operands)


def prologue_body(meta, occupied, k_ref, virt_row, virt_col, kept_ref, own_ref, inverse_ref):
    orb_rows, _, virt, _ = k_ref.shape
    my_row = meta[2 * orb_rows, 0]
    my_col = meta[2 * orb_rows, 1]
    for step in range(kept_ref.shape[0]):
        for t in range(orb_rows):
            orbital = (my_row ^ step) * orb_rows + t
            for i in range(orb_rows):
                block = k_ref[i, orbital]
                keep = jnp.where(meta[i, orbital] > 0, block, jnp.zeros_like(block))
                kept_ref[step, i * virt : (i + 1) * virt, t * virt : (t + 1) * virt] = keep
    virt_pair = virt_col[...] + virt_row[...]
    for i in range(orb_rows):
        own_ref[i] = k_ref[i, my_col]
        inverse_ref[i] = 1.0 / (virt_pair - occupied[0, my_row * orb_rows + i] - occupied[0, my_col])


def prologue(rows, meta, coulomb, virtual_energy, occupied_energy):
    orb_rows, count, virt, _ = coulomb.shape
    shape = (
        jax.ShapeDtypeStruct((rows, orb_rows * virt, orb_rows * virt), jnp.bfloat16),
        jax.ShapeDtypeStruct((orb_rows, virt, virt), jnp.bfloat16),
        jax.ShapeDtypeStruct((orb_rows, virt, virt), jnp.float32),
    )
    return call(
        prologue_body, shape, [SMEM, SMEM, VMEM, VMEM, VMEM], 0, 4 * orb_rows * count * virt**2,
        meta, occupied_energy[None], coulomb, virtual_energy[None], virtual_energy[:, None],
    )


def piece_blocks(refs, rows):
    found, refs, size = [], list(refs), refs[0].shape[0]
    for step in range(rows):
        blocks = []
        while len(blocks) < size:
            ref = refs.pop(0)
            blocks += [(ref, at) for at in range(ref.shape[0])]
        found.append(blocks)
    return found


def coupled_body(rows, k_ref, *refs):
    out_ref, same_ref, other_ref = refs[-3:]
    orb_rows, virt, _ = out_ref.shape
    side = lax.rem(lax.axis_index("col"), 2)
    total = None
    for step in range(rows):
        for t in range(orb_rows):
            left = k_ref[step, :, t * virt : (t + 1) * virt]
            part = jnp.dot(left, refs[step][t], preferred_element_type=jnp.float32)
            total = part if total is None else total + part
    first, second = total[:virt].astype(out_ref.dtype), total[virt:].astype(out_ref.dtype)
    out_ref[0], out_ref[1] = first, second

    @pl.when(side == 0)
    def _():
        same_ref[...], other_ref[...] = first, second

    @pl.when(side == 1)
    def _():
        same_ref[...], other_ref[...] = second, first


def coupled_blocks(rows, kept, pieces):
    orb_rows, virt, _ = pieces[0].shape
    count = rows * orb_rows
    block = jax.ShapeDtypeStruct((virt, virt), jnp.bfloat16)
    shape = (jax.ShapeDtypeStruct((orb_rows, virt, virt), jnp.bfloat16), block, block)
    body = functools.partial(coupled_body, rows)
    flops, moved = 2 * orb_rows * count * virt**3, 2 * (orb_rows + 1) * count * virt**2
    return call(body, shape, [VMEM] * (1 + len(pieces)), flops, moved, kept, *pieces)


def column_body(*refs):
    out_ref = refs[-1]
    orb_rows = refs[0].shape[0]
    my_place = lax.div(lax.axis_index("col"), 2)
    for step in range(out_ref.shape[0] // orb_rows):
        out_ref[pl.ds((my_place ^ step) * orb_rows, orb_rows)] = refs[step][...]


def whole_column(pieces, others):
    orb_rows, virt, _ = pieces[0].shape
    shape = jax.ShapeDtypeStruct((orb_rows * len(pieces), virt, virt), jnp.bfloat16)
    operands = [*pieces, *others]
    moved = 4 * orb_rows * len(pieces) * virt**2
    return call(column_body, shape, [VMEM] * len(operands), 0, moved, *operands)


def tied_body(*refs):
    pass


def tied(x, *others):
    return pl.pallas_call(
        tied_body,
        out_shape=jax.ShapeDtypeStruct(x.shape, x.dtype),
        in_specs=[VMEM] * (1 + len(others)),
        out_specs=VMEM,
        input_output_aliases={0: 0},
        compiler_params=pltpu.CompilerParams(vmem_limit_bytes=VMEM_BYTES),
    )(x, *others)


def masked_pair(meta, orbital, blocks):
    orb_rows = len(blocks)
    kept = [jnp.where(meta[orb_rows + i, orbital] > 0, block, jnp.zeros_like(block)) for i, block in enumerate(blocks)]
    return jnp.concatenate(kept, axis=0)


def turned(block):
    return jnp.transpose(block.astype(jnp.float32), (1, 0))


def first_body(rows, meta, own_ref, other_ref, *refs):
    state_ref, coulomb_ref, inverse_ref, out_ref = refs[-4:]
    orb_rows = out_ref.shape[0]
    blocks = piece_blocks(refs[:-4], rows)
    my_row, side = meta[2 * orb_rows, 0], meta[2 * orb_rows, 1] % 2
    total = None
    for step in range(rows):
        at = my_row ^ step
        for t in range(orb_rows):
            left = [
                jnp.where(side == t, own_ref[at * orb_rows + i], other_ref[at * orb_rows + i]) for i in range(orb_rows)
            ]
            left = masked_pair(meta, at * orb_rows + t, left)
            ref, place = blocks[step][t]
            part = jnp.dot(left, ref[place], preferred_element_type=jnp.float32)
            total = part if total is None else total + part
    linear = coulomb_ref[...].astype(jnp.float32) + coupling * refs[0][...].astype(jnp.float32)
    residual = linear + coupling * coupling * total.reshape(out_ref.shape)
    out_ref[...] = damping * state_ref[...] - residual * inverse_ref[...]


def second_body(same_ref, other_ref, part_ref, inverse_ref, out_ref, *half_refs):
    side = lax.rem(lax.axis_index("col"), 2)
    for ref, at in ((same_ref, side), (other_ref, 1 - side)):
        state = part_ref[at] - coupling * turned(ref[...]) * inverse_ref[at]
        out_ref[at] = state
        for half_ref in half_refs:
            half_ref[at] = state.astype(half_ref.dtype)


def first_update(rows, meta, own, other, c_pieces, state, coulomb_own, inverse):
    orb_rows, virt, _ = state.shape
    shape = jax.ShapeDtypeStruct(state.shape, jnp.float32)
    flops, moved = 2 * orb_rows**2 * rows * virt**3, 4 * (orb_rows + 1) * orb_rows * rows * virt**2
    return call(
        functools.partial(first_body, rows), shape, [SMEM] + [VMEM] * (len(c_pieces) + 5), flops, moved,
        meta, own, other, *c_pieces, state, coulomb_own, inverse,
    )


def second_update(same, other, part, inverse, with_half):
    shape = (jax.ShapeDtypeStruct(part.shape, jnp.float32), jax.ShapeDtypeStruct(part.shape, jnp.bfloat16))
    shape = shape if with_half else shape[:1]
    return call(second_body, shape, [VMEM] * 4, 0, 16 * part.size, same, other, part, inverse)


def on_device(
    rows,
    cols,
    amplitudes,
    coulomb,
    inner_list,
    inner_count,
    reader_list,
    reader_count,
    virtual_energy,
    occupied_energy,
):
    orb_rows, orb_cols, virt, _ = amplitudes.shape
    count = coulomb.shape[1]
    slots = inner_list.shape[2]
    assert orb_cols == 1 and count == cols == rows * orb_rows and orb_rows == 2
    halves = cols // 2
    my_row = lax.axis_index("row")
    my_col = lax.axis_index("col")

    def from_row(x, step):
        return lax.ppermute(x, "row", [(r ^ step, r) for r in range(rows)])

    def row_gathered(x):
        return [x] + [from_row(x, step) for step in range(1, rows)]

    def swapped(x):
        return lax.ppermute(x, "col", [(c ^ 1, c) for c in range(cols)])

    def from_chip(x, step):
        return lax.ppermute(x, "col", [(c ^ 2 * step, c) for c in range(cols)])

    def crossing(x, place, flip=0):
        pairs = []
        for r in range(rows):
            for c in range(cols):
                to_r, to_z = place(r, c // 2)
                pairs.append((r * cols + c, to_r * cols + 2 * to_z + (c % 2 ^ flip)))
        return lax.ppermute(x, ("row", "col"), pairs)

    def high_parts(r, z):
        return z - z % 2 + r % 2, r - r % 2 + z % 2

    def last_bits(r, z):
        return r - r % 2 + z % 2, z - z % 2 + r % 2

    state = amplitudes[:, 0]
    half = state.astype(jnp.bfloat16)

    slot_iota = jnp.arange(slots, dtype=jnp.int32)
    orbital_iota = jnp.arange(count, dtype=jnp.int32)

    def used(lists, counts):
        live = slot_iota[None] < counts[:, None]
        hit = (lists[:, :, None] == orbital_iota) & live[:, :, None]
        return jnp.any(hit, axis=1).astype(jnp.int32)

    inner_used = used(inner_list[:, 0], inner_count[:, 0])
    reader_used = used(
        lax.dynamic_index_in_dim(reader_list, my_col, 1, False), lax.dynamic_index_in_dim(reader_count, my_col, 1, False)
    )
    place = jnp.where(orbital_iota == 0, my_row, my_col).astype(jnp.int32)
    meta = jnp.concatenate([inner_used, reader_used, place[None]], axis=0)

    kept, coulomb_own, inverse = prologue(rows, meta, coulomb, virtual_energy, occupied_energy)

    for sweep_index in range(ITERS):
        a_pieces = row_gathered(half)
        column = {0: half, 1: from_chip(half, 1)}
        for step in range(2, halves, 2):
            column[step] = from_chip(half, step)
        coupled, same, other = coupled_blocks(rows, kept, a_pieces)
        near = from_row(coupled, 1)
        c_pieces, far = [coupled, near], []
        for step in range(2, rows, 2):
            piece = from_row(coupled, step)
            far += [from_row(piece[0:1], 1), from_row(near[1:2], step)]
            c_pieces += [piece, *far[-2:]]
        same, other = crossing(same, high_parts), crossing(other, last_bits)
        for step in range(2, halves, 2):
            column[step] = tied(column[step], column[1], same, other)
            column[step + 1] = from_chip(column[step], 1)
        column = [column[step] for step in range(halves)]
        same, other = crossing(same, last_bits), crossing(other, high_parts, 1)
        own = whole_column(column, [*far, same, other])
        part = first_update(rows, meta, own, swapped(own), c_pieces, state, coulomb_own, inverse)
        state, *halves_out = second_update(same, other, part, inverse, sweep_index < ITERS - 1)
        half = halves_out[0] if halves_out else None
    return state[:, None]


def solution(mesh):
    return jax.shard_map(
        functools.partial(on_device, mesh.shape["row"], mesh.shape["col"]),
        mesh=mesh,
        in_specs=(
            P("row", "col", None, None),
            P("row", None, None, None),
            P("row", "col", None),
            P("row", "col"),
            P("row", None, None),
            P("row", None),
            P(),
            P(),
        ),
        out_specs=P("row", "col", None, None),
        check_vma=False,
    )
```

```python
import functools

import jax
import jax.numpy as jnp
from jax import lax
from jax.experimental import pallas as pl
from jax.experimental.pallas import tpu as pltpu
from jax.sharding import PartitionSpec as P

ITERS = 2


damping = 0.5
coupling = 0.03125
ANY = pl.BlockSpec(memory_space=pl.ANY)
SMEM = pl.BlockSpec(memory_space=pltpu.SMEM)
VMEM = pl.BlockSpec(memory_space=pltpu.VMEM)
VMEM_BYTES = 32 * 1024 * 1024


def call(body, out_shape, in_specs, flops, moved, *operands):
    single = isinstance(out_shape, jax.ShapeDtypeStruct)
    return pl.pallas_call(
        body,
        out_shape=out_shape,
        in_specs=in_specs,
        out_specs=VMEM if single else (VMEM,) * len(out_shape),
        compiler_params=pltpu.CompilerParams(vmem_limit_bytes=VMEM_BYTES),
        cost_estimate=pl.CostEstimate(flops=flops, bytes_accessed=moved, transcendentals=0),
    )(*operands)


def prologue_body(meta, occupied, k_ref, virt_row, virt_col, kept_ref, own_ref, inverse_ref):
    orb_rows, _, virt, _ = k_ref.shape
    my_row = meta[2 * orb_rows, 0]
    my_col = meta[2 * orb_rows, 1]
    for step in range(kept_ref.shape[0]):
        for t in range(orb_rows):
            orbital = (my_row ^ step) * orb_rows + t
            for i in range(orb_rows):
                block = k_ref[i, orbital]
                keep = jnp.where(meta[i, orbital] > 0, block, jnp.zeros_like(block))
                kept_ref[step, i * virt : (i + 1) * virt, t * virt : (t + 1) * virt] = keep
    virt_pair = virt_col[...] + virt_row[...]
    for i in range(orb_rows):
        own_ref[i] = k_ref[i, my_col]
        inverse_ref[i] = 1.0 / (virt_pair - occupied[0, my_row * orb_rows + i] - occupied[0, my_col])


def prologue(rows, meta, coulomb, virtual_energy, occupied_energy):
    orb_rows, count, virt, _ = coulomb.shape
    shape = (
        jax.ShapeDtypeStruct((rows, orb_rows * virt, orb_rows * virt), jnp.bfloat16),
        jax.ShapeDtypeStruct((orb_rows, virt, virt), jnp.bfloat16),
        jax.ShapeDtypeStruct((orb_rows, virt, virt), jnp.float32),
    )
    return call(
        prologue_body, shape, [SMEM, SMEM, VMEM, VMEM, VMEM], 0, 4 * orb_rows * count * virt**2,
        meta, occupied_energy[None], coulomb, virtual_energy[None], virtual_energy[:, None],
    )


def piece_blocks(refs, rows):
    found, refs, size = [], list(refs), refs[0].shape[0]
    for step in range(rows):
        blocks = []
        while len(blocks) < size:
            ref = refs.pop(0)
            blocks += [(ref, at) for at in range(ref.shape[0])]
        found.append(blocks)
    return found


def coupled_body(rows, k_ref, *refs):
    out_ref, same_ref, other_ref = refs[-3:]
    orb_rows, virt, _ = out_ref.shape
    side = lax.rem(lax.axis_index("col"), 2)
    total = None
    for step in range(rows):
        for t in range(orb_rows):
            left = k_ref[step, :, t * virt : (t + 1) * virt]
            part = jnp.dot(left, refs[step][t], preferred_element_type=jnp.float32)
            total = part if total is None else total + part
    first, second = total[:virt].astype(out_ref.dtype), total[virt:].astype(out_ref.dtype)
    out_ref[0], out_ref[1] = first, second

    @pl.when(side == 0)
    def _():
        same_ref[...], other_ref[...] = first, second

    @pl.when(side == 1)
    def _():
        same_ref[...], other_ref[...] = second, first


def coupled_blocks(rows, kept, pieces):
    orb_rows, virt, _ = pieces[0].shape
    count = rows * orb_rows
    block = jax.ShapeDtypeStruct((virt, virt), jnp.bfloat16)
    shape = (jax.ShapeDtypeStruct((orb_rows, virt, virt), jnp.bfloat16), block, block)
    body = functools.partial(coupled_body, rows)
    flops, moved = 2 * orb_rows * count * virt**3, 2 * (orb_rows + 1) * count * virt**2
    return call(body, shape, [VMEM] * (1 + len(pieces)), flops, moved, kept, *pieces)


def column_body(*refs):
    out_ref = refs[-1]
    orb_rows = refs[0].shape[0]
    my_place = lax.div(lax.axis_index("col"), 2)
    for step in range(out_ref.shape[0] // orb_rows):
        out_ref[pl.ds((my_place ^ step) * orb_rows, orb_rows)] = refs[step][...]


def whole_column(pieces, others):
    orb_rows, virt, _ = pieces[0].shape
    shape = jax.ShapeDtypeStruct((orb_rows * len(pieces), virt, virt), jnp.bfloat16)
    operands = [*pieces, *others]
    moved = 4 * orb_rows * len(pieces) * virt**2
    return call(column_body, shape, [VMEM] * len(operands), 0, moved, *operands)


def tied_body(*refs):
    pass


def tied(x, *others):
    return pl.pallas_call(
        tied_body,
        out_shape=jax.ShapeDtypeStruct(x.shape, x.dtype),
        in_specs=[VMEM] * (1 + len(others)),
        out_specs=VMEM,
        input_output_aliases={0: 0},
        compiler_params=pltpu.CompilerParams(vmem_limit_bytes=VMEM_BYTES),
    )(x, *others)


def masked_pair(meta, orbital, blocks):
    orb_rows = len(blocks)
    kept = [jnp.where(meta[orb_rows + i, orbital] > 0, block, jnp.zeros_like(block)) for i, block in enumerate(blocks)]
    return jnp.concatenate(kept, axis=0)


def turned(block):
    return jnp.transpose(block.astype(jnp.float32), (1, 0))


def first_body(rows, meta, own_ref, other_ref, *refs):
    state_ref, coulomb_ref, inverse_ref, out_ref = refs[-4:]
    orb_rows = out_ref.shape[0]
    blocks = piece_blocks(refs[:-4], rows)
    my_row, side = meta[2 * orb_rows, 0], meta[2 * orb_rows, 1] % 2
    total = None
    for step in range(rows):
        at = my_row ^ step
        for t in range(orb_rows):
            left = [
                jnp.where(side == t, own_ref[at * orb_rows + i], other_ref[at * orb_rows + i]) for i in range(orb_rows)
            ]
            left = masked_pair(meta, at * orb_rows + t, left)
            ref, place = blocks[step][t]
            part = jnp.dot(left, ref[place], preferred_element_type=jnp.float32)
            total = part if total is None else total + part
    linear = coulomb_ref[...].astype(jnp.float32) + coupling * refs[0][...].astype(jnp.float32)
    residual = linear + coupling * coupling * total.reshape(out_ref.shape)
    out_ref[...] = damping * state_ref[...] - residual * inverse_ref[...]


def second_body(same_ref, other_ref, part_ref, inverse_ref, out_ref, *half_refs):
    side = lax.rem(lax.axis_index("col"), 2)
    for ref, at in ((same_ref, side), (other_ref, 1 - side)):
        state = part_ref[at] - coupling * turned(ref[...]) * inverse_ref[at]
        out_ref[at] = state
        for half_ref in half_refs:
            half_ref[at] = state.astype(half_ref.dtype)


def first_update(rows, meta, own, other, c_pieces, state, coulomb_own, inverse):
    orb_rows, virt, _ = state.shape
    shape = jax.ShapeDtypeStruct(state.shape, jnp.float32)
    flops, moved = 2 * orb_rows**2 * rows * virt**3, 4 * (orb_rows + 1) * orb_rows * rows * virt**2
    return call(
        functools.partial(first_body, rows), shape, [SMEM] + [VMEM] * (len(c_pieces) + 5), flops, moved,
        meta, own, other, *c_pieces, state, coulomb_own, inverse,
    )


def second_update(same, other, part, inverse, with_half):
    shape = (jax.ShapeDtypeStruct(part.shape, jnp.float32), jax.ShapeDtypeStruct(part.shape, jnp.bfloat16))
    shape = shape if with_half else shape[:1]
    return call(second_body, shape, [VMEM] * 4, 0, 16 * part.size, same, other, part, inverse)


def on_device(
    rows,
    cols,
    amplitudes,
    coulomb,
    inner_list,
    inner_count,
    reader_list,
    reader_count,
    virtual_energy,
    occupied_energy,
):
    orb_rows, orb_cols, virt, _ = amplitudes.shape
    count = coulomb.shape[1]
    slots = inner_list.shape[2]
    assert orb_cols == 1 and count == cols == rows * orb_rows and orb_rows == 2
    halves = cols // 2
    my_row = lax.axis_index("row")
    my_col = lax.axis_index("col")

    def from_row(x, step):
        return lax.ppermute(x, "row", [(r ^ step, r) for r in range(rows)])

    def row_gathered(x):
        return [x] + [from_row(x, step) for step in range(1, rows)]

    def swapped(x):
        return lax.ppermute(x, "col", [(c ^ 1, c) for c in range(cols)])

    def from_chip(x, step):
        return lax.ppermute(x, "col", [(c ^ 2 * step, c) for c in range(cols)])

    def crossing(x, place, flip=0):
        pairs = []
        for r in range(rows):
            for c in range(cols):
                to_r, to_z = place(r, c // 2)
                pairs.append((r * cols + c, to_r * cols + 2 * to_z + (c % 2 ^ flip)))
        return lax.ppermute(x, ("row", "col"), pairs)

    def high_parts(r, z):
        return z - z % 2 + r % 2, r - r % 2 + z % 2

    def last_bits(r, z):
        return r - r % 2 + z % 2, z - z % 2 + r % 2

    state = amplitudes[:, 0]
    half = state.astype(jnp.bfloat16)

    slot_iota = jnp.arange(slots, dtype=jnp.int32)
    orbital_iota = jnp.arange(count, dtype=jnp.int32)

    def used(lists, counts):
        live = slot_iota[None] < counts[:, None]
        hit = (lists[:, :, None] == orbital_iota) & live[:, :, None]
        return jnp.any(hit, axis=1).astype(jnp.int32)

    inner_used = used(inner_list[:, 0], inner_count[:, 0])
    reader_used = used(
        lax.dynamic_index_in_dim(reader_list, my_col, 1, False), lax.dynamic_index_in_dim(reader_count, my_col, 1, False)
    )
    place = jnp.where(orbital_iota == 0, my_row, my_col).astype(jnp.int32)
    meta = jnp.concatenate([inner_used, reader_used, place[None]], axis=0)

    kept, coulomb_own, inverse = prologue(rows, meta, coulomb, virtual_energy, occupied_energy)

    for sweep_index in range(ITERS):
        a_pieces = row_gathered(half)
        column = {0: half, 1: from_chip(half, 1)}
        for step in range(2, halves, 2):
            column[step] = from_chip(half, step)
        coupled, same, other = coupled_blocks(rows, kept, a_pieces)
        near = from_row(coupled, 1)
        c_pieces, far = [coupled, near], []
        for step in range(2, rows, 2):
            far.append(from_row(near, step))
            c_pieces += [from_row(coupled, step), far[-1]]
        same, other = crossing(same, high_parts), crossing(other, last_bits)
        for step in range(2, halves, 2):
            column[step] = tied(column[step], column[1], coupled)
            column[step + 1] = from_chip(column[step], 1)
        column = [column[step] for step in range(halves)]
        own = whole_column(column, [*far, same, other])
        same, other = crossing(same, last_bits), crossing(other, high_parts, 1)
        part = first_update(rows, meta, own, swapped(own), c_pieces, state, coulomb_own, inverse)
        state, *halves_out = second_update(same, other, part, inverse, sweep_index < ITERS - 1)
        half = halves_out[0] if halves_out else None
    return state[:, None]


def solution(mesh):
    return jax.shard_map(
        functools.partial(on_device, mesh.shape["row"], mesh.shape["col"]),
        mesh=mesh,
        in_specs=(
            P("row", "col", None, None),
            P("row", None, None, None),
            P("row", "col", None),
            P("row", "col"),
            P("row", None, None),
            P("row", None),
            P(),
            P(),
        ),
        out_specs=P("row", "col", None, None),
        check_vma=False,
    )
```

```python
import functools

import jax
import jax.numpy as jnp
from jax import lax
from jax.experimental import pallas as pl
from jax.experimental.pallas import tpu as pltpu
from jax.sharding import PartitionSpec as P

ITERS = 2


damping = 0.5
coupling = 0.03125
ANY = pl.BlockSpec(memory_space=pl.ANY)
SMEM = pl.BlockSpec(memory_space=pltpu.SMEM)
VMEM = pl.BlockSpec(memory_space=pltpu.VMEM)
VMEM_BYTES = 32 * 1024 * 1024


def call(body, out_shape, in_specs, flops, moved, *operands):
    single = isinstance(out_shape, jax.ShapeDtypeStruct)
    return pl.pallas_call(
        body,
        out_shape=out_shape,
        in_specs=in_specs,
        out_specs=VMEM if single else (VMEM,) * len(out_shape),
        compiler_params=pltpu.CompilerParams(vmem_limit_bytes=VMEM_BYTES),
        cost_estimate=pl.CostEstimate(flops=flops, bytes_accessed=moved, transcendentals=0),
    )(*operands)


def prologue_body(meta, occupied, k_ref, virt_row, virt_col, kept_ref, own_ref, inverse_ref):
    orb_rows, _, virt, _ = k_ref.shape
    my_row = meta[2 * orb_rows, 0]
    my_col = meta[2 * orb_rows, 1]
    for step in range(kept_ref.shape[0]):
        for t in range(orb_rows):
            orbital = (my_row ^ step) * orb_rows + t
            for i in range(orb_rows):
                block = k_ref[i, orbital]
                keep = jnp.where(meta[i, orbital] > 0, block, jnp.zeros_like(block))
                kept_ref[step, i * virt : (i + 1) * virt, t * virt : (t + 1) * virt] = keep
    virt_pair = virt_col[...] + virt_row[...]
    for i in range(orb_rows):
        own_ref[i] = k_ref[i, my_col]
        inverse_ref[i] = 1.0 / (virt_pair - occupied[0, my_row * orb_rows + i] - occupied[0, my_col])


def prologue(rows, meta, coulomb, virtual_energy, occupied_energy):
    orb_rows, count, virt, _ = coulomb.shape
    shape = (
        jax.ShapeDtypeStruct((rows, orb_rows * virt, orb_rows * virt), jnp.bfloat16),
        jax.ShapeDtypeStruct((orb_rows, virt, virt), jnp.bfloat16),
        jax.ShapeDtypeStruct((orb_rows, virt, virt), jnp.float32),
    )
    return call(
        prologue_body, shape, [SMEM, SMEM, VMEM, VMEM, VMEM], 0, 4 * orb_rows * count * virt**2,
        meta, occupied_energy[None], coulomb, virtual_energy[None], virtual_energy[:, None],
    )


def piece_blocks(refs, rows):
    found, refs, size = [], list(refs), refs[0].shape[0]
    for step in range(rows):
        blocks = []
        while len(blocks) < size:
            ref = refs.pop(0)
            blocks += [(ref, at) for at in range(ref.shape[0])]
        found.append(blocks)
    return found


def coupled_body(rows, k_ref, *refs):
    out_ref, same_ref, other_ref = refs[-3:]
    orb_rows, virt, _ = out_ref.shape
    side = lax.rem(lax.axis_index("col"), 2)
    total = None
    for step in range(rows):
        for t in range(orb_rows):
            left = k_ref[step, :, t * virt : (t + 1) * virt]
            part = jnp.dot(left, refs[step][t], preferred_element_type=jnp.float32)
            total = part if total is None else total + part
    first, second = total[:virt].astype(out_ref.dtype), total[virt:].astype(out_ref.dtype)
    out_ref[0], out_ref[1] = first, second

    @pl.when(side == 0)
    def _():
        same_ref[...], other_ref[...] = first, second

    @pl.when(side == 1)
    def _():
        same_ref[...], other_ref[...] = second, first


def coupled_blocks(rows, kept, pieces):
    orb_rows, virt, _ = pieces[0].shape
    count = rows * orb_rows
    block = jax.ShapeDtypeStruct((virt, virt), jnp.bfloat16)
    shape = (jax.ShapeDtypeStruct((orb_rows, virt, virt), jnp.bfloat16), block, block)
    body = functools.partial(coupled_body, rows)
    flops, moved = 2 * orb_rows * count * virt**3, 2 * (orb_rows + 1) * count * virt**2
    return call(body, shape, [VMEM] * (1 + len(pieces)), flops, moved, kept, *pieces)


def column_body(*refs):
    out_ref = refs[-1]
    orb_rows = refs[0].shape[0]
    my_place = lax.div(lax.axis_index("col"), 2)
    for step in range(out_ref.shape[0] // orb_rows):
        out_ref[pl.ds((my_place ^ step) * orb_rows, orb_rows)] = refs[step][...]


def whole_column(pieces, others):
    orb_rows, virt, _ = pieces[0].shape
    shape = jax.ShapeDtypeStruct((orb_rows * len(pieces), virt, virt), jnp.bfloat16)
    operands = [*pieces, *others]
    moved = 4 * orb_rows * len(pieces) * virt**2
    return call(column_body, shape, [VMEM] * len(operands), 0, moved, *operands)


def tied_body(*refs):
    pass


def tied(x, *others):
    return pl.pallas_call(
        tied_body,
        out_shape=jax.ShapeDtypeStruct(x.shape, x.dtype),
        in_specs=[VMEM] * (1 + len(others)),
        out_specs=VMEM,
        input_output_aliases={0: 0},
        compiler_params=pltpu.CompilerParams(vmem_limit_bytes=VMEM_BYTES),
    )(x, *others)


def masked_pair(meta, orbital, blocks):
    orb_rows = len(blocks)
    kept = [jnp.where(meta[orb_rows + i, orbital] > 0, block, jnp.zeros_like(block)) for i, block in enumerate(blocks)]
    return jnp.concatenate(kept, axis=0)


def turned(block):
    return jnp.transpose(block.astype(jnp.float32), (1, 0))


def first_body(rows, meta, own_ref, other_ref, *refs):
    state_ref, coulomb_ref, inverse_ref, out_ref = refs[-4:]
    orb_rows = out_ref.shape[0]
    blocks = piece_blocks(refs[:-4], rows)
    my_row, side = meta[2 * orb_rows, 0], meta[2 * orb_rows, 1] % 2
    total = None
    for step in range(rows):
        at = my_row ^ step
        for t in range(orb_rows):
            left = [
                jnp.where(side == t, own_ref[at * orb_rows + i], other_ref[at * orb_rows + i]) for i in range(orb_rows)
            ]
            left = masked_pair(meta, at * orb_rows + t, left)
            ref, place = blocks[step][t]
            part = jnp.dot(left, ref[place], preferred_element_type=jnp.float32)
            total = part if total is None else total + part
    linear = coulomb_ref[...].astype(jnp.float32) + coupling * refs[0][...].astype(jnp.float32)
    residual = linear + coupling * coupling * total.reshape(out_ref.shape)
    out_ref[...] = damping * state_ref[...] - residual * inverse_ref[...]


def second_body(same_ref, other_ref, part_ref, inverse_ref, out_ref, *half_refs):
    side = lax.rem(lax.axis_index("col"), 2)
    for ref, at in ((same_ref, side), (other_ref, 1 - side)):
        state = part_ref[at] - coupling * turned(ref[...]) * inverse_ref[at]
        out_ref[at] = state
        for half_ref in half_refs:
            half_ref[at] = state.astype(half_ref.dtype)


def first_update(rows, meta, own, other, c_pieces, state, coulomb_own, inverse):
    orb_rows, virt, _ = state.shape
    shape = jax.ShapeDtypeStruct(state.shape, jnp.float32)
    flops, moved = 2 * orb_rows**2 * rows * virt**3, 4 * (orb_rows + 1) * orb_rows * rows * virt**2
    return call(
        functools.partial(first_body, rows), shape, [SMEM] + [VMEM] * (len(c_pieces) + 5), flops, moved,
        meta, own, other, *c_pieces, state, coulomb_own, inverse,
    )


def second_update(same, other, part, inverse, with_half):
    shape = (jax.ShapeDtypeStruct(part.shape, jnp.float32), jax.ShapeDtypeStruct(part.shape, jnp.bfloat16))
    shape = shape if with_half else shape[:1]
    return call(second_body, shape, [VMEM] * 4, 0, 16 * part.size, same, other, part, inverse)


def on_device(
    rows,
    cols,
    amplitudes,
    coulomb,
    inner_list,
    inner_count,
    reader_list,
    reader_count,
    virtual_energy,
    occupied_energy,
):
    orb_rows, orb_cols, virt, _ = amplitudes.shape
    count = coulomb.shape[1]
    slots = inner_list.shape[2]
    assert orb_cols == 1 and count == cols == rows * orb_rows and orb_rows == 2
    halves = cols // 2
    my_row = lax.axis_index("row")
    my_col = lax.axis_index("col")

    def from_row(x, step):
        return lax.ppermute(x, "row", [(r ^ step, r) for r in range(rows)])

    def row_gathered(x):
        return [x] + [from_row(x, step) for step in range(1, rows)]

    def swapped(x):
        return lax.ppermute(x, "col", [(c ^ 1, c) for c in range(cols)])

    def from_chip(x, step):
        return lax.ppermute(x, "col", [(c ^ 2 * step, c) for c in range(cols)])

    def crossing(x, place, flip=0):
        pairs = []
        for r in range(rows):
            for c in range(cols):
                to_r, to_z = place(r, c // 2)
                pairs.append((r * cols + c, to_r * cols + 2 * to_z + (c % 2 ^ flip)))
        return lax.ppermute(x, ("row", "col"), pairs)

    def high_parts(r, z):
        return z - z % 2 + r % 2, r - r % 2 + z % 2

    def last_bits(r, z):
        return r - r % 2 + z % 2, z - z % 2 + r % 2

    state = amplitudes[:, 0]
    half = state.astype(jnp.bfloat16)

    slot_iota = jnp.arange(slots, dtype=jnp.int32)
    orbital_iota = jnp.arange(count, dtype=jnp.int32)

    def used(lists, counts):
        live = slot_iota[None] < counts[:, None]
        hit = (lists[:, :, None] == orbital_iota) & live[:, :, None]
        return jnp.any(hit, axis=1).astype(jnp.int32)

    inner_used = used(inner_list[:, 0], inner_count[:, 0])
    reader_used = used(
        lax.dynamic_index_in_dim(reader_list, my_col, 1, False), lax.dynamic_index_in_dim(reader_count, my_col, 1, False)
    )
    place = jnp.where(orbital_iota == 0, my_row, my_col).astype(jnp.int32)
    meta = jnp.concatenate([inner_used, reader_used, place[None]], axis=0)

    kept, coulomb_own, inverse = prologue(rows, meta, coulomb, virtual_energy, occupied_energy)

    for sweep_index in range(ITERS):
        a_pieces = row_gathered(half)
        column = {0: half, 1: from_chip(half, 1)}
        for step in range(2, halves, 2):
            column[step] = from_chip(half, step)
        coupled, same, other = coupled_blocks(rows, kept, a_pieces)
        near = from_row(coupled, 1)
        c_pieces, far = [coupled, near], []
        for step in range(2, rows, 2):
            piece = from_row(coupled, step)
            far += [from_row(piece[0:1], 1), from_row(near[1:2], step)]
            c_pieces += [piece, *far[-2:]]
        same, other = crossing(same, high_parts), crossing(other, last_bits)
        for step in range(2, halves, 2):
            column[step] = tied(column[step], column[1], coupled)
            column[step + 1] = from_chip(column[step], 1)
        column = [column[step] for step in range(halves)]
        own = whole_column(column, [c_pieces[1], c_pieces[2], same, other])
        same, other = crossing(same, last_bits), crossing(other, high_parts, 1)
        part = first_update(rows, meta, own, swapped(own), c_pieces, state, coulomb_own, inverse)
        state, *halves_out = second_update(same, other, part, inverse, sweep_index < ITERS - 1)
        half = halves_out[0] if halves_out else None
    return state[:, None]


def solution(mesh):
    return jax.shard_map(
        functools.partial(on_device, mesh.shape["row"], mesh.shape["col"]),
        mesh=mesh,
        in_specs=(
            P("row", "col", None, None),
            P("row", None, None, None),
            P("row", "col", None),
            P("row", "col"),
            P("row", None, None),
            P("row", None),
            P(),
            P(),
        ),
        out_specs=P("row", "col", None, None),
        check_vma=False,
    )
```

```python
import functools

import jax
import jax.numpy as jnp
from jax import lax
from jax.experimental import pallas as pl
from jax.experimental.pallas import tpu as pltpu
from jax.sharding import PartitionSpec as P

ITERS = 2


damping = 0.5
coupling = 0.03125
ANY = pl.BlockSpec(memory_space=pl.ANY)
SMEM = pl.BlockSpec(memory_space=pltpu.SMEM)
VMEM = pl.BlockSpec(memory_space=pltpu.VMEM)
VMEM_BYTES = 32 * 1024 * 1024


def call(body, out_shape, in_specs, flops, moved, *operands):
    single = isinstance(out_shape, jax.ShapeDtypeStruct)
    return pl.pallas_call(
        body,
        out_shape=out_shape,
        in_specs=in_specs,
        out_specs=VMEM if single else (VMEM,) * len(out_shape),
        compiler_params=pltpu.CompilerParams(vmem_limit_bytes=VMEM_BYTES),
        cost_estimate=pl.CostEstimate(flops=flops, bytes_accessed=moved, transcendentals=0),
    )(*operands)


def prologue_body(meta, occupied, k_ref, virt_row, virt_col, kept_ref, own_ref, inverse_ref):
    orb_rows, _, virt, _ = k_ref.shape
    my_row = meta[2 * orb_rows, 0]
    my_col = meta[2 * orb_rows, 1]
    for step in range(kept_ref.shape[0]):
        for t in range(orb_rows):
            orbital = (my_row ^ step) * orb_rows + t
            for i in range(orb_rows):
                block = k_ref[i, orbital]
                keep = jnp.where(meta[i, orbital] > 0, block, jnp.zeros_like(block))
                kept_ref[step, i * virt : (i + 1) * virt, t * virt : (t + 1) * virt] = keep
    virt_pair = virt_col[...] + virt_row[...]
    for i in range(orb_rows):
        own_ref[i] = k_ref[i, my_col]
        inverse_ref[i] = 1.0 / (virt_pair - occupied[0, my_row * orb_rows + i] - occupied[0, my_col])


def prologue(rows, meta, coulomb, virtual_energy, occupied_energy):
    orb_rows, count, virt, _ = coulomb.shape
    shape = (
        jax.ShapeDtypeStruct((rows, orb_rows * virt, orb_rows * virt), jnp.bfloat16),
        jax.ShapeDtypeStruct((orb_rows, virt, virt), jnp.bfloat16),
        jax.ShapeDtypeStruct((orb_rows, virt, virt), jnp.float32),
    )
    return call(
        prologue_body, shape, [SMEM, SMEM, VMEM, VMEM, VMEM], 0, 4 * orb_rows * count * virt**2,
        meta, occupied_energy[None], coulomb, virtual_energy[None], virtual_energy[:, None],
    )


def piece_blocks(refs, rows):
    found, refs, size = [], list(refs), refs[0].shape[0]
    for step in range(rows):
        blocks = []
        while len(blocks) < size:
            ref = refs.pop(0)
            blocks += [(ref, at) for at in range(ref.shape[0])]
        found.append(blocks)
    return found


def coupled_body(rows, k_ref, *refs):
    out_ref, same_ref, other_ref = refs[-3:]
    orb_rows, virt, _ = out_ref.shape
    side = lax.rem(lax.axis_index("col"), 2)
    total = None
    for step in range(rows):
        for t in range(orb_rows):
            left = k_ref[step, :, t * virt : (t + 1) * virt]
            part = jnp.dot(left, refs[step][t], preferred_element_type=jnp.float32)
            total = part if total is None else total + part
    first, second = total[:virt].astype(out_ref.dtype), total[virt:].astype(out_ref.dtype)
    out_ref[0], out_ref[1] = first, second

    @pl.when(side == 0)
    def _():
        same_ref[...], other_ref[...] = first, second

    @pl.when(side == 1)
    def _():
        same_ref[...], other_ref[...] = second, first


def coupled_blocks(rows, kept, pieces):
    orb_rows, virt, _ = pieces[0].shape
    count = rows * orb_rows
    block = jax.ShapeDtypeStruct((virt, virt), jnp.bfloat16)
    shape = (jax.ShapeDtypeStruct((orb_rows, virt, virt), jnp.bfloat16), block, block)
    body = functools.partial(coupled_body, rows)
    flops, moved = 2 * orb_rows * count * virt**3, 2 * (orb_rows + 1) * count * virt**2
    return call(body, shape, [VMEM] * (1 + len(pieces)), flops, moved, kept, *pieces)


def column_body(*refs):
    out_ref = refs[-1]
    orb_rows = refs[0].shape[0]
    my_place = lax.div(lax.axis_index("col"), 2)
    for step in range(out_ref.shape[0] // orb_rows):
        out_ref[pl.ds((my_place ^ step) * orb_rows, orb_rows)] = refs[step][...]


def whole_column(pieces, others):
    orb_rows, virt, _ = pieces[0].shape
    shape = jax.ShapeDtypeStruct((orb_rows * len(pieces), virt, virt), jnp.bfloat16)
    operands = [*pieces, *others]
    moved = 4 * orb_rows * len(pieces) * virt**2
    return call(column_body, shape, [VMEM] * len(operands), 0, moved, *operands)


def tied_body(*refs):
    pass


def tied(x, *others):
    return pl.pallas_call(
        tied_body,
        out_shape=jax.ShapeDtypeStruct(x.shape, x.dtype),
        in_specs=[VMEM] * (1 + len(others)),
        out_specs=VMEM,
        input_output_aliases={0: 0},
        compiler_params=pltpu.CompilerParams(vmem_limit_bytes=VMEM_BYTES),
    )(x, *others)


def masked_pair(meta, orbital, blocks):
    orb_rows = len(blocks)
    kept = [jnp.where(meta[orb_rows + i, orbital] > 0, block, jnp.zeros_like(block)) for i, block in enumerate(blocks)]
    return jnp.concatenate(kept, axis=0)


def turned(block):
    return jnp.transpose(block.astype(jnp.float32), (1, 0))


def first_body(rows, meta, own_ref, other_ref, *refs):
    state_ref, coulomb_ref, inverse_ref, out_ref = refs[-4:]
    orb_rows = out_ref.shape[0]
    blocks = piece_blocks(refs[:-4], rows)
    my_row, side = meta[2 * orb_rows, 0], meta[2 * orb_rows, 1] % 2
    total = None
    for step in range(rows):
        at = my_row ^ step
        for t in range(orb_rows):
            left = [
                jnp.where(side == t, own_ref[at * orb_rows + i], other_ref[at * orb_rows + i]) for i in range(orb_rows)
            ]
            left = masked_pair(meta, at * orb_rows + t, left)
            ref, place = blocks[step][t]
            part = jnp.dot(left, ref[place], preferred_element_type=jnp.float32)
            total = part if total is None else total + part
    linear = coulomb_ref[...].astype(jnp.float32) + coupling * refs[0][...].astype(jnp.float32)
    residual = linear + coupling * coupling * total.reshape(out_ref.shape)
    out_ref[...] = damping * state_ref[...] - residual * inverse_ref[...]


def second_body(same_ref, other_ref, part_ref, inverse_ref, out_ref, *half_refs):
    side = lax.rem(lax.axis_index("col"), 2)
    for ref, at in ((same_ref, side), (other_ref, 1 - side)):
        state = part_ref[at] - coupling * turned(ref[...]) * inverse_ref[at]
        out_ref[at] = state
        for half_ref in half_refs:
            half_ref[at] = state.astype(half_ref.dtype)


def first_update(rows, meta, own, other, c_pieces, state, coulomb_own, inverse):
    orb_rows, virt, _ = state.shape
    shape = jax.ShapeDtypeStruct(state.shape, jnp.float32)
    flops, moved = 2 * orb_rows**2 * rows * virt**3, 4 * (orb_rows + 1) * orb_rows * rows * virt**2
    return call(
        functools.partial(first_body, rows), shape, [SMEM] + [VMEM] * (len(c_pieces) + 5), flops, moved,
        meta, own, other, *c_pieces, state, coulomb_own, inverse,
    )


def second_update(same, other, part, inverse, with_half):
    shape = (jax.ShapeDtypeStruct(part.shape, jnp.float32), jax.ShapeDtypeStruct(part.shape, jnp.bfloat16))
    shape = shape if with_half else shape[:1]
    return call(second_body, shape, [VMEM] * 4, 0, 16 * part.size, same, other, part, inverse)


def on_device(
    rows,
    cols,
    amplitudes,
    coulomb,
    inner_list,
    inner_count,
    reader_list,
    reader_count,
    virtual_energy,
    occupied_energy,
):
    orb_rows, orb_cols, virt, _ = amplitudes.shape
    count = coulomb.shape[1]
    slots = inner_list.shape[2]
    assert orb_cols == 1 and count == cols == rows * orb_rows and orb_rows == 2
    halves = cols // 2
    my_row = lax.axis_index("row")
    my_col = lax.axis_index("col")

    def from_row(x, step):
        return lax.ppermute(x, "row", [(r ^ step, r) for r in range(rows)])

    def row_gathered(x):
        return [x] + [from_row(x, step) for step in range(1, rows)]

    def swapped(x):
        return lax.ppermute(x, "col", [(c ^ 1, c) for c in range(cols)])

    def from_chip(x, step):
        return lax.ppermute(x, "col", [(c ^ 2 * step, c) for c in range(cols)])

    def crossing(x, place, flip=0):
        pairs = []
        for r in range(rows):
            for c in range(cols):
                to_r, to_z = place(r, c // 2)
                pairs.append((r * cols + c, to_r * cols + 2 * to_z + (c % 2 ^ flip)))
        return lax.ppermute(x, ("row", "col"), pairs)

    def high_parts(r, z):
        return z - z % 2 + r % 2, r - r % 2 + z % 2

    def last_bits(r, z):
        return r - r % 2 + z % 2, z - z % 2 + r % 2

    state = amplitudes[:, 0]
    half = state.astype(jnp.bfloat16)

    slot_iota = jnp.arange(slots, dtype=jnp.int32)
    orbital_iota = jnp.arange(count, dtype=jnp.int32)

    def used(lists, counts):
        live = slot_iota[None] < counts[:, None]
        hit = (lists[:, :, None] == orbital_iota) & live[:, :, None]
        return jnp.any(hit, axis=1).astype(jnp.int32)

    inner_used = used(inner_list[:, 0], inner_count[:, 0])
    reader_used = used(
        lax.dynamic_index_in_dim(reader_list, my_col, 1, False), lax.dynamic_index_in_dim(reader_count, my_col, 1, False)
    )
    place = jnp.where(orbital_iota == 0, my_row, my_col).astype(jnp.int32)
    meta = jnp.concatenate([inner_used, reader_used, place[None]], axis=0)

    kept, coulomb_own, inverse = prologue(rows, meta, coulomb, virtual_energy, occupied_energy)

    for sweep_index in range(ITERS):
        a_pieces = row_gathered(half)
        column = {0: half, 1: from_chip(half, 1)}
        for step in range(2, halves, 2):
            column[step] = from_chip(half, step)
        coupled, same, other = coupled_blocks(rows, kept, a_pieces)
        near = from_row(coupled, 1)
        c_pieces, far = [coupled, near], []
        for step in range(2, rows, 2):
            piece = from_row(coupled, step)
            far += [from_row(piece[0:1], 1), from_row(near[1:2], step)]
            c_pieces += [piece, *far[-2:]]
        same, other = crossing(same, high_parts), crossing(other, last_bits)
        for step in range(2, halves, 2):
            column[step] = tied(column[step], column[1], coupled)
            column[step + 1] = from_chip(column[step], 1)
        column = [column[step] for step in range(halves)]
        own = whole_column(column, [*far[1::2], c_pieces[2], same, other])
        same, other = crossing(same, last_bits), crossing(other, high_parts, 1)
        part = first_update(rows, meta, own, swapped(own), c_pieces, state, coulomb_own, inverse)
        state, *halves_out = second_update(same, other, part, inverse, sweep_index < ITERS - 1)
        half = halves_out[0] if halves_out else None
    return state[:, None]


def solution(mesh):
    return jax.shard_map(
        functools.partial(on_device, mesh.shape["row"], mesh.shape["col"]),
        mesh=mesh,
        in_specs=(
            P("row", "col", None, None),
            P("row", None, None, None),
            P("row", "col", None),
            P("row", "col"),
            P("row", None, None),
            P("row", None),
            P(),
            P(),
        ),
        out_specs=P("row", "col", None, None),
        check_vma=False,
    )
```

```python
import functools

import jax
import jax.numpy as jnp
from jax import lax
from jax.experimental import pallas as pl
from jax.experimental.pallas import tpu as pltpu
from jax.sharding import PartitionSpec as P

ITERS = 2


damping = 0.5
coupling = 0.03125
ANY = pl.BlockSpec(memory_space=pl.ANY)
SMEM = pl.BlockSpec(memory_space=pltpu.SMEM)
VMEM = pl.BlockSpec(memory_space=pltpu.VMEM)
VMEM_BYTES = 32 * 1024 * 1024


def call(body, out_shape, in_specs, flops, moved, *operands):
    single = isinstance(out_shape, jax.ShapeDtypeStruct)
    return pl.pallas_call(
        body,
        out_shape=out_shape,
        in_specs=in_specs,
        out_specs=VMEM if single else (VMEM,) * len(out_shape),
        compiler_params=pltpu.CompilerParams(vmem_limit_bytes=VMEM_BYTES),
        cost_estimate=pl.CostEstimate(flops=flops, bytes_accessed=moved, transcendentals=0),
    )(*operands)


def prologue_body(meta, occupied, k_ref, virt_row, virt_col, kept_ref, own_ref, inverse_ref):
    orb_rows, _, virt, _ = k_ref.shape
    my_row = meta[2 * orb_rows, 0]
    my_col = meta[2 * orb_rows, 1]
    for step in range(kept_ref.shape[0]):
        for t in range(orb_rows):
            orbital = (my_row ^ step) * orb_rows + t
            for i in range(orb_rows):
                block = k_ref[i, orbital]
                keep = jnp.where(meta[i, orbital] > 0, block, jnp.zeros_like(block))
                kept_ref[step, i * virt : (i + 1) * virt, t * virt : (t + 1) * virt] = keep
    virt_pair = virt_col[...] + virt_row[...]
    for i in range(orb_rows):
        own_ref[i] = k_ref[i, my_col]
        inverse_ref[i] = 1.0 / (virt_pair - occupied[0, my_row * orb_rows + i] - occupied[0, my_col])


def prologue(rows, meta, coulomb, virtual_energy, occupied_energy):
    orb_rows, count, virt, _ = coulomb.shape
    shape = (
        jax.ShapeDtypeStruct((rows, orb_rows * virt, orb_rows * virt), jnp.bfloat16),
        jax.ShapeDtypeStruct((orb_rows, virt, virt), jnp.bfloat16),
        jax.ShapeDtypeStruct((orb_rows, virt, virt), jnp.float32),
    )
    return call(
        prologue_body, shape, [SMEM, SMEM, VMEM, VMEM, VMEM], 0, 4 * orb_rows * count * virt**2,
        meta, occupied_energy[None], coulomb, virtual_energy[None], virtual_energy[:, None],
    )


def piece_blocks(refs, rows):
    found, refs, size = [], list(refs), refs[0].shape[0]
    for step in range(rows):
        blocks = []
        while len(blocks) < size:
            ref = refs.pop(0)
            blocks += [(ref, at) for at in range(ref.shape[0])]
        found.append(blocks)
    return found


def coupled_body(rows, k_ref, *refs):
    out_ref, same_ref, other_ref = refs[-3:]
    orb_rows, virt, _ = out_ref.shape
    side = lax.rem(lax.axis_index("col"), 2)
    total = None
    for step in range(rows):
        for t in range(orb_rows):
            left = k_ref[step, :, t * virt : (t + 1) * virt]
            part = jnp.dot(left, refs[step][t], preferred_element_type=jnp.float32)
            total = part if total is None else total + part
    first, second = total[:virt].astype(out_ref.dtype), total[virt:].astype(out_ref.dtype)
    out_ref[0], out_ref[1] = first, second

    @pl.when(side == 0)
    def _():
        same_ref[...], other_ref[...] = first, second

    @pl.when(side == 1)
    def _():
        same_ref[...], other_ref[...] = second, first


def coupled_blocks(rows, kept, pieces):
    orb_rows, virt, _ = pieces[0].shape
    count = rows * orb_rows
    block = jax.ShapeDtypeStruct((virt, virt), jnp.bfloat16)
    shape = (jax.ShapeDtypeStruct((orb_rows, virt, virt), jnp.bfloat16), block, block)
    body = functools.partial(coupled_body, rows)
    flops, moved = 2 * orb_rows * count * virt**3, 2 * (orb_rows + 1) * count * virt**2
    return call(body, shape, [VMEM] * (1 + len(pieces)), flops, moved, kept, *pieces)


def column_body(*refs):
    out_ref = refs[-1]
    orb_rows = refs[0].shape[0]
    my_place = lax.div(lax.axis_index("col"), 2)
    for step in range(out_ref.shape[0] // orb_rows):
        out_ref[pl.ds((my_place ^ step) * orb_rows, orb_rows)] = refs[step][...]


def whole_column(pieces, others):
    orb_rows, virt, _ = pieces[0].shape
    shape = jax.ShapeDtypeStruct((orb_rows * len(pieces), virt, virt), jnp.bfloat16)
    operands = [*pieces, *others]
    moved = 4 * orb_rows * len(pieces) * virt**2
    return call(column_body, shape, [VMEM] * len(operands), 0, moved, *operands)


def tied_body(*refs):
    pass


def tied(x, *others):
    return pl.pallas_call(
        tied_body,
        out_shape=jax.ShapeDtypeStruct(x.shape, x.dtype),
        in_specs=[VMEM] * (1 + len(others)),
        out_specs=VMEM,
        input_output_aliases={0: 0},
        compiler_params=pltpu.CompilerParams(vmem_limit_bytes=VMEM_BYTES),
    )(x, *others)


def masked_pair(meta, orbital, blocks):
    orb_rows = len(blocks)
    kept = [jnp.where(meta[orb_rows + i, orbital] > 0, block, jnp.zeros_like(block)) for i, block in enumerate(blocks)]
    return jnp.concatenate(kept, axis=0)


def turned(block):
    return jnp.transpose(block.astype(jnp.float32), (1, 0))


def first_body(rows, meta, own_ref, other_ref, *refs):
    state_ref, coulomb_ref, inverse_ref, out_ref = refs[-4:]
    orb_rows = out_ref.shape[0]
    blocks = piece_blocks(refs[:-4], rows)
    my_row, side = meta[2 * orb_rows, 0], meta[2 * orb_rows, 1] % 2
    total = None
    for step in range(rows):
        at = my_row ^ step
        for t in range(orb_rows):
            left = [
                jnp.where(side == t, own_ref[at * orb_rows + i], other_ref[at * orb_rows + i]) for i in range(orb_rows)
            ]
            left = masked_pair(meta, at * orb_rows + t, left)
            ref, place = blocks[step][t]
            part = jnp.dot(left, ref[place], preferred_element_type=jnp.float32)
            total = part if total is None else total + part
    linear = coulomb_ref[...].astype(jnp.float32) + coupling * refs[0][...].astype(jnp.float32)
    residual = linear + coupling * coupling * total.reshape(out_ref.shape)
    out_ref[...] = damping * state_ref[...] - residual * inverse_ref[...]


def second_body(same_ref, other_ref, part_ref, inverse_ref, out_ref, *half_refs):
    side = lax.rem(lax.axis_index("col"), 2)
    for ref, at in ((same_ref, side), (other_ref, 1 - side)):
        state = part_ref[at] - coupling * turned(ref[...]) * inverse_ref[at]
        out_ref[at] = state
        for half_ref in half_refs:
            half_ref[at] = state.astype(half_ref.dtype)


def first_update(rows, meta, own, other, c_pieces, state, coulomb_own, inverse):
    orb_rows, virt, _ = state.shape
    shape = jax.ShapeDtypeStruct(state.shape, jnp.float32)
    flops, moved = 2 * orb_rows**2 * rows * virt**3, 4 * (orb_rows + 1) * orb_rows * rows * virt**2
    return call(
        functools.partial(first_body, rows), shape, [SMEM] + [VMEM] * (len(c_pieces) + 5), flops, moved,
        meta, own, other, *c_pieces, state, coulomb_own, inverse,
    )


def second_update(same, other, part, inverse, with_half):
    shape = (jax.ShapeDtypeStruct(part.shape, jnp.float32), jax.ShapeDtypeStruct(part.shape, jnp.bfloat16))
    shape = shape if with_half else shape[:1]
    return call(second_body, shape, [VMEM] * 4, 0, 16 * part.size, same, other, part, inverse)


def on_device(
    rows,
    cols,
    amplitudes,
    coulomb,
    inner_list,
    inner_count,
    reader_list,
    reader_count,
    virtual_energy,
    occupied_energy,
):
    orb_rows, orb_cols, virt, _ = amplitudes.shape
    count = coulomb.shape[1]
    slots = inner_list.shape[2]
    assert orb_cols == 1 and count == cols == rows * orb_rows and orb_rows == 2
    halves = cols // 2
    my_row = lax.axis_index("row")
    my_col = lax.axis_index("col")

    def from_row(x, step):
        return lax.ppermute(x, "row", [(r ^ step, r) for r in range(rows)])

    def row_gathered(x):
        return [x] + [from_row(x, step) for step in range(1, rows)]

    def swapped(x):
        return lax.ppermute(x, "col", [(c ^ 1, c) for c in range(cols)])

    def from_chip(x, step):
        return lax.ppermute(x, "col", [(c ^ 2 * step, c) for c in range(cols)])

    def crossing(x, place, flip=0):
        pairs = []
        for r in range(rows):
            for c in range(cols):
                to_r, to_z = place(r, c // 2)
                pairs.append((r * cols + c, to_r * cols + 2 * to_z + (c % 2 ^ flip)))
        return lax.ppermute(x, ("row", "col"), pairs)

    def high_parts(r, z):
        return z - z % 2 + r % 2, r - r % 2 + z % 2

    def last_bits(r, z):
        return r - r % 2 + z % 2, z - z % 2 + r % 2

    state = amplitudes[:, 0]
    half = state.astype(jnp.bfloat16)

    slot_iota = jnp.arange(slots, dtype=jnp.int32)
    orbital_iota = jnp.arange(count, dtype=jnp.int32)

    def used(lists, counts):
        live = slot_iota[None] < counts[:, None]
        hit = (lists[:, :, None] == orbital_iota) & live[:, :, None]
        return jnp.any(hit, axis=1).astype(jnp.int32)

    inner_used = used(inner_list[:, 0], inner_count[:, 0])
    reader_used = used(
        lax.dynamic_index_in_dim(reader_list, my_col, 1, False), lax.dynamic_index_in_dim(reader_count, my_col, 1, False)
    )
    place = jnp.where(orbital_iota == 0, my_row, my_col).astype(jnp.int32)
    meta = jnp.concatenate([inner_used, reader_used, place[None]], axis=0)

    kept, coulomb_own, inverse = prologue(rows, meta, coulomb, virtual_energy, occupied_energy)

    for sweep_index in range(ITERS):
        a_pieces = row_gathered(half)
        column = {0: half, 1: from_chip(half, 1)}
        for step in range(2, halves, 2):
            column[step] = from_chip(half, step)
        coupled, same, other = coupled_blocks(rows, kept, a_pieces)
        near = from_row(coupled, 1)
        c_pieces, far = [coupled, near], []
        for step in range(2, rows, 2):
            piece = from_row(coupled, step)
            far += [from_row(piece[0:1], 1), from_row(near[1:2], step)]
            c_pieces += [piece, *far[-2:]]
        same, other = crossing(same, last_bits), crossing(other, high_parts)
        for step in range(2, halves, 2):
            column[step] = tied(column[step], column[1], coupled)
            column[step + 1] = from_chip(column[step], 1)
        column = [column[step] for step in range(halves)]
        own = whole_column(column, [*far, same, other])
        same, other = crossing(same, high_parts), crossing(other, last_bits, 1)
        part = first_update(rows, meta, own, swapped(own), c_pieces, state, coulomb_own, inverse)
        state, *halves_out = second_update(same, other, part, inverse, sweep_index < ITERS - 1)
        half = halves_out[0] if halves_out else None
    return state[:, None]


def solution(mesh):
    return jax.shard_map(
        functools.partial(on_device, mesh.shape["row"], mesh.shape["col"]),
        mesh=mesh,
        in_specs=(
            P("row", "col", None, None),
            P("row", None, None, None),
            P("row", "col", None),
            P("row", "col"),
            P("row", None, None),
            P("row", None),
            P(),
            P(),
        ),
        out_specs=P("row", "col", None, None),
        check_vma=False,
    )
```
